128 devices in a mesh: src: 16 (over y, x), tm: 8 (over z, core).
Axes of the slice: x: 4, y: 4, z: 4, core: 2. Of those that a mesh axis runs over, the one named last changes fastest.
Arguments:
- knot_index: int32 [1048576], P(('src', 'tm')), may hold values from 0 to 1023
- block_counts: int32 [128, 8], P(('src', 'tm')), may hold values from 1 to 2048, 8192 in all within a row
- knot_phase: float32 [1048576], P(('src', 'tm')), may hold values from 0 to 1
- partials: float32 [4, 1048576], P(None, ('src', 'tm')), may hold values from -5 to 5
- obs_weight: float32 [1048576], P(('src', 'tm')), may hold values from 0.25 to 4
- residuals: float32 [1048576], P(('src', 'tm')), may hold values from -8 to 8
- cal_id: int32 [1048576], P(('src', 'tm')), may hold values from 0 to 511
- across: float32 [1048576], P(('src', 'tm')), may hold values from -1 to 1
- coeffs: float32 [4, 8192], P(None, 'tm'), may hold values from -0.6 to 0.6
Outputs:
- new_coeffs: float32 [4, 8192], P(None, 'tm')
- calibration_step: float32 [2, 512], replicated
The draws below stay inside these ranges and needn't reach their ends.
Inputs may be any that keep to these rules, and one draw needn't show every extreme that they name: `block_counts`: each device's row sums to 8192; that device's observations are stored by time block in this order.
All inputs are finite; a program needn't handle non-finite values.
Results may differ from the reference program's by a relative error of at most 0.0003.
Values sent between devices are 32-bit elements; how exact they have to be, the bound alone decides.
No kernel may reach another device: no remote copies, remote signals or barrier semaphores. Data moves between devices by JAX's collectives and lax.ppermute only.
A program may use at most 128 MiB of HBM per device.

```python
import math
import jax
import jax.numpy as jnp
import numpy as np
from jax import lax

COMPONENTS = 4
K = 1024
OBS_DEV = 8192
NCAL = 512
ITERS = 6
NK = 8192
OBS = 1048576
N_SRC = 16
N_TM = 8
DEVICES = 128


def interval_ids(key):
    return jax.random.randint(key, (OBS_DEV * DEVICES,), 0, NCAL)


def design_values(key):
    key = jax.random.fold_in(key, 17)
    normal_key = jax.random.fold_in(key, 0)
    shape = (4, OBS_DEV * DEVICES)
    peaked = jnp.clip(jax.random.normal(normal_key, shape, jnp.float32), -5.0, 5.0)
    return peaked


def draw_cal_id(key, part):
    return interval_ids(key).astype(jnp.int32)


def draw_partials(key, part):
    values = design_values(key)
    return values.astype(jnp.float32)


def draw_residuals(key, part):
    chosen = interval_ids(key)
    design = design_values(key)
    key = jax.random.fold_in(key, 3)
    table_key, noise_key, field_key = jax.random.split(key, 3)
    offsets = jax.random.uniform(table_key, (NCAL,), jnp.float32, -1.5, 1.5)
    attitude = jax.random.uniform(field_key, (4,), jnp.float32, -1.2, 1.2)
    noise_vals = jnp.clip(jax.random.normal(noise_key, (OBS_DEV * DEVICES,), jnp.float32), -5.0, 5.0)
    signal = jnp.sum(attitude[:, None] * design, axis=0)
    return jnp.clip(noise_vals + offsets[chosen] + signal, -8.0, 8.0).astype(jnp.float32)


def place_ends(values, stream_key, least, high):
    longest = values.shape.index(max(values.shape))
    spots = []
    for shift in (0, 1):
        where = [jax.random.randint(jax.random.fold_in(stream_key, axis), (), 0, length) for axis, length in enumerate(values.shape)]
        where[longest] = (where[longest] + shift) % values.shape[longest]
        spots.append(tuple(where))
    return values.at[spots[0]].set(least).at[spots[1]].set(high)


def shard_levels(rng, dims, cuts, least, high):
    gain, own = 1.0, jax.random.fold_in(rng, 6)
    for dim, parts in cuts:
        draws = jnp.exp(jax.random.uniform(jax.random.fold_in(own, dim), (parts,), jnp.float32, least / len(cuts), high / len(cuts)))
        gain = gain * jnp.repeat(draws, dims[dim] // parts).reshape([-1 if axis == dim else 1 for axis in range(len(dims))])
    return gain


def split_up(count, total, most, slope):
    portions = [(1 << 20) // math.isqrt(grade ** slope) + 1 for grade in range(2, count + 1)]
    rest, holding = total - most - (count - 1), [1] * (count - 1)
    while rest > 0:
        movable = [i for i in range(count - 1) if holding[i] < most]
        pool, remaining = sum([portions[i] for i in movable]), rest
        for i in movable:
            more = min(most - holding[i], max(1, remaining * portions[i] // pool), rest)
            holding[i] = holding[i] + more
            rest = rest - more
    return np.array([most] + holding)


def uneven_parts(key, count, total, most, slope):
    if count == 2:
        one = jax.random.randint(key, (), max(1, total - most), min(most, total - 1) + 1)
        return jnp.stack([one, total - one])
    sizes = jnp.asarray(split_up(count, total, most, slope), jnp.int32)
    couples = (count - 1) // 2
    source_of, taker = sizes[1:1 + 2 * couples:2], sizes[2:2 + 2 * couples:2]
    room = jnp.minimum(source_of - 1, most - taker)
    passed = jax.random.randint(jax.random.fold_in(key, 1), (couples,), 0, 1 << 20) % (room + 1)
    sizes = sizes.at[1:1 + 2 * couples:2].set(source_of - passed).at[2:2 + 2 * couples:2].set(taker + passed)
    return sizes[jax.random.permutation(jax.random.fold_in(key, 2), count)]


def scatter_about(stream_key, extent, scale, most, shards=(), kind=jnp.bfloat16):
    values = scale * jax.random.normal(stream_key, extent, jnp.float32)
    if shards:
        values = values * shard_levels(stream_key, extent, shards, -0.22, 0.18)
    return jnp.clip(values, -most, most).astype(kind)


def setup_inputs(seed: int = 0) -> dict:
    seeds = jax.random.split(jax.random.key(seed), 10)
    knot_index = place_ends(jax.random.randint(seeds[0], (OBS,), 0, K), jax.random.fold_in(seeds[0], 1), 0, K - 1).astype(jnp.int32)
    block_counts = jax.vmap(lambda own: uneven_parts(own, N_TM, OBS_DEV, 2 * OBS_DEV // N_TM, 2))(jax.random.split(seeds[1], DEVICES)).reshape((DEVICES, N_TM)).astype(jnp.int32)
    knot_phase = jnp.clip(1.0 * jax.random.uniform(seeds[2], (OBS,), jnp.float32) ** shard_levels(seeds[2], (OBS,), ((0, 128),), -0.2, 0.2), 0.0, 1.0)
    partials = draw_partials(jax.random.fold_in(seeds[9], 71), 0)
    obs_weight = jnp.clip(jnp.exp(math.log(4.0) - 2.7725887 * jax.random.uniform(seeds[4], (OBS,), jnp.float32) ** shard_levels(seeds[4], (OBS,), ((0, 128),), -0.2, 0.2)), 0.25, 4.0)
    residuals = draw_residuals(jax.random.fold_in(seeds[9], 71), 0)
    cal_id = draw_cal_id(jax.random.fold_in(seeds[9], 71), 0)
    across = jnp.clip(jax.random.uniform(seeds[7], (OBS,), jnp.float32, -1.0, 1.0) * shard_levels(seeds[7], (OBS,), ((0, 128),), -0.4, 0.0), -1.0, 1.0)
    coeffs = scatter_about(seeds[8], (COMPONENTS, NK), 0.1, 0.6, ((1, 8),), jnp.float32)
    return {"knot_index": knot_index, "block_counts": block_counts, "knot_phase": knot_phase, "partials": partials, "obs_weight": obs_weight, "residuals": residuals, "cal_id": cal_id, "across": across, "coeffs": coeffs}


HIGHEST = lax.Precision.HIGHEST
ATTITUDE_PRIOR = 1.0
FILTER_GAIN = 0.05


def spline_weights(knot_phase):
    phase_sq = knot_phase * knot_phase
    phase_cube = phase_sq * knot_phase
    remain = 1.0 - knot_phase
    return jnp.stack([remain * remain * remain / 6.0,
                      (3.0 * phase_cube - 6.0 * phase_sq + 4.0) / 6.0,
                      (-3.0 * phase_cube + 3.0 * phase_sq + 3.0 * knot_phase + 1.0) / 6.0,
                      phase_cube / 6.0])


def moment_rows(knot_phase, partials, weight, residual):
    basis_vals = spline_weights(knot_phase)
    row_count = knot_phase.shape[0]
    design = (basis_vals[:, None, :] * partials[None, :, :]).reshape(16, row_count)
    weighted = weight[None, :] * design
    normal = (weighted[:, None, :] * design[None, :, :]).reshape(256, row_count)
    right_side = weighted * residual[None, :]
    return jnp.concatenate([normal, right_side], axis=0)


def band_rows(moments):
    span_len = moments.shape[1]
    padded = jnp.pad(moments, ((0, 0), (3, 0)))
    pair_rows = padded[:256].reshape(4, 4, 4, 4, span_len + 3)
    sources = padded[256:].reshape(4, 4, span_len + 3)
    blocks = []
    for knot_lag in range(4):
        summed = jnp.zeros((4, 4, span_len), jnp.float32)
        for order_a in range(4 - knot_lag):
            summed = summed + pair_rows[order_a, :, order_a + knot_lag, :, 3 - order_a:3 - order_a + span_len]
        blocks.append(summed.reshape(16, span_len))
    summed = jnp.zeros((4, span_len), jnp.float32)
    for order_a in range(4):
        summed = summed + sources[order_a, :, 3 - order_a:3 - order_a + span_len]
    blocks.append(summed)
    return jnp.concatenate(blocks, axis=0)


def apply_normals(band, field):
    span_len = field.shape[1]
    matrices = band[:64].reshape(4, 4, 4, span_len)
    lower_part = jnp.sum(matrices[1:] * field[None, :, None, :], axis=1)
    near_field = jnp.pad(field, ((0, 0), (3, 3)))
    lower_rim = jnp.pad(lower_part, ((0, 0), (0, 0), (3, 3)))
    result = ATTITUDE_PRIOR * field
    for knot_lag in range(4):
        result = result + jnp.sum(matrices[knot_lag] * near_field[None, :, 3 + knot_lag:3 + knot_lag + span_len], axis=1)
    for knot_lag in range(1, 4):
        result = result + lower_rim[knot_lag - 1, :, 3 - knot_lag:3 - knot_lag + span_len]
    return result


def recursive_filter(field, rate):
    def advance(state_vec, column):
        state_vec = column + rate * state_vec
        return state_vec, state_vec

    start_state = jnp.zeros((field.shape[0],), jnp.float32)
    final_state, forward = lax.scan(advance, start_state, field.T)
    final_state, backward = lax.scan(advance, start_state, forward, reverse=True)
    return backward.T


def reference(knot_index, block_counts, knot_phase, partials, obs_weight, residuals, cal_id, across, coeffs):
    devices_all = N_SRC * N_TM
    knots_all = N_TM * K
    prior = OBS_DEV * N_SRC * N_TM / NCAL
    weighted_x = obs_weight * across
    cal_terms = jnp.stack([obs_weight, weighted_x, weighted_x * across, obs_weight * residuals, weighted_x * residuals])
    cal_totals = jax.ops.segment_sum(cal_terms.T, cal_id, num_segments=NCAL).T
    zero_moment = cal_totals[0] + prior
    second_moment = cal_totals[2] + prior
    determinant = zero_moment * second_moment - cal_totals[1] * cal_totals[1]
    offset_step = (second_moment * cal_totals[3] - cal_totals[1] * cal_totals[4]) / determinant
    slope_step = (zero_moment * cal_totals[4] - cal_totals[1] * cal_totals[3]) / determinant
    calibration_step = jnp.stack([offset_step, slope_step])
    corrected = residuals - offset_step[cal_id] - slope_step[cal_id] * across

    stacked = (knot_index.reshape(devices_all, OBS_DEV), block_counts,
               knot_phase.reshape(devices_all, OBS_DEV),
               partials.reshape(4, devices_all, OBS_DEV).transpose(1, 0, 2),
               obs_weight.reshape(devices_all, OBS_DEV), corrected.reshape(devices_all, OBS_DEV))

    def device_moments(accum, pieces):
        local_knot, counts, local_phase, local_partials, local_weight, local_resid = pieces
        ends = jnp.cumsum(counts).astype(jnp.int32)
        rows_idx = jnp.arange(OBS_DEV, dtype=jnp.int32)
        block_of = jnp.sum((rows_idx[:, None] >= ends[None, :]).astype(jnp.int32), axis=1)
        global_knot = (block_of * K + local_knot).astype(jnp.int32)
        rows = moment_rows(local_phase, local_partials, local_weight, local_resid)
        accum = accum + jax.ops.segment_sum(rows.T, global_knot, num_segments=knots_all).T
        return accum, None

    moments, unused = lax.scan(device_moments, jnp.zeros((272, knots_all), jnp.float32), stacked)
    band = band_rows(moments)
    rhs = band[64:68]
    diag_vals = jnp.stack([band[5 * comp] for comp in range(4)]) + ATTITUDE_PRIOR
    rate = 0.1 ** (1.0 / knots_all)
    filter_scale = (1.0 - rate) ** 2

    def precondition(resid):
        return resid / diag_vals + FILTER_GAIN * filter_scale * recursive_filter(resid, rate)

    solution = jnp.zeros_like(rhs)
    resid = rhs
    search_z = precondition(resid)
    direction = search_z
    energy = jnp.sum(resid * search_z)
    for iteration in range(ITERS):
        applied = apply_normals(band, direction)
        step_len = energy / jnp.sum(direction * applied)
        solution = solution + step_len * direction
        resid = resid - step_len * applied
        search_z = precondition(resid)
        new_energy = jnp.sum(resid * search_z)
        direction = search_z + (new_energy / energy) * direction
        energy = new_energy
    return coeffs + solution, calibration_step
```

```python
import functools

import jax
import jax.numpy as jnp
import numpy as np
from jax import lax
from jax.experimental import pallas as pl
from jax.experimental.pallas import tpu as pltpu
from jax.sharding import PartitionSpec as P

K = 1024
OBS_DEV = 8192
NCAL = 512
ITERS = 6
N_SRC = 16
N_TM = 8
NK = K * N_TM
CAP = 2 * OBS_DEV // N_TM
ATTITUDE_PRIOR = 1.0
FILTER_GAIN = 0.05
CHUNK = 256
HIGHEST = lax.Precision.HIGHEST
F32 = jnp.float32
BF16 = jnp.bfloat16
VMEM_LIMIT = 48 * 1024 * 1024

PAIRS = [(a, b) for a in range(4) for b in range(a, 4)]
PAIR_AT = {pair: i for i, pair in enumerate(PAIRS)}
PAIR_AT.update({(b, a): i for (a, b), i in list(PAIR_AT.items())})
BAND_ROWS = 48
SPILL_ROW = 44


def moment_row(pair, comp_pair):
    if comp_pair < 8:
        return 8 * pair + comp_pair
    if pair < 8:
        return 80 + 8 * (comp_pair - 8) + pair
    return 96 + 2 * (comp_pair - 8) + pair - 8


def select_rows():
    table = np.zeros((4, BAND_ROWS, 256), np.float32)
    for a in range(4):
        for lag in range(4 - a):
            for comp_pair in range(10):
                row = moment_row(PAIR_AT[(a, a + lag)], comp_pair)
                table[a, 10 * lag + comp_pair, row] = 1.0
                table[a, 10 * lag + comp_pair, 128 + row] = 1.0
        for comp in range(4):
            table[a, 40 + comp, 104 + 4 * a + comp] = 1.0
            table[a, 40 + comp, 128 + 104 + 4 * a + comp] = 1.0
    return table


def filter_tables():
    rate = 0.1 ** (1.0 / NK)
    gain = FILTER_GAIN * (1.0 - rate) ** 2 / (1.0 - rate * rate)
    lane = np.arange(128.0)
    row = np.arange(64.0)
    near = rate ** np.abs(lane[:, None] - lane[None, :])
    from_left = np.outer(rate ** (127 - lane), rate ** (lane + 1))
    from_right = np.outer(rate**lane, rate ** (128 - lane))
    edge = np.outer(rate ** (127 - lane), rate ** (128 - lane))
    within = gain * np.concatenate([near, from_left, from_right, edge], axis=1)
    gap = row[:, None] - row[None, :]
    left = np.where(gap > 0, rate ** (128 * np.maximum(gap - 1, 0)), 0.0)
    right = np.where(gap < 0, rate ** (128 * np.maximum(-gap - 1, 0)), 0.0)
    closing = -np.outer(rate ** (NK - 128 * row - 128), rate ** (NK - 128 * row - 127))
    across = np.concatenate([left, right, closing], axis=1)
    return within.astype(np.float32), across.astype(np.float32)


def split_two(value):
    high = value.astype(BF16).astype(F32)
    return jnp.concatenate([high, value - high], axis=0).astype(BF16)


def split_three(value):
    high = value.astype(BF16).astype(F32)
    rest = value - high
    middle = rest.astype(BF16).astype(F32)
    return jnp.concatenate([high, middle, rest - middle, jnp.zeros_like(value)], axis=0).astype(BF16)


def spread(ref, u, rows=8):
    return jnp.broadcast_to(ref[u : u + 1, :], (rows, 128))


def hot_lanes(low, count=128):
    want = lax.broadcasted_iota(jnp.int32, (count, low.shape[1]), 0)
    return jnp.where(jnp.broadcast_to(low, want.shape) == want, 1.0, 0.0).astype(BF16)


def cal_kernel(cal_ref, weight_ref, across_ref, resid_ref, out_ref):
    sub = lax.broadcasted_iota(jnp.int32, (8, 128), 0)
    quarter = sub & 3
    upper = sub < 4

    def step(i, total):
        rows = pl.ds(pl.multiple_of(8 * i, 8), 8)
        ids, weight = cal_ref[rows, :], weight_ref[rows, :]
        shift, resid = across_ref[rows, :], resid_ref[rows, :]
        weighted = weight * shift
        second = weighted * shift
        third = weight * resid
        fourth = weighted * resid
        tiles, hots = [], []
        for u in range(8):
            mask = spread(ids >> 7, u) == quarter
            pick = lambda top, low: jnp.where(
                mask, jnp.where(upper, spread(top, u), spread(low, u)), 0.0
            )
            zero = jnp.zeros_like(weight)
            tiles.append(
                jnp.concatenate([pick(weight, weighted), pick(second, third), pick(fourth, zero)], axis=0)
            )
            hots.append(hot_lanes((ids & 127)[u : u + 1, :]))
        terms = split_two(jnp.concatenate(tiles, axis=1))
        hot = jnp.concatenate(hots, axis=1)
        return total + lax.dot_general(
            terms, hot, (((1,), (1,)), ((), ())), preferred_element_type=F32
        )

    total = lax.fori_loop(0, 8, step, jnp.zeros((48, 128), F32))
    out_ref[...] = total[:24] + total[24:]


def window_kernel(
    counts_ref, cal_ref, weight_ref, across_ref, resid_ref, knot_ref, phase_ref, partial_ref,
    totals_ref, out_ref, step_ref, table,
):
    prior = float(OBS_DEV * N_SRC * N_TM // NCAL)
    totals = totals_ref[0]
    for i in range(1, N_SRC):
        totals = totals + totals_ref[i]
    zero_moment = totals[0:4] + prior
    first = totals[4:8]
    second_moment = totals[8:12] + prior
    third, fourth = totals[12:16], totals[16:20]
    det = zero_moment * second_moment - first * first
    offset = (second_moment * third - first * fourth) / det
    slope = (zero_moment * fourth - first * third) / det
    for h in range(4):
        step_ref[0:1, 128 * h : 128 * (h + 1)] = offset[h : h + 1]
        step_ref[1:2, 128 * h : 128 * (h + 1)] = slope[h : h + 1]
    pieces = split_three(jnp.concatenate([offset, slope], axis=0))
    sub = lax.broadcasted_iota(jnp.int32, (8, 128), 0)
    lane = lax.broadcasted_iota(jnp.int32, (8, 128), 1)

    def step(i, carry):
        rows = pl.ds(pl.multiple_of(8 * i, 8), 8)
        ids, weight = cal_ref[rows, :], weight_ref[rows, :]
        shift, resid = across_ref[rows, :], resid_ref[rows, :]
        knot, phase = knot_ref[rows, :].astype(F32), phase_ref[rows, :]
        hot = jnp.concatenate([hot_lanes((ids & 127)[u : u + 1, :]) for u in range(8)], axis=1)
        found = lax.dot_general(pieces, hot, (((1,), (0,)), ((), ())), preferred_element_type=F32)
        found = found[0:8] + found[8:16] + found[16:24]
        lanes = pl.ds(pl.multiple_of(1024 * i, 1024), 1024)
        table[0:4, lanes] = partial_ref[:, lanes]
        for u in range(8):
            mask = spread(ids >> 7, u) == (sub & 3)
            factor = jnp.where(sub < 4, 1.0, spread(shift, u))
            part = jnp.where(mask, found[:, 128 * u : 128 * (u + 1)], 0.0) * factor
            corrected = resid[u : u + 1, :] - jnp.sum(part, axis=0, keepdims=True)
            here = pl.ds(pl.multiple_of(1024 * i + 128 * u, 128), 128)
            table[4:8, here] = jnp.concatenate(
                [knot[u : u + 1], phase[u : u + 1], weight[u : u + 1], corrected], axis=0
            )
        return carry

    lax.fori_loop(0, 8, step, 0)
    begin = jnp.int32(0)
    dead = jnp.where(sub == 4, -1.0, 0.0)
    for block in range(N_TM):
        count = counts_ref[0, block]
        base = pl.multiple_of((begin >> 7) << 7, 128)
        off = begin & 127
        back = (128 - off) & 127
        rolled = pltpu.roll(table[:, pl.ds(base, 128)], back, 1)
        for j in range(CAP // 128):
            after = pltpu.roll(table[:, pl.ds(base + 128 * (j + 1), 128)], back, 1)
            tile = jnp.where(lane < 128 - off, rolled, after)
            out_ref[block, :, 128 * j : 128 * (j + 1)] = jnp.where(lane + 128 * j < count, tile, dead)
            rolled = after
        begin = begin + count


def moment_kernel(windows_ref, select_ref, out_ref, total, counts):
    total[...] = jnp.zeros_like(total)
    for block in range(N_TM):
        counts[block] = jnp.sum((windows_ref[block, 4:5, :] >= 0.0).astype(jnp.int32))
    knots = lax.broadcasted_iota(jnp.int32, (K, CHUNK), 0).astype(F32)

    def chunk_rows(tile):
        part = [tile[c : c + 1] for c in range(4)]
        phase, weight, resid = tile[5:6], tile[6:7], tile[7:8]
        square = phase * phase
        cube = square * phase
        remain = 1.0 - phase
        basis = [
            remain * remain * remain * (1.0 / 6.0),
            (3.0 * cube - 6.0 * square + 4.0) * (1.0 / 6.0),
            (-3.0 * cube + 3.0 * square + 3.0 * phase + 1.0) * (1.0 / 6.0),
            cube * (1.0 / 6.0),
        ]
        both = [basis[a] * basis[b] for a, b in PAIRS]
        left = jnp.concatenate([part[c] for c, e in PAIRS[:8]], axis=0)
        right = jnp.concatenate([part[e] for c, e in PAIRS[:8]], axis=0)
        eight = weight * left * right
        ninth, tenth = weight * part[2] * part[3], weight * part[3] * part[3]
        rows = [both[i] * eight for i in range(10)]
        stack = jnp.concatenate(both[:8], axis=0)
        rows.append(stack * ninth)
        rows.append(stack * tenth)
        zero = jnp.zeros_like(phase)
        rows.append(
            jnp.concatenate(
                [both[8] * ninth, both[9] * ninth, both[8] * tenth, both[9] * tenth] + [zero] * 4, axis=0
            )
        )
        four = tile[0:4] * (weight * resid)
        double = jnp.concatenate([four, four], axis=0)
        for a in (0, 2):
            order = jnp.concatenate([basis[a]] * 4 + [basis[a + 1]] * 4, axis=0)
            rows.append(double * order)
        rows.append(jnp.zeros_like(eight))
        return split_two(jnp.concatenate(rows, axis=0))

    def block_step(block, carry):
        def step(i, inner):
            tile = windows_ref[block, :, pl.ds(pl.multiple_of(i * CHUNK, CHUNK), CHUNK)]
            rows = chunk_rows(tile)
            hot = jnp.where(tile[4:5] == knots, 1.0, 0.0).astype(BF16)
            total[8 : 8 + K, :] += lax.dot_general(
                hot, rows, (((1,), (1,)), ((), ())), preferred_element_type=F32
            )
            return inner

        return lax.fori_loop(0, (counts[block] + CHUNK - 1) // CHUNK, step, carry)

    lax.fori_loop(0, N_TM, block_step, 0)
    band = jnp.zeros((BAND_ROWS, K), F32)
    spill = jnp.zeros((BAND_ROWS, 128), F32)
    for a in range(4):
        dot = functools.partial(
            lax.dot_general,
            select_ref[a],
            dimension_numbers=(((1,), (1,)), ((), ())),
            precision=HIGHEST,
            preferred_element_type=F32,
        )
        band = band + dot(total[8 - a : 8 - a + K, :])
        spill = spill + dot(total[8 + K - a : 8 + K - a + 128, :])
    for q in range(8):
        out_ref[:, q, :] = band[:, 128 * q : 128 * (q + 1)]
    packed = spill[0:8]
    for g in range(1, 6):
        packed = packed + pltpu.roll(spill[8 * g : 8 * g + 8], 8 * g, 1)
    out_ref[SPILL_ROW] = packed


def solve_kernel(
    place_ref, bands_ref, coeffs_ref, within_ref, across_ref, out_ref,
    band, inverse, field, ahead, lower, applied, resid, delta, filtered,
):
    lane8 = lax.broadcasted_iota(jnp.int32, (8, 128), 1)
    lane = lax.broadcasted_iota(jnp.int32, (64, 128), 1)
    for i in range(44):
        for t in range(N_TM):
            band[i, 8 * t : 8 * t + 8, :] = bands_ref[i // 3, t, 8 * (i % 3) : 8 * (i % 3) + 8, :]
    at, slot = SPILL_ROW // 3, 8 * (SPILL_ROW % 3)
    for t in range(N_TM - 1):
        packed = bands_ref[at, t, slot : slot + 8, :]
        for g in range(6):
            moved = packed if g == 0 else pltpu.roll(packed, 128 - 8 * g, 1)
            moved = jnp.where(lane8 < 3, moved, 0.0)
            for u in range(min(8, 44 - 8 * g)):
                row = 8 * (t + 1)
                band[8 * g + u, row : row + 1, :] += moved[u : u + 1]
    for c in range(4):
        inverse[c] = 1.0 / (ATTITUDE_PRIOR + band[PAIR_AT[(c, c)]])
    field[...] = jnp.zeros_like(field)
    lower[...] = jnp.zeros_like(lower)

    def total_of(left, right):
        value = left * right
        value = jnp.sum(value.reshape(32, 8, 128), axis=0)
        return jnp.sum(jnp.sum(value, axis=0, keepdims=True), axis=1, keepdims=True)

    def precondition():
        res = resid[...].reshape(256, 128)
        spreads = jnp.dot(res, within_ref[...], precision=HIGHEST, preferred_element_type=F32)
        for c in range(4):
            own = spreads[64 * c : 64 * c + 64]
            carried = jnp.concatenate([own[:, 128:256], own[:, 256:384], own[:, 384:512]], axis=0)
            carry = jnp.dot(across_ref[...], carried, precision=HIGHEST, preferred_element_type=F32)
            filtered[c] = resid[c] * inverse[c] + own[:, :128] + carry

    def apply_normals():
        for e in range(4):
            here, after = field[e, 8:72, :], field[e, 9:73, :]
            for d in range(1, 4):
                ahead[d - 1, e] = pltpu.roll(jnp.where(lane < d, after, here), 128 - d, 1)
        for t in range(N_TM):
            rows = slice(8 * t, 8 * t + 8)
            padded = slice(8 * t + 8, 8 * t + 16)
            own = [field[e, padded, :] for e in range(4)]
            sums = [own[c] * ATTITUDE_PRIOR for c in range(4)]
            for d in range(4):
                near = own if d == 0 else [ahead[d - 1, e, rows, :] for e in range(4)]
                tiles = [band[10 * d + i, rows, :] for i in range(10)]
                for c in range(4):
                    for e in range(4):
                        sums[c] = sums[c] + tiles[PAIR_AT[(c, e)]] * near[e]
                if d:
                    for c in range(4):
                        back = tiles[PAIR_AT[(c, 0)]] * own[0]
                        for e in range(1, 4):
                            back = back + tiles[PAIR_AT[(c, e)]] * own[e]
                        lower[d - 1, c, padded, :] = back
            for c in range(4):
                applied[c, rows, :] = sums[c]
        for c in range(4):
            result = applied[c]
            for d in range(1, 4):
                here, before = lower[d - 1, c, 8:72, :], lower[d - 1, c, 7:71, :]
                result = result + pltpu.roll(jnp.where(lane >= 128 - d, before, here), d, 1)
            applied[c] = result

    resid[...] = band[40:44]
    precondition()
    field[:, 8:72, :] = filtered[...]
    delta[...] = jnp.zeros_like(delta)
    energy = total_of(resid[...], filtered[...])

    def iterate(i, energy):
        apply_normals()
        step = energy / total_of(field[:, 8:72, :], applied[...])
        delta[...] += step * field[:, 8:72, :]
        resid[...] -= step * applied[...]
        precondition()
        fresh = total_of(resid[...], filtered[...])
        field[:, 8:72, :] = filtered[...] + (fresh / energy) * field[:, 8:72, :]
        return fresh

    energy = lax.fori_loop(0, ITERS - 1, iterate, energy)
    apply_normals()
    step = energy / total_of(field[:, 8:72, :], applied[...])
    delta[...] += step * field[:, 8:72, :]
    mine = pl.ds(pl.multiple_of(place_ref[0] * 8, 8), 8)
    for c in range(4):
        tile = delta[c, mine, :]
        for q in range(8):
            lanes = slice(128 * q, 128 * q + 128)
            out_ref[c : c + 1, lanes] = coeffs_ref[c : c + 1, lanes] + tile[q : q + 1]


VMEM_SPEC = pl.BlockSpec(memory_space=pltpu.VMEM)
SMEM_SPEC = pl.BlockSpec(memory_space=pltpu.SMEM)
PARAMS = pltpu.CompilerParams(vmem_limit_bytes=VMEM_LIMIT)


def local(
    knot_index, block_counts, knot_phase, partials, obs_weight, residuals, cal_id, across, coeffs
):
    dense = lambda value: value.reshape(64, 128)
    ids, weight, shift, resid = dense(cal_id), dense(obs_weight), dense(across), dense(residuals)
    with jax.named_scope("cal_sums"):
        sums = pl.pallas_call(
            cal_kernel,
            out_shape=jax.ShapeDtypeStruct((24, 128), F32),
            in_specs=[VMEM_SPEC] * 4,
            out_specs=VMEM_SPEC,
            compiler_params=PARAMS,
        )(ids, weight, shift, resid)
    with jax.named_scope("cal_reduce"):
        every = lax.all_to_all(jnp.broadcast_to(sums, (N_TM, 24, 128)), "tm", 0, 0)
        sums = jnp.sum(every, axis=0)
        totals = lax.all_to_all(jnp.broadcast_to(sums, (N_SRC, 24, 128)), "src", 0, 0)
    with jax.named_scope("windows"):
        windows, calibration_step = pl.pallas_call(
            window_kernel,
            out_shape=(
                jax.ShapeDtypeStruct((N_TM, 8, CAP), F32),
                jax.ShapeDtypeStruct((2, NCAL), F32),
            ),
            in_specs=[SMEM_SPEC] + [VMEM_SPEC] * 8,
            out_specs=(VMEM_SPEC, VMEM_SPEC),
            scratch_shapes=[pltpu.VMEM((8, OBS_DEV + CAP + 128), F32)],
            compiler_params=PARAMS,
        )(block_counts, ids, weight, shift, resid, dense(knot_index), dense(knot_phase), partials, totals)
    with jax.named_scope("to_owners"):
        windows = lax.all_to_all(windows, "tm", 0, 0)
    with jax.named_scope("moments"):
        band = pl.pallas_call(
            moment_kernel,
            out_shape=jax.ShapeDtypeStruct((BAND_ROWS, 8, 128), F32),
            in_specs=[VMEM_SPEC] * 2,
            out_specs=VMEM_SPEC,
            scratch_shapes=[
                pltpu.VMEM((8 + K + 136, 256), F32),
                pltpu.SMEM((N_TM,), jnp.int32),
            ],
            compiler_params=PARAMS,
        )(windows, jnp.asarray(select_rows()))
    with jax.named_scope("band_reduce"):
        share = lax.all_to_all(band.reshape(N_SRC, 24, 128), "src", 0, 0)
        share = jnp.sum(share, axis=0)
    with jax.named_scope("band_gather"):
        column = lax.all_to_all(jnp.broadcast_to(share, (N_TM, 24, 128)), "tm", 0, 0)
        bands = lax.all_to_all(
            jnp.broadcast_to(column, (N_SRC, N_TM, 24, 128)).reshape(N_SRC, N_TM * 24, 128), "src", 0, 0
        ).reshape(N_SRC, N_TM, 24, 128)
    within, across_rows = filter_tables()
    with jax.named_scope("solve"):
        new_coeffs = pl.pallas_call(
            solve_kernel,
            out_shape=jax.ShapeDtypeStruct((4, K), F32),
            in_specs=[SMEM_SPEC] + [VMEM_SPEC] * 4,
            out_specs=VMEM_SPEC,
            scratch_shapes=[
                pltpu.VMEM((44, 64, 128), F32),
                pltpu.VMEM((4, 64, 128), F32),
                pltpu.VMEM((4, 80, 128), F32),
                pltpu.VMEM((3, 4, 64, 128), F32),
                pltpu.VMEM((3, 4, 80, 128), F32),
                pltpu.VMEM((4, 64, 128), F32),
                pltpu.VMEM((4, 64, 128), F32),
                pltpu.VMEM((4, 64, 128), F32),
                pltpu.VMEM((4, 64, 128), F32),
            ],
            compiler_params=PARAMS,
        )(lax.axis_index("tm").reshape(1), bands, coeffs, jnp.asarray(within), jnp.asarray(across_rows))
    return (new_coeffs, calibration_step)


def solution(mesh):
    placed = (
        P(("src", "tm")),
        P(("src", "tm"), None),
        P(("src", "tm")),
        P(None, ("src", "tm")),
        P(("src", "tm")),
        P(("src", "tm")),
        P(("src", "tm")),
        P(("src", "tm")),
        P(None, "tm"),
    )
    return jax.shard_map(
        local, mesh=mesh, in_specs=placed, out_specs=(P(None, "tm"), P()), check_vma=False
    )
```

```python
import jax
import jax.numpy as jnp
import numpy as np
from jax import lax
from jax.experimental import pallas as pl
from jax.experimental.pallas import tpu as pltpu
from jax.sharding import PartitionSpec as P

K = 1024
OBS_DEV = 8192
NCAL = 512
ITERS = 6
N_SRC = 16
N_TM = 8
NK = K * N_TM
CAP = 2 * OBS_DEV // N_TM
ATTITUDE_PRIOR = 1.0
FILTER_GAIN = 0.05
CHUNK = 512
HIGHEST = lax.Precision.HIGHEST
F32 = jnp.float32
BF16 = jnp.bfloat16
VMEM_LIMIT = 48 * 1024 * 1024

PAIRS = [(a, b) for a in range(4) for b in range(a, 4)]
PAIR_AT = {pair: i for i, pair in enumerate(PAIRS)}
PAIR_AT.update({(b, a): i for (a, b), i in list(PAIR_AT.items())})
SPILL, SIDE, SIDE_SPILL, TILES = 40, 48, 52, 53
MORE, SUMS, WIDTH = CAP, CAP + CHUNK, CAP + CHUNK + 384


def moment_row(pair, comp_pair):
    if comp_pair < 8:
        return 8 * pair + comp_pair
    if pair < 8:
        return 80 + 8 * (comp_pair - 8) + pair
    return 96 + 2 * (comp_pair - 8) + pair - 8


def select_rows():
    table = np.zeros((4, 40, 256), np.float32)
    for a in range(4):
        for lag in range(4 - a):
            for comp_pair in range(10):
                row = moment_row(PAIR_AT[(a, a + lag)], comp_pair)
                table[a, 10 * lag + comp_pair, row] = 1.0
                table[a, 10 * lag + comp_pair, 128 + row] = 1.0
    return table.reshape(160, 256)


def filter_tables():
    rate = 0.1 ** (1.0 / NK)
    gain = FILTER_GAIN * (1.0 - rate) ** 2 / (1.0 - rate * rate)
    lane = np.arange(128.0)
    row = np.arange(64.0)
    near = rate ** np.abs(lane[:, None] - lane[None, :])
    from_left = np.outer(rate ** (127 - lane), rate ** (lane + 1))
    from_right = np.outer(rate**lane, rate ** (128 - lane))
    edge = np.outer(rate ** (127 - lane), rate ** (128 - lane))
    within = gain * np.concatenate([near, from_left, from_right, edge], axis=1)
    gap = row[:, None] - row[None, :]
    left = np.where(gap > 0, rate ** (128 * np.maximum(gap - 1, 0)), 0.0)
    right = np.where(gap < 0, rate ** (128 * np.maximum(-gap - 1, 0)), 0.0)
    closing = -np.outer(rate ** (NK - 128 * row - 128), rate ** (NK - 128 * row - 127))
    across = np.concatenate([left, right, closing], axis=1)
    return within.astype(np.float32), across.astype(np.float32)


def split_two(value):
    high = value.astype(BF16).astype(F32)
    return jnp.concatenate([high, value - high], axis=0).astype(BF16)


def split_three(value):
    high = value.astype(BF16).astype(F32)
    rest = value - high
    middle = rest.astype(BF16).astype(F32)
    return jnp.concatenate([high, middle, rest - middle, jnp.zeros_like(value)], axis=0).astype(BF16)


def spread(value, u, rows=8):
    return jnp.broadcast_to(value[u : u + 1, :], (rows, value.shape[1]))


def sixteen(row):
    return jnp.broadcast_to(row, (16, row.shape[1])).astype(BF16)


def hot_lanes(low, count):
    low = sixteen(low)
    want = lax.broadcasted_iota(jnp.int32, low.shape, 0).astype(F32).astype(BF16)
    one, zero = jnp.ones_like(low), jnp.zeros_like(low)
    return jnp.concatenate(
        [jnp.where(low == want + BF16(16 * j), one, zero) for j in range(count // 16)], axis=0
    )


def grouped(rows, group, count):
    parts = []
    for g in range(count):
        mask = sixteen(jnp.where(group == float(g), 1.0, 0.0))
        parts.append(rows * jnp.concatenate([mask] * (rows.shape[0] // 16), axis=0))
    return jnp.concatenate(parts, axis=0)


def outer(rows, hot):
    return lax.dot_general(rows, hot, (((1,), (1,)), ((), ())), preferred_element_type=F32)


def window_kernel(
    counts_ref, cal_hbm, weight_hbm, across_hbm, resid_hbm, knot_hbm, phase_hbm, partial_hbm,
    out_ref, cal_ref, weight_ref, across_ref, resid_ref, knot_ref, phase_ref, partial_ref,
    table, more, sems,
):
    pairs = [
        (cal_hbm, cal_ref), (weight_hbm, weight_ref), (across_hbm, across_ref), (resid_hbm, resid_ref),
        (knot_hbm, knot_ref), (phase_hbm, phase_ref), (partial_hbm, partial_ref),
    ]
    copies = [pltpu.make_async_copy(a, b, sems.at[i]) for i, (a, b) in enumerate(pairs)]
    for copy in copies:
        copy.start()
    for copy in copies:
        copy.wait()
    sub = lax.broadcasted_iota(jnp.int32, (8, 128), 0)
    lane = lax.broadcasted_iota(jnp.int32, (8, 128), 1)
    quarter = sub & 3
    upper = sub < 4

    def step(i, total):
        rows = pl.ds(pl.multiple_of(8 * i, 8), 8)
        ids, weight = cal_ref[rows, :], weight_ref[rows, :]
        shift, resid = across_ref[rows, :], resid_ref[rows, :]
        knot, phase = knot_ref[rows, :].astype(F32), phase_ref[rows, :]
        low, high = (ids & 127).astype(F32), ids >> 7
        number = ids.astype(F32)
        weighted = weight * shift
        second = weighted * shift
        third = weight * resid
        fourth = weighted * resid
        tiles, hots = [], []
        for u in range(8):
            mask = spread(high, u) == quarter

            def pick(top, bottom):
                return jnp.where(mask, jnp.where(upper, spread(top, u), spread(bottom, u)), 0.0)

            last = jnp.where(mask & upper, spread(fourth, u), 0.0)
            tiles.append(jnp.concatenate([pick(weight, weighted), pick(second, third), last], axis=0))
            hots.append(hot_lanes(low[u : u + 1, :], 128))
            here = pl.ds(pl.multiple_of(1024 * i + 128 * u, 128), 128)
            table[4:8, here] = jnp.concatenate(
                [knot[u : u + 1], phase[u : u + 1], weight[u : u + 1], resid[u : u + 1]], axis=0
            )
            more[0:2, here] = jnp.concatenate([shift[u : u + 1], number[u : u + 1]], axis=0)
        lanes = pl.ds(pl.multiple_of(1024 * i, 1024), 1024)
        table[0:4, lanes] = partial_ref[:, lanes]
        return total + outer(split_two(jnp.concatenate(tiles, axis=1)), jnp.concatenate(hots, axis=1))

    total = lax.fori_loop(0, 8, step, jnp.zeros((48, 128), F32))
    total = total[:24] + total[24:]
    begin = jnp.int32(0)
    dead = jnp.where(sub == 4, -1.0, 0.0)
    for block in range(N_TM):
        count = counts_ref[0, block]
        base = pl.multiple_of((begin >> 7) << 7, 128)
        off = begin & 127
        back = (128 - off) & 127
        early = lane < 128 - off
        rolled = pltpu.roll(table[:, pl.ds(base, 128)], back, 1)
        rolled_more = pltpu.roll(more[:, pl.ds(base, 128)], back, 1)
        for j in range(CAP // 128):
            here = pl.ds(base + 128 * (j + 1), 128)
            after = pltpu.roll(table[:, here], back, 1)
            after_more = pltpu.roll(more[:, here], back, 1)
            live = lane + 128 * j < count
            out_ref[block, :, 128 * j : 128 * (j + 1)] = jnp.where(
                live, jnp.where(early, rolled, after), dead
            )
            tile = jnp.where(live, jnp.where(early, rolled_more, after_more), 0.0)
            row, lanes = j // 4, slice(MORE + 128 * (j % 4), MORE + 128 * (j % 4) + 128)
            out_ref[block, row : row + 1, lanes] = tile[0:1]
            out_ref[block, 4 + row : 5 + row, lanes] = tile[1:2]
            rolled, rolled_more = after, after_more
        for k in range(3):
            out_ref[block, :, SUMS + 128 * k : SUMS + 128 * (k + 1)] = total[8 * k : 8 * k + 8]
        begin = begin + count


def count_live(windows_ref, counts):
    for block in range(N_TM):
        counts[block] = jnp.sum((windows_ref[block, 4:5, :CAP] >= 0.0).astype(jnp.int32))


def each_chunk(counts, body):
    def block_step(block, carry):
        def step(i, inner):
            body(block, i)
            return inner

        return lax.fori_loop(0, (counts[block] + CHUNK - 1) // CHUNK, step, carry)

    lax.fori_loop(0, N_TM, block_step, 0)


def spline_basis(phase):
    square = phase * phase
    cube = square * phase
    remain = 1.0 - phase
    return [
        remain * remain * remain * (1.0 / 6.0),
        (3.0 * cube - 6.0 * square + 4.0) * (1.0 / 6.0),
        (-3.0 * cube + 3.0 * square + 3.0 * phase + 1.0) * (1.0 / 6.0),
        cube * (1.0 / 6.0),
    ]


def moment_kernel(windows_ref, select_ref, out_ref, total, tiles, counts):
    total[...] = jnp.zeros_like(total)
    count_live(windows_ref, counts)

    def body(block, i):
        tile = windows_ref[block, :, pl.ds(pl.multiple_of(i * CHUNK, CHUNK), CHUNK)]
        part = [tile[c : c + 1] for c in range(4)]
        knot, phase, weight = tile[4:5], tile[5:6], tile[6:7]
        basis = spline_basis(phase)
        both = [basis[a] * basis[b] for a, b in PAIRS]
        left = jnp.concatenate([part[c] for c, e in PAIRS[:8]], axis=0)
        right = jnp.concatenate([part[e] for c, e in PAIRS[:8]], axis=0)
        eight = weight * left * right
        ninth, tenth = weight * part[2] * part[3], weight * part[3] * part[3]
        rows = [both[i] * eight for i in range(10)]
        stack = jnp.concatenate(both[:8], axis=0)
        rows.append(stack * ninth)
        rows.append(stack * tenth)
        rows.append(
            jnp.concatenate(
                [both[8] * ninth, both[9] * ninth, both[8] * tenth, both[9] * tenth]
                + [jnp.zeros_like(phase)] * 4,
                axis=0,
            )
        )
        rows += [jnp.zeros_like(eight)] * 3
        rows = split_two(jnp.concatenate(rows, axis=0))
        group = jnp.floor(knot * (1.0 / 256.0))
        low = jnp.maximum(knot, 0.0) - 256.0 * jnp.maximum(group, 0.0)
        total[...] += outer(grouped(rows, group, 4), hot_lanes(low, 256))

    each_chunk(counts, body)
    parts = [
        jnp.dot(
            select_ref[...], total[256 * g : 256 * g + 256], precision=HIGHEST, preferred_element_type=F32
        )
        for g in range(4)
    ]
    parts.append(jnp.zeros((160, 128), F32))
    orders = jnp.concatenate(parts, axis=1)
    band = orders[0:40]
    for a in range(1, 4):
        band = band + pltpu.roll(orders[40 * a : 40 * a + 40], a, 1)
    for q in range(8):
        tiles[0:40, q, :] = band[:, 128 * q : 128 * (q + 1)]
    spill = band[:, K : K + 128]
    packed = spill[0:8]
    for g in range(1, 5):
        packed = packed + pltpu.roll(spill[8 * g : 8 * g + 8], 8 * g, 1)
    tiles[SPILL] = packed
    sums = windows_ref[0, :, SUMS:WIDTH]
    for block in range(1, N_TM):
        sums = sums + windows_ref[block, :, SUMS:WIDTH]
    for s in range(N_SRC):
        for r in range(3):
            at = 3 * s + r
            out_ref[s, 8 * r : 8 * r + 8, :] = tiles[at] if at <= SPILL else jnp.zeros((8, 128), F32)
            out_ref[s, 24 + 8 * r : 32 + 8 * r, :] = sums[:, 128 * r : 128 * (r + 1)]


def side_kernel(windows_ref, parts_ref, out_ref, step_ref, total, counts):
    total[...] = jnp.zeros_like(total)
    count_live(windows_ref, counts)
    both = parts_ref[0]
    for s in range(1, N_SRC):
        both = both + parts_ref[s]
    prior = float(OBS_DEV * N_SRC * N_TM // NCAL)
    totals = both[24:48]
    zero_moment = totals[0:4] + prior
    first = totals[4:8]
    second_moment = totals[8:12] + prior
    third, fourth = totals[12:16], totals[16:20]
    det = zero_moment * second_moment - first * first
    offset = (second_moment * third - first * fourth) / det
    slope = (zero_moment * fourth - first * third) / det
    for h in range(4):
        step_ref[0:1, 128 * h : 128 * (h + 1)] = offset[h : h + 1]
        step_ref[1:2, 128 * h : 128 * (h + 1)] = slope[h : h + 1]
    pieces = split_three(jnp.concatenate([offset, slope], axis=0))
    sub = lax.broadcasted_iota(jnp.int32, (8, CHUNK), 0)
    quarter = (sub & 3).astype(F32)
    upper = sub < 4

    def body(block, i):
        tile = windows_ref[block, :, pl.ds(pl.multiple_of(i * CHUNK, CHUNK), CHUNK)]
        shift = windows_ref[block, pl.ds(i, 1), MORE:SUMS]
        ids = windows_ref[block, pl.ds(4 + i, 1), MORE:SUMS]
        knot, phase, weight, resid = tile[4:5], tile[5:6], tile[6:7], tile[7:8]
        high = jnp.floor(ids * (1.0 / 128.0))
        found = jnp.dot(pieces, hot_lanes(ids - 128.0 * high, 128), preferred_element_type=F32)
        found = found[0:8] + found[8:16] + found[16:24]
        found = jnp.where(quarter == high, found, 0.0) * jnp.where(upper, 1.0, shift)
        corrected = resid - jnp.sum(found, axis=0, keepdims=True)
        basis = spline_basis(phase)
        four = tile[0:4] * (weight * corrected)
        double = jnp.concatenate([four, four], axis=0)
        rows = []
        for a in (0, 2):
            order = jnp.concatenate([basis[a]] * 4 + [basis[a + 1]] * 4, axis=0)
            rows.append(double * order)
        rows = split_two(jnp.concatenate(rows, axis=0))
        group = jnp.floor(knot * (1.0 / 128.0))
        low = jnp.maximum(knot, 0.0) - 128.0 * jnp.maximum(group, 0.0)
        total[...] += outer(grouped(rows, group, 8), hot_lanes(low, 128))

    each_chunk(counts, body)
    orders = [total[32 * g : 32 * g + 16] + total[32 * g + 16 : 32 * g + 32] for g in range(8)]
    orders = jnp.concatenate(orders + [jnp.zeros((16, 128), F32)], axis=1)
    side = orders[0:4]
    for a in range(1, 4):
        side = side + pltpu.roll(orders, a, 1)[4 * a : 4 * a + 4]
    share = both[0:24]
    spill = jnp.concatenate([side[:, K : K + 128], jnp.zeros((4, 128), F32)], axis=0)
    rows = [share]
    for c in range(4):
        rows += [side[c : c + 1, 128 * q : 128 * (q + 1)] for q in range(8)]
    rows = jnp.concatenate(rows + [spill], axis=0)
    for s in range(N_SRC):
        out_ref[s] = rows


def gather_kernel(parts_ref, out_ref):
    side = parts_ref[0, 24:64, :]
    for s in range(1, N_SRC):
        side = side + parts_ref[s, 24:64, :]
    for copy in range(4):
        for s in range(N_SRC):
            out_ref[copy, 24 * s : 24 * s + 24, :] = parts_ref[s, 0:24, :]
        out_ref[copy, 384:424, :] = side


def solve_kernel(
    place_ref, mine_ref, other_ref, coeffs_ref, within_ref, across_ref, out_ref,
    band, inverse, field, ahead, lower, applied, resid, delta, filtered,
):
    lane8 = lax.broadcasted_iota(jnp.int32, (8, 128), 1)
    lane = lax.broadcasted_iota(jnp.int32, (64, 128), 1)
    core = place_ref[0] & 1
    halves = ((mine_ref, core), (other_ref, 1 - core))
    for ref, parity in halves:
        for z in range(N_TM // 2):
            rows = pl.ds(pl.multiple_of(8 * (2 * z + parity), 8), 8)
            for i in range(44):
                at = i if i < 40 else SIDE + i - 40
                band[i, rows, :] = ref[z, 8 * at : 8 * at + 8, :]
    for ref, parity in halves:
        for z in range(N_TM // 2):
            row = pl.ds(pl.multiple_of(8 * (2 * z + parity) + 8, 8), 1)
            packed = ref[z, 8 * SPILL : 8 * SPILL + 8, :]
            for g in range(5):
                moved = packed if g == 0 else pltpu.roll(packed, 128 - 8 * g, 1)
                moved = jnp.where(lane8 < 3, moved, 0.0)
                for u in range(8):
                    band[8 * g + u, row, :] += moved[u : u + 1]
            moved = ref[z, 8 * SIDE_SPILL : 8 * SIDE_SPILL + 8, :]
            for u in range(4):
                band[40 + u, row, :] += moved[u : u + 1]
    for c in range(4):
        inverse[c] = 1.0 / (ATTITUDE_PRIOR + band[PAIR_AT[(c, c)], 0:64, :])
    field[...] = jnp.zeros_like(field)
    lower[...] = jnp.zeros_like(lower)

    def total_of(left, right):
        value = left * right
        value = jnp.sum(value.reshape(32, 8, 128), axis=0)
        return jnp.sum(jnp.sum(value, axis=0, keepdims=True), axis=1, keepdims=True)

    def precondition():
        res = resid[...].reshape(256, 128)
        spreads = jnp.dot(res, within_ref[...], precision=HIGHEST, preferred_element_type=F32)
        for c in range(4):
            own = spreads[64 * c : 64 * c + 64]
            carried = jnp.concatenate([own[:, 128:256], own[:, 256:384], own[:, 384:512]], axis=0)
            carry = jnp.dot(across_ref[...], carried, precision=HIGHEST, preferred_element_type=F32)
            filtered[c] = resid[c] * inverse[c] + own[:, :128] + carry

    def apply_normals():
        for e in range(4):
            here, after = field[e, 8:72, :], field[e, 9:73, :]
            for d in range(1, 4):
                ahead[d - 1, e] = pltpu.roll(jnp.where(lane < d, after, here), 128 - d, 1)
        for t in range(N_TM):
            rows = slice(8 * t, 8 * t + 8)
            padded = slice(8 * t + 8, 8 * t + 16)
            own = [field[e, padded, :] for e in range(4)]
            sums = [own[c] * ATTITUDE_PRIOR for c in range(4)]
            for d in range(4):
                near = own if d == 0 else [ahead[d - 1, e, rows, :] for e in range(4)]
                tiles = [band[10 * d + i, rows, :] for i in range(10)]
                for c in range(4):
                    for e in range(4):
                        sums[c] = sums[c] + tiles[PAIR_AT[(c, e)]] * near[e]
                if d:
                    for c in range(4):
                        back = tiles[PAIR_AT[(c, 0)]] * own[0]
                        for e in range(1, 4):
                            back = back + tiles[PAIR_AT[(c, e)]] * own[e]
                        lower[d - 1, c, padded, :] = back
            for c in range(4):
                applied[c, rows, :] = sums[c]
        for c in range(4):
            result = applied[c]
            for d in range(1, 4):
                here, before = lower[d - 1, c, 8:72, :], lower[d - 1, c, 7:71, :]
                result = result + pltpu.roll(jnp.where(lane >= 128 - d, before, here), d, 1)
            applied[c] = result

    resid[...] = band[40:44, 0:64, :]
    precondition()
    field[:, 8:72, :] = filtered[...]
    delta[...] = jnp.zeros_like(delta)
    energy = total_of(resid[...], filtered[...])

    def iterate(i, energy):
        apply_normals()
        step = energy / total_of(field[:, 8:72, :], applied[...])
        delta[...] += step * field[:, 8:72, :]
        resid[...] -= step * applied[...]
        precondition()
        fresh = total_of(resid[...], filtered[...])
        field[:, 8:72, :] = filtered[...] + (fresh / energy) * field[:, 8:72, :]
        return fresh

    energy = lax.fori_loop(0, ITERS - 1, iterate, energy)
    apply_normals()
    step = energy / total_of(field[:, 8:72, :], applied[...])
    delta[...] += step * field[:, 8:72, :]
    mine = pl.ds(pl.multiple_of(place_ref[0] * 8, 8), 8)
    for c in range(4):
        tile = delta[c, mine, :]
        for q in range(8):
            lanes = slice(128 * q, 128 * q + 128)
            out_ref[c : c + 1, lanes] = coeffs_ref[c : c + 1, lanes] + tile[q : q + 1]


VMEM_SPEC = pl.BlockSpec(memory_space=pltpu.VMEM)
SMEM_SPEC = pl.BlockSpec(memory_space=pltpu.SMEM)
HBM_SPEC = pl.BlockSpec(memory_space=pltpu.HBM)
PARAMS = pltpu.CompilerParams(vmem_limit_bytes=VMEM_LIMIT)
SAME_CORE = [[0, 2, 4, 6], [1, 3, 5, 7]]


def local(
    knot_index, block_counts, knot_phase, partials, obs_weight, residuals, cal_id, across, coeffs
):
    dense = [
        value.reshape(64, 128)
        for value in (cal_id, obs_weight, across, residuals, knot_index, knot_phase)
    ]
    with jax.named_scope("windows"):
        windows = pl.pallas_call(
            window_kernel,
            out_shape=jax.ShapeDtypeStruct((N_TM, 8, WIDTH), F32),
            in_specs=[SMEM_SPEC] + [HBM_SPEC] * 7,
            out_specs=VMEM_SPEC,
            scratch_shapes=[pltpu.VMEM((64, 128), value.dtype) for value in dense]
            + [
                pltpu.VMEM((4, OBS_DEV), F32),
                pltpu.VMEM((8, OBS_DEV + CAP + 128), F32),
                pltpu.VMEM((8, OBS_DEV + CAP + 128), F32),
                pltpu.SemaphoreType.DMA((7,)),
            ],
            compiler_params=PARAMS,
        )(block_counts, *dense, partials)
    with jax.named_scope("to_owners"):
        windows = lax.all_to_all(windows, "tm", 0, 0)
    with jax.named_scope("moments"):
        parts = pl.pallas_call(
            moment_kernel,
            out_shape=jax.ShapeDtypeStruct((N_SRC, 48, 128), F32),
            in_specs=[VMEM_SPEC] * 2,
            out_specs=VMEM_SPEC,
            scratch_shapes=[
                pltpu.VMEM((1024, 256), F32),
                pltpu.VMEM((SPILL + 1, 8, 128), F32),
                pltpu.SMEM((N_TM,), jnp.int32),
            ],
            compiler_params=PARAMS,
        )(windows, jnp.asarray(select_rows()))
    with jax.named_scope("band_reduce"):
        parts = lax.all_to_all(parts, "src", 0, 0)
    with jax.named_scope("side"):
        parts, calibration_step = pl.pallas_call(
            side_kernel,
            out_shape=(
                jax.ShapeDtypeStruct((N_SRC, 64, 128), F32),
                jax.ShapeDtypeStruct((2, NCAL), F32),
            ),
            in_specs=[VMEM_SPEC] * 2,
            out_specs=(VMEM_SPEC, VMEM_SPEC),
            scratch_shapes=[pltpu.VMEM((256, 128), F32), pltpu.SMEM((N_TM,), jnp.int32)],
            compiler_params=PARAMS,
        )(windows, parts)
    with jax.named_scope("gather_src"):
        parts = lax.all_to_all(parts, "src", 0, 0)
    with jax.named_scope("gather"):
        parts = pl.pallas_call(
            gather_kernel,
            out_shape=jax.ShapeDtypeStruct((4, 8 * TILES, 128), F32),
            in_specs=[VMEM_SPEC],
            out_specs=VMEM_SPEC,
            compiler_params=PARAMS,
        )(parts)
    with jax.named_scope("gather_z"):
        mine = lax.all_to_all(parts, "tm", 0, 0, axis_index_groups=SAME_CORE)
    with jax.named_scope("gather_core"):
        other = lax.ppermute(mine, "tm", [(i, i ^ 1) for i in range(N_TM)])
    within, across_rows = filter_tables()
    with jax.named_scope("solve"):
        new_coeffs = pl.pallas_call(
            solve_kernel,
            out_shape=jax.ShapeDtypeStruct((4, K), F32),
            in_specs=[SMEM_SPEC] + [VMEM_SPEC] * 5,
            out_specs=VMEM_SPEC,
            scratch_shapes=[
                pltpu.VMEM((44, 72, 128), F32),
                pltpu.VMEM((4, 64, 128), F32),
                pltpu.VMEM((4, 80, 128), F32),
                pltpu.VMEM((3, 4, 64, 128), F32),
                pltpu.VMEM((3, 4, 80, 128), F32),
                pltpu.VMEM((4, 64, 128), F32),
                pltpu.VMEM((4, 64, 128), F32),
                pltpu.VMEM((4, 64, 128), F32),
                pltpu.VMEM((4, 64, 128), F32),
            ],
            compiler_params=PARAMS,
        )(
            lax.axis_index("tm").reshape(1), mine, other, coeffs, jnp.asarray(within),
            jnp.asarray(across_rows),
        )
    return (new_coeffs, calibration_step)


def solution(mesh):
    placed = (
        P(("src", "tm")),
        P(("src", "tm"), None),
        P(("src", "tm")),
        P(None, ("src", "tm")),
        P(("src", "tm")),
        P(("src", "tm")),
        P(("src", "tm")),
        P(("src", "tm")),
        P(None, "tm"),
    )
    return jax.shard_map(
        local, mesh=mesh, in_specs=placed, out_specs=(P(None, "tm"), P()), check_vma=False
    )
```

```python
import jax
import jax.numpy as jnp
import numpy as np
from jax import lax
from jax.experimental import pallas as pl
from jax.experimental.pallas import tpu as pltpu
from jax.sharding import PartitionSpec as P

K = 1024
OBS_DEV = 8192
NCAL = 512
ITERS = 6
N_SRC = 16
N_TM = 8
NK = K * N_TM
CAP = 2 * OBS_DEV // N_TM
ATTITUDE_PRIOR = 1.0
FILTER_GAIN = 0.05
CHUNK = 512
HIGHEST = lax.Precision.HIGHEST
F32 = jnp.float32
BF16 = jnp.bfloat16
VMEM_LIMIT = 48 * 1024 * 1024

PAIRS = [(a, b) for a in range(4) for b in range(a, 4)]
PAIR_AT = {pair: i for i, pair in enumerate(PAIRS)}
PAIR_AT.update({(b, a): i for (a, b), i in list(PAIR_AT.items())})
SPILL, SIDE, TILES = 40, 41, 45
MORE, SUMS, WIDTH = CAP, CAP + CHUNK, CAP + CHUNK + 384
MOMENTS = 72
BINOMIAL = [1.0, 6.0, 15.0, 20.0, 15.0, 6.0, 1.0]


def select_rows():
    cubic = np.array([[1, 0, 0, 0], [4, 4, 2, 1], [1, 2, 4, 4], [0, 0, 0, 1]]) / 6.0
    scaled = cubic * np.array([1.0, 3.0, 3.0, 1.0])
    table = np.zeros((4, 40, 2 * MOMENTS))
    for a in range(4):
        for lag in range(4 - a):
            share = np.convolve(scaled[a], scaled[a + lag]) / np.array(BINOMIAL)
            for pair in range(10):
                for n in range(7):
                    row = 8 * n + pair if pair < 8 else 56 + 8 * (pair - 8) + n
                    table[a, 10 * lag + pair, row] = share[n]
                    table[a, 10 * lag + pair, MOMENTS + row] = share[n]
    return table.reshape(160, 2 * MOMENTS).astype(np.float32)


def filter_tables():
    rate = 0.1 ** (1.0 / NK)
    gain = FILTER_GAIN * (1.0 - rate) ** 2 / (1.0 - rate * rate)
    lane = np.arange(128.0)
    row = np.arange(64.0)
    near = rate ** np.abs(lane[:, None] - lane[None, :])
    from_left = np.outer(rate ** (127 - lane), rate ** (lane + 1))
    from_right = np.outer(rate**lane, rate ** (128 - lane))
    edge = np.outer(rate ** (127 - lane), rate ** (128 - lane))
    within = gain * np.concatenate([near, from_left, from_right, edge], axis=1)
    gap = row[:, None] - row[None, :]
    left = np.where(gap > 0, rate ** (128 * np.maximum(gap - 1, 0)), 0.0)
    right = np.where(gap < 0, rate ** (128 * np.maximum(-gap - 1, 0)), 0.0)
    closing = -np.outer(rate ** (NK - 128 * row - 128), rate ** (NK - 128 * row - 127))
    across = np.concatenate([left, right, closing], axis=1)
    return within.astype(np.float32), across.astype(np.float32)


def split_two(value):
    high = value.astype(BF16).astype(F32)
    return jnp.concatenate([high, value - high], axis=0).astype(BF16)


def split_three(value):
    high = value.astype(BF16).astype(F32)
    rest = value - high
    middle = rest.astype(BF16).astype(F32)
    return jnp.concatenate([high, middle, rest - middle, jnp.zeros_like(value)], axis=0).astype(BF16)


def spread(value, u, rows=8):
    return jnp.broadcast_to(value[u : u + 1, :], (rows, value.shape[1]))


def sixteen(row):
    return jnp.broadcast_to(row, (16, row.shape[1])).astype(BF16)


def hot_lanes(low, count):
    low = sixteen(low)
    want = lax.broadcasted_iota(jnp.int32, low.shape, 0).astype(F32).astype(BF16)
    one, zero = jnp.ones_like(low), jnp.zeros_like(low)
    return jnp.concatenate(
        [jnp.where(low == want + BF16(16 * j), one, zero) for j in range(count // 16)], axis=0
    )


def grouped(rows, group, count):
    parts = []
    for g in range(count):
        mask = sixteen(jnp.where(group == float(g), 1.0, 0.0))
        parts.append(rows * jnp.concatenate([mask] * (rows.shape[0] // 16), axis=0))
    return jnp.concatenate(parts, axis=0)


def outer(rows, hot):
    return lax.dot_general(rows, hot, (((1,), (1,)), ((), ())), preferred_element_type=F32)


def window_kernel(
    counts_ref, cal_hbm, weight_hbm, across_hbm, resid_hbm, knot_hbm, phase_hbm, partial_hbm,
    out_ref, cal_ref, weight_ref, across_ref, resid_ref, knot_ref, phase_ref, partial_ref,
    table, more, sems,
):
    pairs = [
        (cal_hbm, cal_ref), (weight_hbm, weight_ref), (across_hbm, across_ref), (resid_hbm, resid_ref),
        (knot_hbm, knot_ref), (phase_hbm, phase_ref), (partial_hbm, partial_ref),
    ]
    copies = [pltpu.make_async_copy(a, b, sems.at[i]) for i, (a, b) in enumerate(pairs)]
    for copy in copies:
        copy.start()
    for copy in copies:
        copy.wait()
    sub = lax.broadcasted_iota(jnp.int32, (8, 128), 0)
    lane = lax.broadcasted_iota(jnp.int32, (8, 128), 1)
    quarter = sub & 3
    upper = sub < 4

    def step(i, total):
        rows = pl.ds(pl.multiple_of(8 * i, 8), 8)
        ids, weight = cal_ref[rows, :], weight_ref[rows, :]
        shift, resid = across_ref[rows, :], resid_ref[rows, :]
        knot, phase = knot_ref[rows, :].astype(F32), phase_ref[rows, :]
        low, high = (ids & 127).astype(F32), ids >> 7
        number = ids.astype(F32)
        weighted = weight * shift
        second = weighted * shift
        third = weight * resid
        fourth = weighted * resid
        tiles, hots = [], []
        for u in range(8):
            mask = spread(high, u) == quarter

            def pick(top, bottom):
                return jnp.where(mask, jnp.where(upper, spread(top, u), spread(bottom, u)), 0.0)

            last = jnp.where(mask & upper, spread(fourth, u), 0.0)
            tiles.append(jnp.concatenate([pick(weight, weighted), pick(second, third), last], axis=0))
            hots.append(hot_lanes(low[u : u + 1, :], 128))
            here = pl.ds(pl.multiple_of(1024 * i + 128 * u, 128), 128)
            table[4:8, here] = jnp.concatenate(
                [knot[u : u + 1], phase[u : u + 1], weight[u : u + 1], resid[u : u + 1]], axis=0
            )
            more[0:2, here] = jnp.concatenate([shift[u : u + 1], number[u : u + 1]], axis=0)
        lanes = pl.ds(pl.multiple_of(1024 * i, 1024), 1024)
        table[0:4, lanes] = partial_ref[:, lanes]
        return total + outer(split_two(jnp.concatenate(tiles, axis=1)), jnp.concatenate(hots, axis=1))

    total = lax.fori_loop(0, 8, step, jnp.zeros((48, 128), F32))
    total = total[:24] + total[24:]
    begin = jnp.int32(0)
    dead = jnp.where(sub == 4, -1.0, 0.0)
    for block in range(N_TM):
        count = counts_ref[0, block]
        base = pl.multiple_of((begin >> 7) << 7, 128)
        off = begin & 127
        back = (128 - off) & 127
        early = lane < 128 - off
        rolled = pltpu.roll(table[:, pl.ds(base, 128)], back, 1)
        rolled_more = pltpu.roll(more[:, pl.ds(base, 128)], back, 1)
        for j in range(CAP // 128):
            here = pl.ds(base + 128 * (j + 1), 128)
            after = pltpu.roll(table[:, here], back, 1)
            after_more = pltpu.roll(more[:, here], back, 1)
            live = lane + 128 * j < count
            out_ref[block, :, 128 * j : 128 * (j + 1)] = jnp.where(
                live, jnp.where(early, rolled, after), dead
            )
            tile = jnp.where(live, jnp.where(early, rolled_more, after_more), 0.0)
            row, lanes = j // 4, slice(MORE + 128 * (j % 4), MORE + 128 * (j % 4) + 128)
            out_ref[block, row : row + 1, lanes] = tile[0:1]
            out_ref[block, 4 + row : 5 + row, lanes] = tile[1:2]
            rolled, rolled_more = after, after_more
        for k in range(3):
            out_ref[block, :, SUMS + 128 * k : SUMS + 128 * (k + 1)] = total[8 * k : 8 * k + 8]
        begin = begin + count


def count_live(windows_ref, counts):
    for block in range(N_TM):
        counts[block] = jnp.sum((windows_ref[block, 4:5, :CAP] >= 0.0).astype(jnp.int32))


def each_chunk(counts, body):
    def block_step(block, carry):
        def step(i, inner):
            body(block, i)
            return inner

        return lax.fori_loop(0, (counts[block] + CHUNK - 1) // CHUNK, step, carry)

    lax.fori_loop(0, N_TM, block_step, 0)


def spline_basis(phase):
    square = phase * phase
    cube = square * phase
    remain = 1.0 - phase
    return [
        remain * remain * remain * (1.0 / 6.0),
        (3.0 * cube - 6.0 * square + 4.0) * (1.0 / 6.0),
        (-3.0 * cube + 3.0 * square + 3.0 * phase + 1.0) * (1.0 / 6.0),
        cube * (1.0 / 6.0),
    ]


def moment_kernel(windows_ref, select_ref, out_ref, total, tiles, counts):
    total[...] = jnp.zeros_like(total)
    count_live(windows_ref, counts)

    def body(block, i):
        tile = windows_ref[block, :, pl.ds(pl.multiple_of(i * CHUNK, CHUNK), CHUNK)]
        part = [tile[c : c + 1] for c in range(4)]
        knot, phase, weight = tile[4:5], tile[5:6], tile[6:7]
        remain = 1.0 - phase
        powers, others = [jnp.ones_like(phase), phase], [jnp.ones_like(phase), remain]
        for n in range(2, 7):
            powers.append(powers[n // 2] * powers[n - n // 2])
            others.append(others[n // 2] * others[n - n // 2])
        order = [weight * (BINOMIAL[n] * (powers[n] * others[6 - n])) for n in range(7)]
        left = jnp.concatenate([part[c] for c, e in PAIRS[:8]], axis=0)
        right = jnp.concatenate([part[e] for c, e in PAIRS[:8]], axis=0)
        eight = left * right
        rows = [order[n] * eight for n in range(7)]
        stack = jnp.concatenate(order + [jnp.zeros_like(phase)], axis=0)
        rows.append(stack * (part[2] * part[3]))
        rows.append(stack * (part[3] * part[3]))
        rows = split_two(jnp.concatenate(rows, axis=0))
        group = jnp.floor(knot * (1.0 / 256.0))
        low = jnp.maximum(knot, 0.0) - 256.0 * jnp.maximum(group, 0.0)
        total[...] += outer(grouped(rows, group, 4), hot_lanes(low, 256))

    each_chunk(counts, body)
    parts = [
        jnp.dot(
            select_ref[...], total[2 * MOMENTS * g : 2 * MOMENTS * (g + 1)], precision=HIGHEST, preferred_element_type=F32
        )
        for g in range(4)
    ]
    parts.append(jnp.zeros((160, 128), F32))
    orders = jnp.concatenate(parts, axis=1)
    band = orders[0:40]
    for a in range(1, 4):
        band = band + pltpu.roll(orders[40 * a : 40 * a + 40], a, 1)
    for q in range(8):
        tiles[0:40, q, :] = band[:, 128 * q : 128 * (q + 1)]
    spill = band[:, K : K + 128]
    packed = spill[0:8]
    for g in range(1, 5):
        packed = packed + pltpu.roll(spill[8 * g : 8 * g + 8], 8 * g, 1)
    tiles[SPILL] = packed
    sums = windows_ref[0, :, SUMS:WIDTH]
    for block in range(1, N_TM):
        sums = sums + windows_ref[block, :, SUMS:WIDTH]
    for s in range(N_SRC):
        for r in range(3):
            at = 3 * s + r
            out_ref[s, 8 * r : 8 * r + 8, :] = tiles[at] if at <= SPILL else jnp.zeros((8, 128), F32)
            out_ref[s, 24 + 8 * r : 32 + 8 * r, :] = sums[:, 128 * r : 128 * (r + 1)]


def side_kernel(windows_ref, parts_ref, out_ref, step_ref, total, counts):
    total[...] = jnp.zeros_like(total)
    count_live(windows_ref, counts)
    both = parts_ref[0]
    for s in range(1, N_SRC):
        both = both + parts_ref[s]
    prior = float(OBS_DEV * N_SRC * N_TM // NCAL)
    totals = both[24:48]
    zero_moment = totals[0:4] + prior
    first = totals[4:8]
    second_moment = totals[8:12] + prior
    third, fourth = totals[12:16], totals[16:20]
    det = zero_moment * second_moment - first * first
    offset = (second_moment * third - first * fourth) / det
    slope = (zero_moment * fourth - first * third) / det
    for h in range(4):
        step_ref[0:1, 128 * h : 128 * (h + 1)] = offset[h : h + 1]
        step_ref[1:2, 128 * h : 128 * (h + 1)] = slope[h : h + 1]
    pieces = split_three(jnp.concatenate([offset, slope], axis=0))
    sub = lax.broadcasted_iota(jnp.int32, (8, CHUNK), 0)
    quarter = (sub & 3).astype(F32)
    upper = sub < 4

    def body(block, i):
        tile = windows_ref[block, :, pl.ds(pl.multiple_of(i * CHUNK, CHUNK), CHUNK)]
        shift = windows_ref[block, pl.ds(i, 1), MORE:SUMS]
        ids = windows_ref[block, pl.ds(4 + i, 1), MORE:SUMS]
        knot, phase, weight, resid = tile[4:5], tile[5:6], tile[6:7], tile[7:8]
        high = jnp.floor(ids * (1.0 / 128.0))
        found = jnp.dot(pieces, hot_lanes(ids - 128.0 * high, 128), preferred_element_type=F32)
        found = found[0:8] + found[8:16] + found[16:24]
        found = jnp.where(quarter == high, found, 0.0) * jnp.where(upper, 1.0, shift)
        corrected = resid - jnp.sum(found, axis=0, keepdims=True)
        basis = spline_basis(phase)
        four = tile[0:4] * (weight * corrected)
        double = jnp.concatenate([four, four], axis=0)
        rows = []
        for a in (0, 2):
            order = jnp.concatenate([basis[a]] * 4 + [basis[a + 1]] * 4, axis=0)
            rows.append(double * order)
        rows = split_two(jnp.concatenate(rows, axis=0))
        group = jnp.floor(knot * (1.0 / 128.0))
        low = jnp.maximum(knot, 0.0) - 128.0 * jnp.maximum(group, 0.0)
        total[...] += outer(grouped(rows, group, 8), hot_lanes(low, 128))

    each_chunk(counts, body)
    orders = [total[32 * g : 32 * g + 16] + total[32 * g + 16 : 32 * g + 32] for g in range(8)]
    orders = jnp.concatenate(orders + [jnp.zeros((16, 128), F32)], axis=1)
    side = orders[0:4]
    for a in range(1, 4):
        side = side + pltpu.roll(orders, a, 1)[4 * a : 4 * a + 4]
    share = both[0:24]
    spill = jnp.concatenate([side[:, K : K + 128], jnp.zeros((4, 128), F32)], axis=0)
    rows = [share]
    for c in range(4):
        rows += [side[c : c + 1, 128 * q : 128 * (q + 1)] for q in range(8)]
    rows = jnp.concatenate(rows + [spill], axis=0)
    for s in range(N_SRC):
        out_ref[s] = rows


def gather_kernel(parts_ref, out_ref):
    side = parts_ref[0, 24:64, :]
    for s in range(1, N_SRC):
        side = side + parts_ref[s, 24:64, :]
    spill = pltpu.roll(side[32:40], SPILL, 1) + parts_ref[SPILL // 3, 8 * (SPILL % 3) : 8 * (SPILL % 3) + 8, :]
    for copy in range(4):
        for i in range(40):
            out_ref[copy, 8 * i : 8 * i + 8, :] = parts_ref[i // 3, 8 * (i % 3) : 8 * (i % 3) + 8, :]
        out_ref[copy, 8 * SPILL : 8 * SPILL + 8, :] = spill
        out_ref[copy, 8 * SIDE : 8 * TILES, :] = side[0:32]


def solve_kernel(
    place_ref, mine_ref, other_ref, coeffs_ref, within_ref, across_ref, out_ref,
    band, inverse, field, ahead, lower, applied, resid, delta, filtered,
):
    lane8 = lax.broadcasted_iota(jnp.int32, (8, 128), 1)
    lane = lax.broadcasted_iota(jnp.int32, (64, 128), 1)
    core = place_ref[0] & 1
    halves = ((mine_ref, core), (other_ref, 1 - core))
    for ref, parity in halves:
        for z in range(N_TM // 2):
            rows = pl.ds(pl.multiple_of(8 * (2 * z + parity), 8), 8)
            for i in range(44):
                at = i if i < 40 else SIDE + i - 40
                band[i, rows, :] = ref[z, 8 * at : 8 * at + 8, :]
    for ref, parity in halves:
        for z in range(N_TM // 2):
            row = pl.ds(pl.multiple_of(8 * (2 * z + parity) + 8, 8), 1)
            packed = ref[z, 8 * SPILL : 8 * SPILL + 8, :]
            for g in range(6):
                moved = packed if g == 0 else pltpu.roll(packed, 128 - 8 * g, 1)
                moved = jnp.where(lane8 < 3, moved, 0.0)
                for u in range(min(8, 44 - 8 * g)):
                    band[8 * g + u, row, :] += moved[u : u + 1]
    for c in range(4):
        inverse[c] = 1.0 / (ATTITUDE_PRIOR + band[PAIR_AT[(c, c)], 0:64, :])
    field[...] = jnp.zeros_like(field)
    lower[...] = jnp.zeros_like(lower)

    def total_of(left, right):
        value = left * right
        value = jnp.sum(value.reshape(32, 8, 128), axis=0)
        return jnp.sum(jnp.sum(value, axis=0, keepdims=True), axis=1, keepdims=True)

    def precondition():
        res = resid[...].reshape(256, 128)
        spreads = jnp.dot(res, within_ref[...], precision=HIGHEST, preferred_element_type=F32)
        for c in range(4):
            own = spreads[64 * c : 64 * c + 64]
            carried = jnp.concatenate([own[:, 128:256], own[:, 256:384], own[:, 384:512]], axis=0)
            carry = jnp.dot(across_ref[...], carried, precision=HIGHEST, preferred_element_type=F32)
            filtered[c] = resid[c] * inverse[c] + own[:, :128] + carry

    def apply_normals():
        for e in range(4):
            here, after = field[e, 8:72, :], field[e, 9:73, :]
            for d in range(1, 4):
                ahead[d - 1, e] = pltpu.roll(jnp.where(lane < d, after, here), 128 - d, 1)
        for t in range(N_TM):
            rows = slice(8 * t, 8 * t + 8)
            padded = slice(8 * t + 8, 8 * t + 16)
            own = [field[e, padded, :] for e in range(4)]
            sums = [own[c] * ATTITUDE_PRIOR for c in range(4)]
            for d in range(4):
                near = own if d == 0 else [ahead[d - 1, e, rows, :] for e in range(4)]
                tiles = [band[10 * d + i, rows, :] for i in range(10)]
                for c in range(4):
                    for e in range(4):
                        sums[c] = sums[c] + tiles[PAIR_AT[(c, e)]] * near[e]
                if d:
                    for c in range(4):
                        back = tiles[PAIR_AT[(c, 0)]] * own[0]
                        for e in range(1, 4):
                            back = back + tiles[PAIR_AT[(c, e)]] * own[e]
                        lower[d - 1, c, padded, :] = back
            for c in range(4):
                applied[c, rows, :] = sums[c]
        for c in range(4):
            result = applied[c]
            for d in range(1, 4):
                here, before = lower[d - 1, c, 8:72, :], lower[d - 1, c, 7:71, :]
                result = result + pltpu.roll(jnp.where(lane >= 128 - d, before, here), d, 1)
            applied[c] = result

    resid[...] = band[40:44, 0:64, :]
    precondition()
    field[:, 8:72, :] = filtered[...]
    delta[...] = jnp.zeros_like(delta)
    energy = total_of(resid[...], filtered[...])

    def iterate(i, energy):
        apply_normals()
        step = energy / total_of(field[:, 8:72, :], applied[...])
        delta[...] += step * field[:, 8:72, :]
        resid[...] -= step * applied[...]
        precondition()
        fresh = total_of(resid[...], filtered[...])
        field[:, 8:72, :] = filtered[...] + (fresh / energy) * field[:, 8:72, :]
        return fresh

    energy = lax.fori_loop(0, ITERS - 1, iterate, energy)
    apply_normals()
    step = energy / total_of(field[:, 8:72, :], applied[...])
    delta[...] += step * field[:, 8:72, :]
    mine = pl.ds(pl.multiple_of(place_ref[0] * 8, 8), 8)
    for c in range(4):
        tile = delta[c, mine, :]
        for q in range(8):
            lanes = slice(128 * q, 128 * q + 128)
            out_ref[c : c + 1, lanes] = coeffs_ref[c : c + 1, lanes] + tile[q : q + 1]


VMEM_SPEC = pl.BlockSpec(memory_space=pltpu.VMEM)
SMEM_SPEC = pl.BlockSpec(memory_space=pltpu.SMEM)
HBM_SPEC = pl.BlockSpec(memory_space=pltpu.HBM)
PARAMS = pltpu.CompilerParams(vmem_limit_bytes=VMEM_LIMIT)
SAME_CORE = [[0, 2, 4, 6], [1, 3, 5, 7]]


def local(
    knot_index, block_counts, knot_phase, partials, obs_weight, residuals, cal_id, across, coeffs
):
    dense = [
        value.reshape(64, 128)
        for value in (cal_id, obs_weight, across, residuals, knot_index, knot_phase)
    ]
    with jax.named_scope("windows"):
        windows = pl.pallas_call(
            window_kernel,
            out_shape=jax.ShapeDtypeStruct((N_TM, 8, WIDTH), F32),
            in_specs=[SMEM_SPEC] + [HBM_SPEC] * 7,
            out_specs=VMEM_SPEC,
            scratch_shapes=[pltpu.VMEM((64, 128), value.dtype) for value in dense]
            + [
                pltpu.VMEM((4, OBS_DEV), F32),
                pltpu.VMEM((8, OBS_DEV + CAP + 128), F32),
                pltpu.VMEM((8, OBS_DEV + CAP + 128), F32),
                pltpu.SemaphoreType.DMA((7,)),
            ],
            compiler_params=pltpu.CompilerParams(vmem_limit_bytes=56 * 1024 * 1024),
        )(block_counts, *dense, partials)
    with jax.named_scope("to_owners"):
        windows = lax.all_to_all(windows, "tm", 0, 0)
    with jax.named_scope("moments"):
        parts = pl.pallas_call(
            moment_kernel,
            out_shape=jax.ShapeDtypeStruct((N_SRC, 48, 128), F32),
            in_specs=[VMEM_SPEC] * 2,
            out_specs=VMEM_SPEC,
            scratch_shapes=[
                pltpu.VMEM((8 * MOMENTS, 256), F32),
                pltpu.VMEM((SPILL + 1, 8, 128), F32),
                pltpu.SMEM((N_TM,), jnp.int32),
            ],
            compiler_params=PARAMS,
        )(windows, jnp.asarray(select_rows()))
    with jax.named_scope("band_reduce"):
        parts = lax.all_to_all(parts, "src", 0, 0)
    with jax.named_scope("side"):
        parts, calibration_step = pl.pallas_call(
            side_kernel,
            out_shape=(
                jax.ShapeDtypeStruct((N_SRC, 64, 128), F32),
                jax.ShapeDtypeStruct((2, NCAL), F32),
            ),
            in_specs=[VMEM_SPEC] * 2,
            out_specs=(VMEM_SPEC, VMEM_SPEC),
            scratch_shapes=[pltpu.VMEM((256, 128), F32), pltpu.SMEM((N_TM,), jnp.int32)],
            compiler_params=PARAMS,
        )(windows, parts)
    with jax.named_scope("gather_src"):
        parts = lax.all_to_all(parts, "src", 0, 0)
    with jax.named_scope("gather"):
        parts = pl.pallas_call(
            gather_kernel,
            out_shape=jax.ShapeDtypeStruct((4, 8 * TILES, 128), F32),
            in_specs=[VMEM_SPEC],
            out_specs=VMEM_SPEC,
            compiler_params=PARAMS,
        )(parts)
    with jax.named_scope("gather_z"):
        mine = lax.all_to_all(parts, "tm", 0, 0, axis_index_groups=SAME_CORE)
    with jax.named_scope("gather_core"):
        other = lax.ppermute(mine, "tm", [(i, i ^ 1) for i in range(N_TM)])
    within, across_rows = filter_tables()
    with jax.named_scope("solve"):
        new_coeffs = pl.pallas_call(
            solve_kernel,
            out_shape=jax.ShapeDtypeStruct((4, K), F32),
            in_specs=[SMEM_SPEC] + [VMEM_SPEC] * 5,
            out_specs=VMEM_SPEC,
            scratch_shapes=[
                pltpu.VMEM((44, 72, 128), F32),
                pltpu.VMEM((4, 64, 128), F32),
                pltpu.VMEM((4, 80, 128), F32),
                pltpu.VMEM((3, 4, 64, 128), F32),
                pltpu.VMEM((3, 4, 80, 128), F32),
                pltpu.VMEM((4, 64, 128), F32),
                pltpu.VMEM((4, 64, 128), F32),
                pltpu.VMEM((4, 64, 128), F32),
                pltpu.VMEM((4, 64, 128), F32),
            ],
            compiler_params=PARAMS,
        )(
            lax.axis_index("tm").reshape(1), mine, other, coeffs, jnp.asarray(within),
            jnp.asarray(across_rows),
        )
    return (new_coeffs, calibration_step)


def solution(mesh):
    placed = (
        P(("src", "tm")),
        P(("src", "tm"), None),
        P(("src", "tm")),
        P(None, ("src", "tm")),
        P(("src", "tm")),
        P(("src", "tm")),
        P(("src", "tm")),
        P(("src", "tm")),
        P(None, "tm"),
    )
    return jax.shard_map(
        local, mesh=mesh, in_specs=placed, out_specs=(P(None, "tm"), P()), check_vma=False
    )
```

```python
import jax
import jax.numpy as jnp
import ml_dtypes
import numpy as np
from jax import lax
from jax.experimental import pallas as pl
from jax.experimental.pallas import tpu as pltpu
from jax.sharding import PartitionSpec as P

K = 1024
OBS_DEV = 8192
NCAL = 512
ITERS = 6
N_SRC = 16
N_TM = 8
NK = K * N_TM
CAP = 2 * OBS_DEV // N_TM
ATTITUDE_PRIOR = 1.0
FILTER_GAIN = 0.05
CHUNK = 512
BATCH = 4
UNROLL = 8
HIGHEST = lax.Precision.HIGHEST
F32 = jnp.float32
BF16 = jnp.bfloat16
VMEM_LIMIT = 48 * 1024 * 1024

PAIRS = [(a, b) for a in range(4) for b in range(a, 4)]
PAIR_AT = {pair: i for i, pair in enumerate(PAIRS)}
PAIR_AT.update({(b, a): i for (a, b), i in list(PAIR_AT.items())})
SPILL, SIDE, TILES = 40, 41, 45
MORE, SUMS, WIDTH = CAP, CAP + CHUNK, CAP + CHUNK + 384
MOMENTS = 72
BINOMIAL = [1.0, 6.0, 15.0, 20.0, 15.0, 6.0, 1.0]


def select_rows():
    cubic = np.array([[1, 0, 0, 0], [4, 4, 2, 1], [1, 2, 4, 4], [0, 0, 0, 1]]) / 6.0
    scaled = cubic * np.array([1.0, 3.0, 3.0, 1.0])
    table = np.zeros((4, 40, 2 * MOMENTS))
    for a in range(4):
        for lag in range(4 - a):
            share = np.convolve(scaled[a], scaled[a + lag]) / np.array(BINOMIAL)
            for pair in range(10):
                for n in range(7):
                    row = 8 * n + pair if pair < 8 else 56 + 8 * (pair - 8) + n
                    table[a, 10 * lag + pair, row] = share[n]
                    table[a, 10 * lag + pair, MOMENTS + row] = share[n]
    return table.reshape(160, 2 * MOMENTS).astype(np.float32)


def filter_tables():
    rate = 0.1 ** (1.0 / NK)
    gain = FILTER_GAIN * (1.0 - rate) ** 2 / (1.0 - rate * rate)
    lane = np.arange(128.0)
    row = np.arange(64.0)
    near = rate ** np.abs(lane[:, None] - lane[None, :])
    from_left = np.outer(rate ** (127 - lane), rate ** (lane + 1))
    from_right = np.outer(rate**lane, rate ** (128 - lane))
    edge = np.outer(rate ** (127 - lane), rate ** (128 - lane))
    within = gain * np.concatenate([near, from_left, from_right, edge], axis=1)
    gap = row[:, None] - row[None, :]
    left = np.where(gap > 0, rate ** (128 * np.maximum(gap - 1, 0)), 0.0)
    right = np.where(gap < 0, rate ** (128 * np.maximum(-gap - 1, 0)), 0.0)
    closing = -np.outer(rate ** (NK - 128 * row - 128), rate ** (NK - 128 * row - 127))
    across = np.concatenate([left, right, closing], axis=1)
    def halves(table):
        high = table.astype(ml_dtypes.bfloat16)
        return high, (table - high.astype(np.float64)).astype(ml_dtypes.bfloat16)

    (near_high, near_low), (far_high, far_low) = halves(within), halves(across)
    return (
        np.concatenate([near_high, near_high, near_low], axis=0),
        np.concatenate([far_high, far_high, far_low], axis=1),
    )


def split_two(value):
    high = value.astype(BF16).astype(F32)
    return jnp.concatenate([high, value - high], axis=0).astype(BF16)


def split_three(value):
    high = value.astype(BF16).astype(F32)
    rest = value - high
    middle = rest.astype(BF16).astype(F32)
    return jnp.concatenate([high, middle, rest - middle, jnp.zeros_like(value)], axis=0).astype(BF16)


def spread(value, u, rows=8):
    return jnp.broadcast_to(value[u : u + 1, :], (rows, value.shape[1]))


def sixteen(row):
    return jnp.broadcast_to(row, (16, row.shape[1])).astype(BF16)


def hot_lanes(low, count):
    low = sixteen(low)
    want = lax.broadcasted_iota(jnp.int32, low.shape, 0).astype(F32).astype(BF16)
    one, zero = jnp.ones_like(low), jnp.zeros_like(low)
    return jnp.concatenate(
        [jnp.where(low == want + BF16(16 * j), one, zero) for j in range(count // 16)], axis=0
    )


def grouped(rows, group, count):
    parts = []
    for g in range(count):
        mask = sixteen(jnp.where(group == float(g), 1.0, 0.0))
        parts.append(rows * jnp.concatenate([mask] * (rows.shape[0] // 16), axis=0))
    return jnp.concatenate(parts, axis=0)


def outer(rows, hot):
    return lax.dot_general(rows, hot, (((1,), (1,)), ((), ())), preferred_element_type=F32)


def window_kernel(
    counts_ref, cal_hbm, weight_hbm, across_hbm, resid_hbm, knot_hbm, phase_hbm, partial_hbm,
    out_hbm, cal_ref, weight_ref, across_ref, resid_ref, knot_ref, phase_ref, partial_ref,
    table, more, window, sems, out_sems,
):
    pairs = [
        (cal_hbm, cal_ref), (weight_hbm, weight_ref), (across_hbm, across_ref), (resid_hbm, resid_ref),
        (knot_hbm, knot_ref), (phase_hbm, phase_ref), (partial_hbm, partial_ref),
    ]
    copies = [pltpu.make_async_copy(a, b, sems.at[i]) for i, (a, b) in enumerate(pairs)]
    for copy in copies:
        copy.start()
    sub = lax.broadcasted_iota(jnp.int32, (8, 128), 0)
    lane = lax.broadcasted_iota(jnp.int32, (8, 128), 1)
    quarter = sub & 3
    upper = sub < 4
    for copy in copies[:4]:
        copy.wait()

    def step(i, total):
        tiles, hots = [], []
        for part in range(UNROLL):
            rows = pl.ds(pl.multiple_of(8 * UNROLL * i + 8 * part, 8), 8)
            ids, weight = cal_ref[rows, :], weight_ref[rows, :]
            shift, resid = across_ref[rows, :], resid_ref[rows, :]
            low, high = (ids & 127).astype(F32), ids >> 7
            weighted = weight * shift
            second = weighted * shift
            third = weight * resid
            fourth = weighted * resid
            for u in range(8):
                mask = spread(high, u) == quarter

                def pick(top, bottom):
                    return jnp.where(mask, jnp.where(upper, spread(top, u), spread(bottom, u)), 0.0)

                last = jnp.where(mask & upper, spread(fourth, u), 0.0)
                tiles.append(jnp.concatenate([pick(weight, weighted), pick(second, third), last], axis=0))
                hots.append(hot_lanes(low[u : u + 1, :], 128))
        return total + outer(split_two(jnp.concatenate(tiles, axis=1)), jnp.concatenate(hots, axis=1))

    total = lax.fori_loop(0, 8 // UNROLL, step, jnp.zeros((48, 128), F32))
    total = total[:24] + total[24:]
    for copy in copies[4:]:
        copy.wait()

    def fill(i, carry):
        rows = pl.ds(pl.multiple_of(8 * i, 8), 8)
        knot, phase = knot_ref[rows, :].astype(F32), phase_ref[rows, :]
        weight, resid = weight_ref[rows, :], resid_ref[rows, :]
        shift, number = across_ref[rows, :], cal_ref[rows, :].astype(F32)
        for u in range(8):
            here = pl.ds(pl.multiple_of(1024 * i + 128 * u, 128), 128)
            table[4:8, here] = jnp.concatenate(
                [knot[u : u + 1], phase[u : u + 1], weight[u : u + 1], resid[u : u + 1]], axis=0
            )
            more[0:2, here] = jnp.concatenate([shift[u : u + 1], number[u : u + 1]], axis=0)
        lanes = pl.ds(pl.multiple_of(1024 * i, 1024), 1024)
        table[0:4, lanes] = partial_ref[:, lanes]
        return carry

    lax.fori_loop(0, 8, fill, 0)
    begin = jnp.int32(0)
    dead = jnp.where(sub == 4, -1.0, 0.0)
    sent = []
    for block in range(N_TM):
        count = counts_ref[0, block]
        base = pl.multiple_of((begin >> 7) << 7, 128)
        off = begin & 127
        back = (128 - off) & 127
        early = lane < 128 - off
        rolled = pltpu.roll(table[:, pl.ds(base, 128)], back, 1)
        rolled_more = pltpu.roll(more[:, pl.ds(base, 128)], back, 1)
        for j in range(CAP // 128):
            here = pl.ds(base + 128 * (j + 1), 128)
            after = pltpu.roll(table[:, here], back, 1)
            after_more = pltpu.roll(more[:, here], back, 1)
            live = lane + 128 * j < count
            window[block, :, 128 * j : 128 * (j + 1)] = jnp.where(
                live, jnp.where(early, rolled, after), dead
            )
            tile = jnp.where(live, jnp.where(early, rolled_more, after_more), 0.0)
            row, lanes = j // 4, slice(MORE + 128 * (j % 4), MORE + 128 * (j % 4) + 128)
            window[block, row : row + 1, lanes] = tile[0:1]
            window[block, 4 + row : 5 + row, lanes] = tile[1:2]
            rolled, rolled_more = after, after_more
        for k in range(3):
            window[block, :, SUMS + 128 * k : SUMS + 128 * (k + 1)] = total[8 * k : 8 * k + 8]
        sent.append(pltpu.make_async_copy(window.at[block], out_hbm.at[block], out_sems.at[block]))
        sent[-1].start()
        begin = begin + count
    for copy in sent:
        copy.wait()


def each_batch(windows_ref, order, body):
    found = jnp.int32(0)
    for block in range(N_TM):
        count = jnp.sum((windows_ref[block, 4:5, :CAP] >= 0.0).astype(jnp.int32))
        for i in range(CAP // CHUNK):
            order[found] = 4 * block + i
            found = found + (count > i * CHUNK).astype(jnp.int32)
    for u in range(BATCH - 1):
        order[found + u] = 0

    def step(batch, carry):
        chunks = []
        for u in range(BATCH):
            at = order[BATCH * batch + u]
            block, i = at >> 2, at & 3
            tile = windows_ref[block, :, pl.ds(pl.multiple_of(i * CHUNK, CHUNK), CHUNK)]
            knot = jnp.where(BATCH * batch + u < found, tile[4:5], -1.0)
            chunks.append((tile, knot, block, i))
        body(chunks)
        return carry

    lax.fori_loop(0, (found + BATCH - 1) // BATCH, step, 0)


def spline_basis(phase):
    square = phase * phase
    cube = square * phase
    remain = 1.0 - phase
    return [
        remain * remain * remain * (1.0 / 6.0),
        (3.0 * cube - 6.0 * square + 4.0) * (1.0 / 6.0),
        (-3.0 * cube + 3.0 * square + 3.0 * phase + 1.0) * (1.0 / 6.0),
        cube * (1.0 / 6.0),
    ]


def moment_kernel(windows_ref, select_ref, out_ref, total, tiles, order):
    total[...] = jnp.zeros_like(total)

    def work(tile, knot):
        part = [tile[c : c + 1] for c in range(4)]
        phase, weight = tile[5:6], tile[6:7]
        remain = 1.0 - phase
        powers, others = [jnp.ones_like(phase), phase], [jnp.ones_like(phase), remain]
        for n in range(2, 7):
            powers.append(powers[n // 2] * powers[n - n // 2])
            others.append(others[n // 2] * others[n - n // 2])
        order = [weight * (BINOMIAL[n] * (powers[n] * others[6 - n])) for n in range(7)]
        left = jnp.concatenate([part[c] for c, e in PAIRS[:8]], axis=0)
        right = jnp.concatenate([part[e] for c, e in PAIRS[:8]], axis=0)
        eight = left * right
        rows = [order[n] * eight for n in range(7)]
        stack = jnp.concatenate(order + [jnp.zeros_like(phase)], axis=0)
        rows.append(stack * (part[2] * part[3]))
        rows.append(stack * (part[3] * part[3]))
        rows = split_two(jnp.concatenate(rows, axis=0))
        group = jnp.floor(knot * (1.0 / 256.0))
        low = jnp.maximum(knot, 0.0) - 256.0 * jnp.maximum(group, 0.0)
        return grouped(rows, group, 4), hot_lanes(low, 256)

    def body(chunks):
        rows, hots = zip(*[work(tile, knot) for tile, knot, block, i in chunks])
        total[...] += outer(jnp.concatenate(rows, axis=1), jnp.concatenate(hots, axis=1))

    each_batch(windows_ref, order, body)
    parts = [
        jnp.dot(
            select_ref[...], total[2 * MOMENTS * g : 2 * MOMENTS * (g + 1)], precision=HIGHEST, preferred_element_type=F32
        )
        for g in range(4)
    ]
    parts.append(jnp.zeros((160, 128), F32))
    orders = jnp.concatenate(parts, axis=1)
    band = orders[0:40]
    for a in range(1, 4):
        band = band + pltpu.roll(orders[40 * a : 40 * a + 40], a, 1)
    for q in range(8):
        tiles[0:40, q, :] = band[:, 128 * q : 128 * (q + 1)]
    spill = band[:, K : K + 128]
    packed = spill[0:8]
    for g in range(1, 5):
        packed = packed + pltpu.roll(spill[8 * g : 8 * g + 8], 8 * g, 1)
    tiles[SPILL] = packed
    sums = windows_ref[0, :, SUMS:WIDTH]
    for block in range(1, N_TM):
        sums = sums + windows_ref[block, :, SUMS:WIDTH]
    for s in range(N_SRC):
        for r in range(3):
            at = 3 * s + r
            out_ref[s, 8 * r : 8 * r + 8, :] = tiles[at] if at <= SPILL else jnp.zeros((8, 128), F32)
            out_ref[s, 24 + 8 * r : 32 + 8 * r, :] = sums[:, 128 * r : 128 * (r + 1)]


def side_kernel(windows_ref, parts_ref, out_ref, step_ref, total, order):
    total[...] = jnp.zeros_like(total)
    both = parts_ref[0]
    for s in range(1, N_SRC):
        both = both + parts_ref[s]
    prior = float(OBS_DEV * N_SRC * N_TM // NCAL)
    totals = both[24:48]
    zero_moment = totals[0:4] + prior
    first = totals[4:8]
    second_moment = totals[8:12] + prior
    third, fourth = totals[12:16], totals[16:20]
    det = zero_moment * second_moment - first * first
    offset = (second_moment * third - first * fourth) / det
    slope = (zero_moment * fourth - first * third) / det
    for h in range(4):
        step_ref[0:1, 128 * h : 128 * (h + 1)] = offset[h : h + 1]
        step_ref[1:2, 128 * h : 128 * (h + 1)] = slope[h : h + 1]
    pieces = split_three(jnp.concatenate([offset, slope], axis=0))
    sub = lax.broadcasted_iota(jnp.int32, (8, CHUNK), 0)
    quarter = (sub & 3).astype(F32)
    upper = sub < 4

    def work(tile, knot, block, i):
        shift = windows_ref[block, pl.ds(i, 1), MORE:SUMS]
        ids = windows_ref[block, pl.ds(4 + i, 1), MORE:SUMS]
        phase, weight, resid = tile[5:6], tile[6:7], tile[7:8]
        high = jnp.floor(ids * (1.0 / 128.0))
        found = jnp.dot(pieces, hot_lanes(ids - 128.0 * high, 128), preferred_element_type=F32)
        found = found[0:8] + found[8:16] + found[16:24]
        found = jnp.where(quarter == high, found, 0.0) * jnp.where(upper, 1.0, shift)
        corrected = resid - jnp.sum(found, axis=0, keepdims=True)
        basis = spline_basis(phase)
        four = tile[0:4] * (weight * corrected)
        double = jnp.concatenate([four, four], axis=0)
        rows = []
        for a in (0, 2):
            order = jnp.concatenate([basis[a]] * 4 + [basis[a + 1]] * 4, axis=0)
            rows.append(double * order)
        rows = split_two(jnp.concatenate(rows, axis=0))
        group = jnp.floor(knot * (1.0 / 128.0))
        low = jnp.maximum(knot, 0.0) - 128.0 * jnp.maximum(group, 0.0)
        return grouped(rows, group, 8), hot_lanes(low, 128)

    def body(chunks):
        rows, hots = zip(*[work(*chunk) for chunk in chunks])
        total[...] += outer(jnp.concatenate(rows, axis=1), jnp.concatenate(hots, axis=1))

    each_batch(windows_ref, order, body)
    orders = [total[32 * g : 32 * g + 16] + total[32 * g + 16 : 32 * g + 32] for g in range(8)]
    orders = jnp.concatenate(orders + [jnp.zeros((16, 128), F32)], axis=1)
    side = orders[0:4]
    for a in range(1, 4):
        side = side + pltpu.roll(orders, a, 1)[4 * a : 4 * a + 4]
    share = both[0:24]
    spill = jnp.concatenate([side[:, K : K + 128], jnp.zeros((4, 128), F32)], axis=0)
    rows = [share]
    for c in range(4):
        rows += [side[c : c + 1, 128 * q : 128 * (q + 1)] for q in range(8)]
    rows = jnp.concatenate(rows + [spill], axis=0)
    for s in range(N_SRC):
        out_ref[s] = rows


def gather_kernel(parts_ref, out_ref):
    side = parts_ref[0, 24:64, :]
    for s in range(1, N_SRC):
        side = side + parts_ref[s, 24:64, :]
    spill = pltpu.roll(side[32:40], SPILL, 1) + parts_ref[SPILL // 3, 8 * (SPILL % 3) : 8 * (SPILL % 3) + 8, :]
    for copy in range(4):
        for i in range(40):
            out_ref[copy, 8 * i : 8 * i + 8, :] = parts_ref[i // 3, 8 * (i % 3) : 8 * (i % 3) + 8, :]
        out_ref[copy, 8 * SPILL : 8 * SPILL + 8, :] = spill
        out_ref[copy, 8 * SIDE : 8 * TILES, :] = side[0:32]


def solve_kernel(
    place_ref, mine_ref, other_ref, coeffs_ref, within_ref, across_ref, out_ref,
    band, inverse, field, ahead, lower, applied, resid, delta, filtered, smooth,
):
    lane8 = lax.broadcasted_iota(jnp.int32, (8, 128), 1)
    lane = lax.broadcasted_iota(jnp.int32, (64, 128), 1)
    core = place_ref[0] & 1
    halves = ((mine_ref, core), (other_ref, 1 - core))
    for ref, parity in halves:
        for z in range(N_TM // 2):
            rows = pl.ds(pl.multiple_of(8 * (2 * z + parity), 8), 8)
            for i in range(44):
                at = i if i < 40 else SIDE + i - 40
                band[i, rows, :] = ref[z, 8 * at : 8 * at + 8, :]
    for ref, parity in halves:
        for z in range(N_TM // 2):
            row = pl.ds(pl.multiple_of(8 * (2 * z + parity) + 8, 8), 1)
            packed = ref[z, 8 * SPILL : 8 * SPILL + 8, :]
            for g in range(6):
                moved = packed if g == 0 else pltpu.roll(packed, 128 - 8 * g, 1)
                moved = jnp.where(lane8 < 3, moved, 0.0)
                for u in range(min(8, 44 - 8 * g)):
                    band[8 * g + u, row, :] += moved[u : u + 1]
    for c in range(4):
        inverse[c] = 1.0 / (ATTITUDE_PRIOR + band[PAIR_AT[(c, c)], 0:64, :])
    field[...] = jnp.zeros_like(field)
    lower[...] = jnp.zeros_like(lower)

    def total_of(left, right):
        value = left * right
        value = jnp.sum(value.reshape(32, 8, 128), axis=0)
        return jnp.sum(jnp.sum(value, axis=0, keepdims=True), axis=1, keepdims=True)

    def precondition(source):
        res = source[...].reshape(256, 128)
        high = res.astype(BF16)
        low = (res - high.astype(F32)).astype(BF16)
        spreads = jnp.dot(
            jnp.concatenate([high, low, high], axis=1), within_ref[...], preferred_element_type=F32
        )
        for c in range(4):
            own = spreads[64 * c : 64 * c + 64]
            carried = jnp.concatenate([own[:, 128:256], own[:, 256:384], own[:, 384:512]], axis=0)
            high = carried.astype(BF16)
            low = (carried - high.astype(F32)).astype(BF16)
            carry = jnp.dot(
                across_ref[...], jnp.concatenate([high, low, high], axis=0), preferred_element_type=F32
            )
            filtered[c] = source[c] * inverse[c] + own[:, :128] + carry

    def apply_normals():
        for e in range(4):
            here, after = field[e, 8:72, :], field[e, 9:73, :]
            for d in range(1, 4):
                ahead[d - 1, e] = pltpu.roll(jnp.where(lane < d, after, here), 128 - d, 1)
        for t in range(N_TM):
            rows = slice(8 * t, 8 * t + 8)
            padded = slice(8 * t + 8, 8 * t + 16)
            own = [field[e, padded, :] for e in range(4)]
            sums = [own[c] * ATTITUDE_PRIOR for c in range(4)]
            for d in range(4):
                near = own if d == 0 else [ahead[d - 1, e, rows, :] for e in range(4)]
                tiles = [band[10 * d + i, rows, :] for i in range(10)]
                for c in range(4):
                    for e in range(4):
                        sums[c] = sums[c] + tiles[PAIR_AT[(c, e)]] * near[e]
                if d:
                    for c in range(4):
                        back = tiles[PAIR_AT[(c, 0)]] * own[0]
                        for e in range(1, 4):
                            back = back + tiles[PAIR_AT[(c, e)]] * own[e]
                        lower[d - 1, c, padded, :] = back
            for c in range(4):
                applied[c, rows, :] = sums[c]
        for c in range(4):
            result = applied[c]
            for d in range(1, 4):
                here, before = lower[d - 1, c, 8:72, :], lower[d - 1, c, 7:71, :]
                result = result + pltpu.roll(jnp.where(lane >= 128 - d, before, here), d, 1)
            applied[c] = result

    resid[...] = band[40:44, 0:64, :]
    precondition(resid)
    smooth[...] = filtered[...]
    field[:, 8:72, :] = filtered[...]
    delta[...] = jnp.zeros_like(delta)
    energy = total_of(resid[...], smooth[...])

    def iterate(i, energy):
        apply_normals()
        precondition(applied)
        step = energy / total_of(field[:, 8:72, :], applied[...])
        delta[...] += step * field[:, 8:72, :]
        rest = resid[...] - step * applied[...]
        after = smooth[...] - step * filtered[...]
        resid[...] = rest
        smooth[...] = after
        fresh = total_of(rest, after)
        field[:, 8:72, :] = after + (fresh / energy) * field[:, 8:72, :]
        return fresh

    energy = lax.fori_loop(0, ITERS - 1, iterate, energy)
    apply_normals()
    step = energy / total_of(field[:, 8:72, :], applied[...])
    delta[...] += step * field[:, 8:72, :]
    mine = pl.ds(pl.multiple_of(place_ref[0] * 8, 8), 8)
    for c in range(4):
        tile = delta[c, mine, :]
        for q in range(8):
            lanes = slice(128 * q, 128 * q + 128)
            out_ref[c : c + 1, lanes] = coeffs_ref[c : c + 1, lanes] + tile[q : q + 1]


VMEM_SPEC = pl.BlockSpec(memory_space=pltpu.VMEM)
SMEM_SPEC = pl.BlockSpec(memory_space=pltpu.SMEM)
HBM_SPEC = pl.BlockSpec(memory_space=pltpu.HBM)
PARAMS = pltpu.CompilerParams(vmem_limit_bytes=VMEM_LIMIT)
SAME_CORE = [[0, 2, 4, 6], [1, 3, 5, 7]]


def local(
    knot_index, block_counts, knot_phase, partials, obs_weight, residuals, cal_id, across, coeffs
):
    dense = [
        value.reshape(64, 128)
        for value in (cal_id, obs_weight, across, residuals, knot_index, knot_phase)
    ]
    with jax.named_scope("windows"):
        windows = pl.pallas_call(
            window_kernel,
            out_shape=jax.ShapeDtypeStruct((N_TM, 8, WIDTH), F32),
            in_specs=[SMEM_SPEC] + [HBM_SPEC] * 7,
            out_specs=HBM_SPEC,
            scratch_shapes=[pltpu.VMEM((64, 128), value.dtype) for value in dense]
            + [
                pltpu.VMEM((4, OBS_DEV), F32),
                pltpu.VMEM((8, OBS_DEV + CAP + 128), F32),
                pltpu.VMEM((8, OBS_DEV + CAP + 128), F32),
                pltpu.VMEM((N_TM, 8, WIDTH), F32),
                pltpu.SemaphoreType.DMA((7,)),
                pltpu.SemaphoreType.DMA((N_TM,)),
            ],
            compiler_params=pltpu.CompilerParams(vmem_limit_bytes=56 * 1024 * 1024),
        )(block_counts, *dense, partials)
    with jax.named_scope("to_owners"):
        windows = lax.all_to_all(windows, "tm", 0, 0)
    with jax.named_scope("moments"):
        parts = pl.pallas_call(
            moment_kernel,
            out_shape=jax.ShapeDtypeStruct((N_SRC, 48, 128), F32),
            in_specs=[VMEM_SPEC] * 2,
            out_specs=VMEM_SPEC,
            scratch_shapes=[
                pltpu.VMEM((8 * MOMENTS, 256), F32),
                pltpu.VMEM((SPILL + 1, 8, 128), F32),
                pltpu.SMEM((N_TM * CAP // CHUNK + BATCH,), jnp.int32),
            ],
            compiler_params=PARAMS,
        )(windows, jnp.asarray(select_rows()))
    with jax.named_scope("band_reduce"):
        parts = lax.all_to_all(parts, "src", 0, 0)
    with jax.named_scope("side"):
        parts, calibration_step = pl.pallas_call(
            side_kernel,
            out_shape=(
                jax.ShapeDtypeStruct((N_SRC, 64, 128), F32),
                jax.ShapeDtypeStruct((2, NCAL), F32),
            ),
            in_specs=[VMEM_SPEC] * 2,
            out_specs=(VMEM_SPEC, VMEM_SPEC),
            scratch_shapes=[pltpu.VMEM((256, 128), F32), pltpu.SMEM((N_TM * CAP // CHUNK + BATCH,), jnp.int32)],
            compiler_params=PARAMS,
        )(windows, parts)
    with jax.named_scope("gather_src"):
        parts = lax.all_to_all(parts, "src", 0, 0)
    with jax.named_scope("gather"):
        parts = pl.pallas_call(
            gather_kernel,
            out_shape=jax.ShapeDtypeStruct((4, 8 * TILES, 128), F32),
            in_specs=[VMEM_SPEC],
            out_specs=VMEM_SPEC,
            compiler_params=PARAMS,
        )(parts)
    with jax.named_scope("gather_z"):
        mine = lax.all_to_all(parts, "tm", 0, 0, axis_index_groups=SAME_CORE)
    with jax.named_scope("gather_core"):
        other = lax.ppermute(mine, "tm", [(i, i ^ 1) for i in range(N_TM)])
    within, across_rows = filter_tables()
    with jax.named_scope("solve"):
        new_coeffs = pl.pallas_call(
            solve_kernel,
            out_shape=jax.ShapeDtypeStruct((4, K), F32),
            in_specs=[SMEM_SPEC] + [VMEM_SPEC] * 5,
            out_specs=VMEM_SPEC,
            scratch_shapes=[
                pltpu.VMEM((44, 72, 128), F32),
                pltpu.VMEM((4, 64, 128), F32),
                pltpu.VMEM((4, 80, 128), F32),
                pltpu.VMEM((3, 4, 64, 128), F32),
                pltpu.VMEM((3, 4, 80, 128), F32),
                pltpu.VMEM((4, 64, 128), F32),
                pltpu.VMEM((4, 64, 128), F32),
                pltpu.VMEM((4, 64, 128), F32),
                pltpu.VMEM((4, 64, 128), F32),
                pltpu.VMEM((4, 64, 128), F32),
            ],
            compiler_params=PARAMS,
        )(
            lax.axis_index("tm").reshape(1), mine, other, coeffs, jnp.asarray(within),
            jnp.asarray(across_rows),
        )
    return (new_coeffs, calibration_step)


def solution(mesh):
    placed = (
        P(("src", "tm")),
        P(("src", "tm"), None),
        P(("src", "tm")),
        P(None, ("src", "tm")),
        P(("src", "tm")),
        P(("src", "tm")),
        P(("src", "tm")),
        P(("src", "tm")),
        P(None, "tm"),
    )
    return jax.shard_map(
        local, mesh=mesh, in_specs=placed, out_specs=(P(None, "tm"), P()), check_vma=False
    )
```

```python
import jax
import jax.numpy as jnp
import ml_dtypes
import numpy as np
from jax import lax
from jax.experimental import pallas as pl
from jax.experimental.pallas import tpu as pltpu
from jax.sharding import PartitionSpec as P

K = 1024
OBS_DEV = 8192
NCAL = 512
ITERS = 6
N_SRC = 16
N_TM = 8
NK = K * N_TM
CAP = 2 * OBS_DEV // N_TM
ATTITUDE_PRIOR = 1.0
FILTER_GAIN = 0.05
CHUNK = 512
PART, BATCH = 2, 4
UNROLL = 8
HIGHEST = lax.Precision.HIGHEST
F32 = jnp.float32
BF16 = jnp.bfloat16
VMEM_LIMIT = 48 * 1024 * 1024

PAIRS = [(a, b) for a in range(4) for b in range(a, 4)]
PAIR_AT = {pair: i for i, pair in enumerate(PAIRS)}
PAIR_AT.update({(b, a): i for (a, b), i in list(PAIR_AT.items())})
SPILL, SIDE, TILES = 40, 41, 45
MORE, SUMS, WIDTH = CAP, CAP + CHUNK, CAP + CHUNK + 384
MOMENTS = 72
BINOMIAL = [1.0, 6.0, 15.0, 20.0, 15.0, 6.0, 1.0]


def halves(table):
    high = table.astype(ml_dtypes.bfloat16)
    return high, (table - high.astype(np.float64)).astype(ml_dtypes.bfloat16)


def select_rows():
    cubic = np.array([[1, 0, 0, 0], [4, 4, 2, 1], [1, 2, 4, 4], [0, 0, 0, 1]]) / 6.0
    scaled = cubic * np.array([1.0, 3.0, 3.0, 1.0])
    table = np.zeros((4, 40, 2 * MOMENTS))
    for a in range(4):
        for lag in range(4 - a):
            share = np.convolve(scaled[a], scaled[a + lag]) / np.array(BINOMIAL)
            for pair in range(10):
                for n in range(7):
                    row = 8 * n + pair if pair < 8 else 56 + 8 * (pair - 8) + n
                    table[a, 10 * lag + pair, row] = share[n]
                    table[a, 10 * lag + pair, MOMENTS + row] = share[n]
    high, low = halves(table.reshape(160, 2 * MOMENTS))
    return np.concatenate([high, high, low], axis=1)


def filter_tables():
    rate = 0.1 ** (1.0 / NK)
    gain = FILTER_GAIN * (1.0 - rate) ** 2 / (1.0 - rate * rate)
    lane = np.arange(128.0)
    row = np.arange(64.0)
    near = rate ** np.abs(lane[:, None] - lane[None, :])
    from_left = np.outer(rate ** (127 - lane), rate ** (lane + 1))
    from_right = np.outer(rate**lane, rate ** (128 - lane))
    edge = np.outer(rate ** (127 - lane), rate ** (128 - lane))
    within = gain * np.concatenate([near, from_left, from_right, edge], axis=1)
    gap = row[:, None] - row[None, :]
    left = np.where(gap > 0, rate ** (128 * np.maximum(gap - 1, 0)), 0.0)
    right = np.where(gap < 0, rate ** (128 * np.maximum(-gap - 1, 0)), 0.0)
    closing = -np.outer(rate ** (NK - 128 * row - 128), rate ** (NK - 128 * row - 127))
    across = np.concatenate([left, right, closing], axis=1)
    (near_high, near_low), (far_high, far_low) = halves(within), halves(across)
    return (
        np.concatenate([near_high, near_high, near_low], axis=0),
        np.concatenate([far_high, far_high, far_low], axis=1),
    )


def split_two(value):
    high = value.astype(BF16).astype(F32)
    return jnp.concatenate([high, value - high], axis=0).astype(BF16)


def spread(value, u, rows=8):
    return jnp.broadcast_to(value[u : u + 1, :], (rows, value.shape[1]))


def sixteen(row):
    return jnp.broadcast_to(row, (16, row.shape[1])).astype(BF16)


def hot_lanes(low, count):
    low = sixteen(low)
    want = lax.broadcasted_iota(jnp.int32, low.shape, 0).astype(F32).astype(BF16)
    one, zero = jnp.ones_like(low), jnp.zeros_like(low)
    return jnp.concatenate(
        [jnp.where(low == want + BF16(16 * j), one, zero) for j in range(count // 16)], axis=0
    )


def grouped(rows, group, count):
    parts = []
    for g in range(count):
        mask = sixteen(jnp.where(group == float(g), 1.0, 0.0))
        parts.append(rows * jnp.concatenate([mask] * (rows.shape[0] // 16), axis=0))
    return jnp.concatenate(parts, axis=0)


def outer(rows, hot):
    return lax.dot_general(rows, hot, (((1,), (1,)), ((), ())), preferred_element_type=F32)


def window_kernel(
    place_ref, counts_ref, cal_hbm, weight_hbm, across_hbm, resid_hbm, knot_hbm, phase_hbm, partial_hbm,
    near_hbm, one_hbm, two_hbm, three_hbm, cal_ref, weight_ref, across_ref, resid_ref, knot_ref, phase_ref, partial_ref,
    table, more, window, begins, sems, out_sems,
):
    pairs = [
        (cal_hbm, cal_ref), (weight_hbm, weight_ref), (across_hbm, across_ref), (resid_hbm, resid_ref),
        (knot_hbm, knot_ref), (phase_hbm, phase_ref), (partial_hbm, partial_ref),
    ]
    copies = [pltpu.make_async_copy(a, b, sems.at[i]) for i, (a, b) in enumerate(pairs)]
    for copy in copies:
        copy.start()
    sub = lax.broadcasted_iota(jnp.int32, (8, 128), 0)
    lane = lax.broadcasted_iota(jnp.int32, (8, 128), 1)
    quarter = sub & 3
    upper = sub < 4
    for copy in copies[:4]:
        copy.wait()

    def step(i, total):
        tiles, hots = [], []
        for part in range(UNROLL):
            rows = pl.ds(pl.multiple_of(8 * UNROLL * i + 8 * part, 8), 8)
            ids, weight = cal_ref[rows, :], weight_ref[rows, :]
            shift, resid = across_ref[rows, :], resid_ref[rows, :]
            low, high = (ids & 127).astype(F32), ids >> 7
            weighted = weight * shift
            second = weighted * shift
            third = weight * resid
            fourth = weighted * resid
            for u in range(8):
                mask = spread(high, u) == quarter

                def pick(top, bottom):
                    return jnp.where(mask, jnp.where(upper, spread(top, u), spread(bottom, u)), 0.0)

                last = jnp.where(mask & upper, spread(fourth, u), 0.0)
                tiles.append(jnp.concatenate([pick(weight, weighted), pick(second, third), last], axis=0))
                hots.append(hot_lanes(low[u : u + 1, :], 128))
        return total + outer(split_two(jnp.concatenate(tiles, axis=1)), jnp.concatenate(hots, axis=1))

    total = lax.fori_loop(0, 8 // UNROLL, step, jnp.zeros((48, 128), F32))
    total = total[:24] + total[24:]
    for copy in copies[4:]:
        copy.wait()

    def fill(i, carry):
        rows = pl.ds(pl.multiple_of(8 * i, 8), 8)
        knot, phase = knot_ref[rows, :].astype(F32), phase_ref[rows, :]
        weight, resid = weight_ref[rows, :], resid_ref[rows, :]
        shift, number = across_ref[rows, :], cal_ref[rows, :].astype(F32)
        for u in range(8):
            here = pl.ds(pl.multiple_of(1024 * i + 128 * u, 128), 128)
            table[4:8, here] = jnp.concatenate(
                [knot[u : u + 1], phase[u : u + 1], weight[u : u + 1], resid[u : u + 1]], axis=0
            )
            more[0:2, here] = jnp.concatenate([shift[u : u + 1], number[u : u + 1]], axis=0)
        lanes = pl.ds(pl.multiple_of(1024 * i, 1024), 1024)
        table[0:4, lanes] = partial_ref[:, lanes]
        return carry

    lax.fori_loop(0, 8, fill, 0)
    begin = jnp.int32(0)
    for block in range(N_TM):
        begins[block] = begin
        begin = begin + counts_ref[0, block]
    dead = jnp.where(sub == 4, -1.0, 0.0)
    core, place_z = place_ref[0] & 1, place_ref[0] >> 1
    sent = []
    for n in range(N_TM):
        d, half = (2, 1, 3, 0)[n // 2], n % 2
        out_hbm = (near_hbm, one_hbm, two_hbm, three_hbm)[d]
        block = 2 * ((place_z + d) & 3) + (1 - core if half else core)
        count, begin = counts_ref[0, block], begins[block]
        base = pl.multiple_of((begin >> 7) << 7, 128)
        off = begin & 127
        back = (128 - off) & 127
        early = lane < 128 - off
        rolled = pltpu.roll(table[:, pl.ds(base, 128)], back, 1)
        rolled_more = pltpu.roll(more[:, pl.ds(base, 128)], back, 1)
        for j in range(CAP // 128):
            here = pl.ds(base + 128 * (j + 1), 128)
            after = pltpu.roll(table[:, here], back, 1)
            after_more = pltpu.roll(more[:, here], back, 1)
            live = lane + 128 * j < count
            window[n, :, 128 * j : 128 * (j + 1)] = jnp.where(live, jnp.where(early, rolled, after), dead)
            tile = jnp.where(live, jnp.where(early, rolled_more, after_more), 0.0)
            row, lanes = j // 4, slice(MORE + 128 * (j % 4), MORE + 128 * (j % 4) + 128)
            window[n, row : row + 1, lanes] = tile[0:1]
            window[n, 4 + row : 5 + row, lanes] = tile[1:2]
            rolled, rolled_more = after, after_more
        for k in range(3):
            window[n, :, SUMS + 128 * k : SUMS + 128 * (k + 1)] = total[8 * k : 8 * k + 8]
        sent.append(pltpu.make_async_copy(window.at[n], out_hbm.at[half], out_sems.at[n]))
        sent[-1].start()
    for copy in sent:
        copy.wait()


def each_batch(windows_ref, order, size, body):
    found = jnp.int32(0)
    for block in range(windows_ref.shape[0]):
        count = jnp.sum((windows_ref[block, 4:5, :CAP] >= 0.0).astype(jnp.int32))
        for i in range(CAP // CHUNK):
            order[found] = 4 * block + i
            found = found + (count > i * CHUNK).astype(jnp.int32)
    for u in range(size - 1):
        order[found + u] = 0

    def step(batch, carry):
        chunks = []
        for u in range(size):
            at = order[size * batch + u]
            block, i = at >> 2, at & 3
            tile = windows_ref[block, :, pl.ds(pl.multiple_of(i * CHUNK, CHUNK), CHUNK)]
            knot = jnp.where(size * batch + u < found, tile[4:5], -1.0)
            chunks.append((tile, knot, block, i))
        body(chunks)
        return carry

    lax.fori_loop(0, (found + size - 1) // size, step, 0)


def spline_basis(phase):
    square = phase * phase
    cube = square * phase
    remain = 1.0 - phase
    return [
        remain * remain * remain * (1.0 / 6.0),
        (3.0 * cube - 6.0 * square + 4.0) * (1.0 / 6.0),
        (-3.0 * cube + 3.0 * square + 3.0 * phase + 1.0) * (1.0 / 6.0),
        cube * (1.0 / 6.0),
    ]


def add_moments(windows_ref, total, order):
    def work(tile, knot):
        part = [tile[c : c + 1] for c in range(4)]
        phase, weight = tile[5:6], tile[6:7]
        remain = 1.0 - phase
        powers, others = [jnp.ones_like(phase), phase], [jnp.ones_like(phase), remain]
        for n in range(2, 7):
            powers.append(powers[n // 2] * powers[n - n // 2])
            others.append(others[n // 2] * others[n - n // 2])
        order = [weight * (BINOMIAL[n] * (powers[n] * others[6 - n])) for n in range(7)]
        left = jnp.concatenate([part[c] for c, e in PAIRS[:8]], axis=0)
        right = jnp.concatenate([part[e] for c, e in PAIRS[:8]], axis=0)
        eight = left * right
        rows = [order[n] * eight for n in range(7)]
        stack = jnp.concatenate(order + [jnp.zeros_like(phase)], axis=0)
        rows.append(stack * (part[2] * part[3]))
        rows.append(stack * (part[3] * part[3]))
        rows = split_two(jnp.concatenate(rows, axis=0))
        group = jnp.floor(knot * (1.0 / 256.0))
        low = jnp.maximum(knot, 0.0) - 256.0 * jnp.maximum(group, 0.0)
        return grouped(rows, group, 4), hot_lanes(low, 256)

    def body(chunks):
        rows, hots = zip(*[work(tile, knot) for tile, knot, block, i in chunks])
        total[...] += outer(jnp.concatenate(rows, axis=1), jnp.concatenate(hots, axis=1))

    each_batch(windows_ref, order, PART, body)


def join(here_ref, there_ref, windows_ref, at=0):
    windows_ref[at] = here_ref[0, :, :SUMS]
    windows_ref[at + 1] = there_ref[1, :, :SUMS]


def first_kernel(here_hbm, there_ref, total, windows_ref, order, sem):
    copy = pltpu.make_async_copy(here_hbm.at[0, :, pl.ds(0, SUMS)], windows_ref.at[0], sem)
    copy.start()
    total[...] = jnp.zeros_like(total)
    windows_ref[1] = there_ref[1, :, :SUMS]
    copy.wait()
    add_moments(windows_ref, total, order)


def next_kernel(before_ref, here_ref, there_ref, total, windows_ref, order):
    total[...] = before_ref[...]
    join(here_ref, there_ref, windows_ref)
    add_moments(windows_ref, total, order)


def last_kernel(before_ref, *refs):
    pairs, (select_ref, out_ref, total, tiles, windows_ref, order) = refs[:8], refs[8:]
    total[...] = before_ref[...]
    join(pairs[4], pairs[5], windows_ref)
    add_moments(windows_ref, total, order)
    parts = []
    for g in range(4):
        group = total[2 * MOMENTS * g : 2 * MOMENTS * (g + 1)]
        high = group.astype(BF16)
        low = (group - high.astype(F32)).astype(BF16)
        parts.append(
            jnp.dot(
                select_ref[...], jnp.concatenate([high, low, high], axis=0), preferred_element_type=F32
            )
        )
    parts.append(jnp.zeros((160, 128), F32))
    orders = jnp.concatenate(parts, axis=1)
    band = orders[0:40]
    for a in range(1, 4):
        band = band + pltpu.roll(orders[40 * a : 40 * a + 40], a, 1)
    for q in range(8):
        tiles[0:40, q, :] = band[:, 128 * q : 128 * (q + 1)]
    spill = band[:, K : K + 128]
    packed = spill[0:8]
    for g in range(1, 5):
        packed = packed + pltpu.roll(spill[8 * g : 8 * g + 8], 8 * g, 1)
    tiles[SPILL] = packed
    near, one, two, three = [
        pairs[2 * d][0, :, SUMS:WIDTH] + pairs[2 * d + 1][1, :, SUMS:WIDTH] for d in range(4)
    ]
    sums = (near + two) + (one + three)
    for s in range(N_SRC):
        for r in range(3):
            at = 3 * s + r
            out_ref[s, 8 * r : 8 * r + 8, :] = tiles[at] if at <= SPILL else jnp.zeros((8, 128), F32)
            out_ref[s, 24 + 8 * r : 32 + 8 * r, :] = sums[:, 128 * r : 128 * (r + 1)]


def side_kernel(*refs):
    pairs, (parts_ref, out_ref, step_ref, total, windows_ref, order) = refs[:8], refs[8:]
    total[...] = jnp.zeros_like(total)
    for d in range(4):
        join(pairs[2 * d], pairs[2 * d + 1], windows_ref, 2 * d)
    both = parts_ref[0]
    for s in range(1, N_SRC):
        both = both + parts_ref[s]
    prior = float(OBS_DEV * N_SRC * N_TM // NCAL)
    totals = both[24:48]
    zero_moment = totals[0:4] + prior
    first = totals[4:8]
    second_moment = totals[8:12] + prior
    third, fourth = totals[12:16], totals[16:20]
    det = zero_moment * second_moment - first * first
    offset = (second_moment * third - first * fourth) / det
    slope = (zero_moment * fourth - first * third) / det
    for h in range(4):
        step_ref[0:1, 128 * h : 128 * (h + 1)] = offset[h : h + 1]
        step_ref[1:2, 128 * h : 128 * (h + 1)] = slope[h : h + 1]
    steps = jnp.concatenate([offset, slope], axis=0)
    sub = lax.broadcasted_iota(jnp.int32, (8, CHUNK), 0)
    quarter = (sub & 3).astype(F32)
    upper = sub < 4

    def work(tile, knot, block, i):
        shift = windows_ref[block, pl.ds(i, 1), MORE:SUMS]
        ids = windows_ref[block, pl.ds(4 + i, 1), MORE:SUMS]
        phase, weight, resid = tile[5:6], tile[6:7], tile[7:8]
        high = jnp.floor(ids * (1.0 / 128.0))
        low = jnp.broadcast_to((ids - 128.0 * high).astype(jnp.int32), (8, CHUNK))
        found = jnp.concatenate(
            [jnp.take_along_axis(steps, low[:, 128 * k : 128 * (k + 1)], axis=1) for k in range(CHUNK // 128)],
            axis=1,
        )
        found = jnp.where(quarter == high, found, 0.0) * jnp.where(upper, 1.0, shift)
        corrected = resid - jnp.sum(found, axis=0, keepdims=True)
        basis = spline_basis(phase)
        four = tile[0:4] * (weight * corrected)
        double = jnp.concatenate([four, four], axis=0)
        rows = []
        for a in (0, 2):
            order = jnp.concatenate([basis[a]] * 4 + [basis[a + 1]] * 4, axis=0)
            rows.append(double * order)
        rows = split_two(jnp.concatenate(rows, axis=0))
        group = jnp.floor(knot * (1.0 / 128.0))
        low = jnp.maximum(knot, 0.0) - 128.0 * jnp.maximum(group, 0.0)
        return grouped(rows, group, 8), hot_lanes(low, 128)

    def body(chunks):
        rows, hots = zip(*[work(*chunk) for chunk in chunks])
        total[...] += outer(jnp.concatenate(rows, axis=1), jnp.concatenate(hots, axis=1))

    each_batch(windows_ref, order, BATCH, body)
    orders = [total[32 * g : 32 * g + 16] + total[32 * g + 16 : 32 * g + 32] for g in range(8)]
    orders = jnp.concatenate(orders + [jnp.zeros((16, 128), F32)], axis=1)
    side = orders[0:4]
    for a in range(1, 4):
        side = side + pltpu.roll(orders, a, 1)[4 * a : 4 * a + 4]
    share = both[0:24]
    spill = jnp.concatenate([side[:, K : K + 128], jnp.zeros((4, 128), F32)], axis=0)
    rows = [share]
    for c in range(4):
        rows += [side[c : c + 1, 128 * q : 128 * (q + 1)] for q in range(8)]
    rows = jnp.concatenate(rows + [spill], axis=0)
    for s in range(N_SRC):
        out_ref[s] = rows


def gather_kernel(parts_ref, out_ref):
    side = parts_ref[0, 24:64, :]
    for s in range(1, N_SRC):
        side = side + parts_ref[s, 24:64, :]
    spill = pltpu.roll(side[32:40], SPILL, 1) + parts_ref[SPILL // 3, 8 * (SPILL % 3) : 8 * (SPILL % 3) + 8, :]
    for i in range(40):
        out_ref[8 * i : 8 * i + 8, :] = parts_ref[i // 3, 8 * (i % 3) : 8 * (i % 3) + 8, :]
    out_ref[8 * SPILL : 8 * SPILL + 8, :] = spill
    out_ref[8 * SIDE : 8 * TILES, :] = side[0:32]


def stack_kernel(first_ref, second_ref, third_ref, fourth_ref, out_ref):
    for d, ref in enumerate((first_ref, second_ref, third_ref, fourth_ref)):
        out_ref[d] = ref[...]


def solve_kernel(
    place_ref, mine_ref, other_ref, coeffs_ref, within_ref, across_ref, out_ref,
    band, inverse, field, ahead, lower, applied, resid, delta, filtered, smooth,
):
    lane8 = lax.broadcasted_iota(jnp.int32, (8, 128), 1)
    lane = lax.broadcasted_iota(jnp.int32, (64, 128), 1)
    core, place_z = place_ref[0] & 1, place_ref[0] >> 1
    halves = ((mine_ref, core), (other_ref, 1 - core))
    for ref, parity in halves:
        for d in range(4):
            rows = pl.ds(pl.multiple_of(8 * (2 * ((place_z - d) & 3) + parity), 8), 8)
            for i in range(44):
                at = i if i < 40 else SIDE + i - 40
                band[i, rows, :] = ref[d, 8 * at : 8 * at + 8, :]
    for ref, parity in halves:
        for d in range(4):
            row = pl.ds(pl.multiple_of(8 * (2 * ((place_z - d) & 3) + parity) + 8, 8), 1)
            packed = ref[d, 8 * SPILL : 8 * SPILL + 8, :]
            for g in range(6):
                moved = packed if g == 0 else pltpu.roll(packed, 128 - 8 * g, 1)
                moved = jnp.where(lane8 < 3, moved, 0.0)
                for u in range(min(8, 44 - 8 * g)):
                    band[8 * g + u, row, :] += moved[u : u + 1]
    for c in range(4):
        inverse[c] = 1.0 / (ATTITUDE_PRIOR + band[PAIR_AT[(c, c)], 0:64, :])
    field[...] = jnp.zeros_like(field)
    lower[...] = jnp.zeros_like(lower)

    def total_of(left, right):
        value = left * right
        value = jnp.sum(value.reshape(32, 8, 128), axis=0)
        return jnp.sum(jnp.sum(value, axis=0, keepdims=True), axis=1, keepdims=True)

    def precondition(source):
        res = source[...].reshape(256, 128)
        high = res.astype(BF16)
        low = (res - high.astype(F32)).astype(BF16)
        spreads = jnp.dot(
            jnp.concatenate([high, low, high], axis=1), within_ref[...], preferred_element_type=F32
        )
        for c in range(4):
            own = spreads[64 * c : 64 * c + 64]
            carried = jnp.concatenate([own[:, 128:256], own[:, 256:384], own[:, 384:512]], axis=0)
            high = carried.astype(BF16)
            low = (carried - high.astype(F32)).astype(BF16)
            carry = jnp.dot(
                across_ref[...], jnp.concatenate([high, low, high], axis=0), preferred_element_type=F32
            )
            filtered[c] = source[c] * inverse[c] + own[:, :128] + carry

    def apply_normals():
        for e in range(4):
            here, after = field[e, 8:72, :], field[e, 9:73, :]
            for d in range(1, 4):
                ahead[d - 1, e] = pltpu.roll(jnp.where(lane < d, after, here), 128 - d, 1)
        for t in range(N_TM):
            rows = slice(8 * t, 8 * t + 8)
            padded = slice(8 * t + 8, 8 * t + 16)
            own = [field[e, padded, :] for e in range(4)]
            sums = [own[c] * ATTITUDE_PRIOR for c in range(4)]
            for d in range(4):
                near = own if d == 0 else [ahead[d - 1, e, rows, :] for e in range(4)]
                tiles = [band[10 * d + i, rows, :] for i in range(10)]
                for c in range(4):
                    for e in range(4):
                        sums[c] = sums[c] + tiles[PAIR_AT[(c, e)]] * near[e]
                if d:
                    for c in range(4):
                        back = tiles[PAIR_AT[(c, 0)]] * own[0]
                        for e in range(1, 4):
                            back = back + tiles[PAIR_AT[(c, e)]] * own[e]
                        lower[d - 1, c, padded, :] = back
            for c in range(4):
                applied[c, rows, :] = sums[c]
        for c in range(4):
            result = applied[c]
            for d in range(1, 4):
                here, before = lower[d - 1, c, 8:72, :], lower[d - 1, c, 7:71, :]
                result = result + pltpu.roll(jnp.where(lane >= 128 - d, before, here), d, 1)
            applied[c] = result

    resid[...] = band[40:44, 0:64, :]
    precondition(resid)
    smooth[...] = filtered[...]
    field[:, 8:72, :] = filtered[...]
    delta[...] = jnp.zeros_like(delta)
    energy = total_of(resid[...], smooth[...])

    def iterate(i, energy):
        apply_normals()
        precondition(applied)
        step = energy / total_of(field[:, 8:72, :], applied[...])
        delta[...] += step * field[:, 8:72, :]
        rest = resid[...] - step * applied[...]
        after = smooth[...] - step * filtered[...]
        resid[...] = rest
        smooth[...] = after
        fresh = total_of(rest, after)
        field[:, 8:72, :] = after + (fresh / energy) * field[:, 8:72, :]
        return fresh

    energy = lax.fori_loop(0, ITERS - 1, iterate, energy)
    apply_normals()
    step = energy / total_of(field[:, 8:72, :], applied[...])
    delta[...] += step * field[:, 8:72, :]
    mine = pl.ds(pl.multiple_of(place_ref[0] * 8, 8), 8)
    for c in range(4):
        tile = delta[c, mine, :]
        for q in range(8):
            lanes = slice(128 * q, 128 * q + 128)
            out_ref[c : c + 1, lanes] = coeffs_ref[c : c + 1, lanes] + tile[q : q + 1]


VMEM_SPEC = pl.BlockSpec(memory_space=pltpu.VMEM)
SMEM_SPEC = pl.BlockSpec(memory_space=pltpu.SMEM)
HBM_SPEC = pl.BlockSpec(memory_space=pltpu.HBM)
PARAMS = pltpu.CompilerParams(vmem_limit_bytes=VMEM_LIMIT)
CHUNKS = N_TM * CAP // CHUNK


def to_other_core(value):
    return lax.ppermute(value, "tm", [(i, i ^ 1) for i in range(N_TM)])


def along_z(value, d):
    return lax.ppermute(value, "tm", [(i, (i + 2 * d) % N_TM) for i in range(N_TM)])


def cost(microseconds):
    return pl.CostEstimate(
        flops=int(microseconds * 1_000_000_000), bytes_accessed=1_000_000, transcendentals=0
    )


def local(
    knot_index, block_counts, knot_phase, partials, obs_weight, residuals, cal_id, across, coeffs
):
    dense = [
        value.reshape(64, 128)
        for value in (cal_id, obs_weight, across, residuals, knot_index, knot_phase)
    ]
    place = lax.axis_index("tm").reshape(1)
    with jax.named_scope("windows"):
        windows = pl.pallas_call(
            window_kernel,
            out_shape=(jax.ShapeDtypeStruct((2, 8, WIDTH), F32),) * 4,
            in_specs=[SMEM_SPEC] * 2 + [HBM_SPEC] * 7,
            out_specs=(HBM_SPEC,) * 4,
            scratch_shapes=[pltpu.VMEM((64, 128), value.dtype) for value in dense]
            + [
                pltpu.VMEM((4, OBS_DEV), F32),
                pltpu.VMEM((8, OBS_DEV + CAP + 128), F32),
                pltpu.VMEM((8, OBS_DEV + CAP + 128), F32),
                pltpu.VMEM((N_TM, 8, WIDTH), F32),
                pltpu.SMEM((N_TM,), jnp.int32),
                pltpu.SemaphoreType.DMA((7,)),
                pltpu.SemaphoreType.DMA((N_TM,)),
            ],
            compiler_params=pltpu.CompilerParams(vmem_limit_bytes=56 * 1024 * 1024),
        )(place, block_counts, *dense, partials)
    with jax.named_scope("to_owners"):
        windows = [windows[0]] + [along_z(windows[d], d) for d in (1, 2, 3)]
        near = (windows[0], to_other_core(windows[0]))
    with jax.named_scope("moments"):
        total = jax.ShapeDtypeStruct((8 * MOMENTS, 256), F32)
        scratch = [pltpu.VMEM((2, 8, SUMS), F32), pltpu.SMEM((CHUNKS,), jnp.int32)]
        moments = pl.pallas_call(
            first_kernel,
            out_shape=total,
            in_specs=[HBM_SPEC, VMEM_SPEC],
            out_specs=VMEM_SPEC,
            scratch_shapes=[*scratch, pltpu.SemaphoreType.DMA],
            compiler_params=PARAMS,
            cost_estimate=cost(2),
        )(*near)
        moments, one = lax.optimization_barrier((moments, windows[1]))
        moments, three = lax.optimization_barrier((moments, windows[3]))
        pairs = [near] + [(here, to_other_core(here)) for here in (one, windows[2], three)]
        for d in (1, 3):
            moments = pl.pallas_call(
                next_kernel,
                out_shape=total,
                in_specs=[VMEM_SPEC] * 3,
                out_specs=VMEM_SPEC,
                scratch_shapes=scratch,
                compiler_params=PARAMS,
                cost_estimate=cost(2),
            )(moments, *pairs[d])
        refs = [ref for pair in pairs for ref in pair]
        parts = pl.pallas_call(
            last_kernel,
            out_shape=jax.ShapeDtypeStruct((N_SRC, 48, 128), F32),
            in_specs=[VMEM_SPEC] * 10,
            out_specs=VMEM_SPEC,
            scratch_shapes=[
                pltpu.VMEM((8 * MOMENTS, 256), F32),
                pltpu.VMEM((SPILL + 1, 8, 128), F32),
                *scratch,
            ],
            compiler_params=PARAMS,
        )(moments, *refs, jnp.asarray(select_rows()))
    with jax.named_scope("band_reduce"):
        parts = lax.all_to_all(parts, "src", 0, 0)
    with jax.named_scope("side"):
        parts, calibration_step = pl.pallas_call(
            side_kernel,
            out_shape=(
                jax.ShapeDtypeStruct((N_SRC, 64, 128), F32),
                jax.ShapeDtypeStruct((2, NCAL), F32),
            ),
            in_specs=[VMEM_SPEC] * 9,
            out_specs=(VMEM_SPEC, VMEM_SPEC),
            scratch_shapes=[
                pltpu.VMEM((256, 128), F32),
                pltpu.VMEM((N_TM, 8, SUMS), F32),
                pltpu.SMEM((CHUNKS + BATCH,), jnp.int32),
            ],
            compiler_params=PARAMS,
        )(*refs, parts)
    with jax.named_scope("gather_src"):
        parts = lax.all_to_all(parts, "src", 0, 0)
    with jax.named_scope("gather"):
        parts = pl.pallas_call(
            gather_kernel,
            out_shape=jax.ShapeDtypeStruct((8 * TILES, 128), F32),
            in_specs=[VMEM_SPEC],
            out_specs=VMEM_SPEC,
            compiler_params=PARAMS,
        )(parts)
    with jax.named_scope("gather_z"):
        mine = pl.pallas_call(
            stack_kernel,
            out_shape=jax.ShapeDtypeStruct((4, 8 * TILES, 128), F32),
            in_specs=[VMEM_SPEC] * 4,
            out_specs=VMEM_SPEC,
            compiler_params=PARAMS,
        )(parts, *[along_z(parts, d) for d in (1, 2, 3)])
    with jax.named_scope("gather_core"):
        other = to_other_core(mine)
    within, across_rows = filter_tables()
    with jax.named_scope("solve"):
        new_coeffs = pl.pallas_call(
            solve_kernel,
            out_shape=jax.ShapeDtypeStruct((4, K), F32),
            in_specs=[SMEM_SPEC] + [VMEM_SPEC] * 5,
            out_specs=VMEM_SPEC,
            scratch_shapes=[
                pltpu.VMEM((44, 72, 128), F32),
                pltpu.VMEM((4, 64, 128), F32),
                pltpu.VMEM((4, 80, 128), F32),
                pltpu.VMEM((3, 4, 64, 128), F32),
                pltpu.VMEM((3, 4, 80, 128), F32),
                pltpu.VMEM((4, 64, 128), F32),
                pltpu.VMEM((4, 64, 128), F32),
                pltpu.VMEM((4, 64, 128), F32),
                pltpu.VMEM((4, 64, 128), F32),
                pltpu.VMEM((4, 64, 128), F32),
            ],
            compiler_params=PARAMS,
        )(
            place, mine, other, coeffs, jnp.asarray(within),
            jnp.asarray(across_rows),
        )
    return (new_coeffs, calibration_step)


def solution(mesh):
    placed = (
        P(("src", "tm")),
        P(("src", "tm"), None),
        P(("src", "tm")),
        P(None, ("src", "tm")),
        P(("src", "tm")),
        P(("src", "tm")),
        P(("src", "tm")),
        P(("src", "tm")),
        P(None, "tm"),
    )
    return jax.shard_map(
        local, mesh=mesh, in_specs=placed, out_specs=(P(None, "tm"), P()), check_vma=False
    )
```

```python
import jax
import jax.numpy as jnp
import ml_dtypes
import numpy as np
from jax import lax
from jax.experimental import pallas as pl
from jax.experimental.pallas import tpu as pltpu
from jax.sharding import PartitionSpec as P

K = 1024
OBS_DEV = 8192
NCAL = 512
ITERS = 6
N_SRC = 16
N_TM = 8
NK = K * N_TM
CAP = 2 * OBS_DEV // N_TM
ATTITUDE_PRIOR = 1.0
FILTER_GAIN = 0.05
CHUNK = 512
PART, BATCH = 2, 4
UNROLL = 8
HIGHEST = lax.Precision.HIGHEST
F32 = jnp.float32
BF16 = jnp.bfloat16
VMEM_LIMIT = 48 * 1024 * 1024

PAIRS = [(a, b) for a in range(4) for b in range(a, 4)]
PAIR_AT = {pair: i for i, pair in enumerate(PAIRS)}
PAIR_AT.update({(b, a): i for (a, b), i in list(PAIR_AT.items())})
SPILL, SIDE, TILES = 40, 41, 45
MORE, SPAN = CAP, CAP + CHUNK
WIDTH = 2 * SPAN + 384
MOMENTS = 72
BINOMIAL = [1.0, 6.0, 15.0, 20.0, 15.0, 6.0, 1.0]


def halves(table):
    high = table.astype(ml_dtypes.bfloat16)
    return high, (table - high.astype(np.float64)).astype(ml_dtypes.bfloat16)


def select_rows():
    cubic = np.array([[1, 0, 0, 0], [4, 4, 2, 1], [1, 2, 4, 4], [0, 0, 0, 1]]) / 6.0
    scaled = cubic * np.array([1.0, 3.0, 3.0, 1.0])
    table = np.zeros((4, 40, 2 * MOMENTS))
    for a in range(4):
        for lag in range(4 - a):
            share = np.convolve(scaled[a], scaled[a + lag]) / np.array(BINOMIAL)
            for pair in range(10):
                for n in range(7):
                    row = 8 * n + pair if pair < 8 else 56 + 8 * (pair - 8) + n
                    table[a, 10 * lag + pair, row] = share[n]
                    table[a, 10 * lag + pair, MOMENTS + row] = share[n]
    high, low = halves(table.reshape(160, 2 * MOMENTS))
    return np.concatenate([high, high, low], axis=1)


def filter_tables():
    rate = 0.1 ** (1.0 / NK)
    gain = FILTER_GAIN * (1.0 - rate) ** 2 / (1.0 - rate * rate)
    lane = np.arange(128.0)
    row = np.arange(64.0)
    near = rate ** np.abs(lane[:, None] - lane[None, :])
    from_left = np.outer(rate ** (127 - lane), rate ** (lane + 1))
    from_right = np.outer(rate**lane, rate ** (128 - lane))
    edge = np.outer(rate ** (127 - lane), rate ** (128 - lane))
    within = gain * np.concatenate([near, from_left, from_right, edge], axis=1)
    gap = row[:, None] - row[None, :]
    left = np.where(gap > 0, rate ** (128 * np.maximum(gap - 1, 0)), 0.0)
    right = np.where(gap < 0, rate ** (128 * np.maximum(-gap - 1, 0)), 0.0)
    closing = -np.outer(rate ** (NK - 128 * row - 128), rate ** (NK - 128 * row - 127))
    across = np.concatenate([left, right, closing], axis=1)
    (near_high, near_low), (far_high, far_low) = halves(within), halves(across)
    return (
        np.concatenate([near_high, near_high, near_low], axis=0),
        np.concatenate([far_high, far_high, far_low], axis=1),
    )


def split_two(value):
    high = value.astype(BF16).astype(F32)
    return jnp.concatenate([high, value - high], axis=0).astype(BF16)


def spread(value, u, rows=8):
    return jnp.broadcast_to(value[u : u + 1, :], (rows, value.shape[1]))


def sixteen(row):
    return jnp.broadcast_to(row, (16, row.shape[1])).astype(BF16)


def hot_lanes(low, count):
    low = sixteen(low)
    want = lax.broadcasted_iota(jnp.int32, low.shape, 0).astype(F32).astype(BF16)
    one, zero = jnp.ones_like(low), jnp.zeros_like(low)
    return jnp.concatenate(
        [jnp.where(low == want + BF16(16 * j), one, zero) for j in range(count // 16)], axis=0
    )


def grouped(rows, group, count):
    parts = []
    for g in range(count):
        mask = sixteen(jnp.where(group == float(g), 1.0, 0.0))
        parts.append(rows * jnp.concatenate([mask] * (rows.shape[0] // 16), axis=0))
    return jnp.concatenate(parts, axis=0)


def outer(rows, hot):
    return lax.dot_general(rows, hot, (((1,), (1,)), ((), ())), preferred_element_type=F32)


def window_kernel(
    place_ref, counts_ref, cal_hbm, weight_hbm, across_hbm, resid_hbm, knot_hbm, phase_hbm, partial_hbm,
    near_hbm, one_hbm, two_hbm, three_hbm, cal_ref, weight_ref, across_ref, resid_ref, knot_ref, phase_ref, partial_ref,
    table, more, window, begins, sems, out_sems,
):
    pairs = [
        (cal_hbm, cal_ref), (weight_hbm, weight_ref), (across_hbm, across_ref), (resid_hbm, resid_ref),
        (knot_hbm, knot_ref), (phase_hbm, phase_ref), (partial_hbm, partial_ref),
    ]
    copies = [pltpu.make_async_copy(a, b, sems.at[i]) for i, (a, b) in enumerate(pairs)]
    for copy in copies:
        copy.start()
    sub = lax.broadcasted_iota(jnp.int32, (8, 128), 0)
    lane = lax.broadcasted_iota(jnp.int32, (8, 128), 1)
    quarter = sub & 3
    upper = sub < 4
    for copy in copies[:4]:
        copy.wait()

    def step(i, total):
        tiles, hots = [], []
        for part in range(UNROLL):
            rows = pl.ds(pl.multiple_of(8 * UNROLL * i + 8 * part, 8), 8)
            ids, weight = cal_ref[rows, :], weight_ref[rows, :]
            shift, resid = across_ref[rows, :], resid_ref[rows, :]
            low, high = (ids & 127).astype(F32), ids >> 7
            weighted = weight * shift
            second = weighted * shift
            third = weight * resid
            fourth = weighted * resid
            for u in range(8):
                mask = spread(high, u) == quarter

                def pick(top, bottom):
                    return jnp.where(mask, jnp.where(upper, spread(top, u), spread(bottom, u)), 0.0)

                last = jnp.where(mask & upper, spread(fourth, u), 0.0)
                tiles.append(jnp.concatenate([pick(weight, weighted), pick(second, third), last], axis=0))
                hots.append(hot_lanes(low[u : u + 1, :], 128))
        return total + outer(split_two(jnp.concatenate(tiles, axis=1)), jnp.concatenate(hots, axis=1))

    total = lax.fori_loop(0, 8 // UNROLL, step, jnp.zeros((48, 128), F32))
    total = total[:24] + total[24:]
    for copy in copies[4:]:
        copy.wait()

    def fill(i, carry):
        rows = pl.ds(pl.multiple_of(8 * i, 8), 8)
        knot, phase = knot_ref[rows, :].astype(F32), phase_ref[rows, :]
        weight, resid = weight_ref[rows, :], resid_ref[rows, :]
        shift, number = across_ref[rows, :], cal_ref[rows, :].astype(F32)
        for u in range(8):
            here = pl.ds(pl.multiple_of(1024 * i + 128 * u, 128), 128)
            table[4:8, here] = jnp.concatenate(
                [knot[u : u + 1], phase[u : u + 1], weight[u : u + 1], resid[u : u + 1]], axis=0
            )
            more[0:2, here] = jnp.concatenate([shift[u : u + 1], number[u : u + 1]], axis=0)
        lanes = pl.ds(pl.multiple_of(1024 * i, 1024), 1024)
        table[0:4, lanes] = partial_ref[:, lanes]
        return carry

    lax.fori_loop(0, 8, fill, 0)
    begin = jnp.int32(0)
    for block in range(N_TM):
        begins[block] = begin
        begin = begin + counts_ref[0, block]
    dead = jnp.where(sub == 4, -1.0, 0.0)
    core, place_z = place_ref[0] & 1, place_ref[0] >> 1
    sent = []
    for n in range(N_TM):
        d, half = (2, 1, 3, 0)[n // 2], n % 2
        start = SPAN * half
        out_hbm = (near_hbm, one_hbm, two_hbm, three_hbm)[d]
        block = 2 * ((place_z + d) & 3) + (1 - core if half else core)
        count, begin = counts_ref[0, block], begins[block]
        base = pl.multiple_of((begin >> 7) << 7, 128)
        off = begin & 127
        back = (128 - off) & 127
        early = lane < 128 - off
        rolled = pltpu.roll(table[:, pl.ds(base, 128)], back, 1)
        rolled_more = pltpu.roll(more[:, pl.ds(base, 128)], back, 1)
        for j in range(CAP // 128):
            here = pl.ds(base + 128 * (j + 1), 128)
            after = pltpu.roll(table[:, here], back, 1)
            after_more = pltpu.roll(more[:, here], back, 1)
            live = lane + 128 * j < count
            window[d, :, start + 128 * j : start + 128 * (j + 1)] = jnp.where(live, jnp.where(early, rolled, after), dead)
            tile = jnp.where(live, jnp.where(early, rolled_more, after_more), 0.0)
            row, lanes = j // 4, pl.ds(start + MORE + 128 * (j % 4), 128)
            window[d, row : row + 1, lanes] = tile[0:1]
            window[d, 4 + row : 5 + row, lanes] = tile[1:2]
            rolled, rolled_more = after, after_more
        if half:
            for k in range(3):
                at = 2 * SPAN + 128 * k
                window[d, :, at : at + 128] = total[8 * k : 8 * k + 8]
            sent.append(pltpu.make_async_copy(window.at[d], out_hbm, out_sems.at[d]))
            sent[-1].start()
    for copy in sent:
        copy.wait()


def each_batch(windows_ref, order, size, body):
    found = jnp.int32(0)
    for block in range(windows_ref.shape[0]):
        count = jnp.sum((windows_ref[block, 4:5, :CAP] >= 0.0).astype(jnp.int32))
        for i in range(CAP // CHUNK):
            order[found] = 4 * block + i
            found = found + (count > i * CHUNK).astype(jnp.int32)
    for u in range(size - 1):
        order[found + u] = 0

    def step(batch, carry):
        chunks = []
        for u in range(size):
            at = order[size * batch + u]
            block, i = at >> 2, at & 3
            tile = windows_ref[block, :, pl.ds(pl.multiple_of(i * CHUNK, CHUNK), CHUNK)]
            knot = jnp.where(size * batch + u < found, tile[4:5], -1.0)
            chunks.append((tile, knot, block, i))
        body(chunks)
        return carry

    lax.fori_loop(0, (found + size - 1) // size, step, 0)


def spline_basis(phase):
    square = phase * phase
    cube = square * phase
    remain = 1.0 - phase
    return [
        remain * remain * remain * (1.0 / 6.0),
        (3.0 * cube - 6.0 * square + 4.0) * (1.0 / 6.0),
        (-3.0 * cube + 3.0 * square + 3.0 * phase + 1.0) * (1.0 / 6.0),
        cube * (1.0 / 6.0),
    ]


def add_moments(windows_ref, total, order, size):
    def work(tile, knot):
        part = [tile[c : c + 1] for c in range(4)]
        phase, weight = tile[5:6], tile[6:7]
        remain = 1.0 - phase
        powers, others = [jnp.ones_like(phase), phase], [jnp.ones_like(phase), remain]
        for n in range(2, 7):
            powers.append(powers[n // 2] * powers[n - n // 2])
            others.append(others[n // 2] * others[n - n // 2])
        order = [weight * (BINOMIAL[n] * (powers[n] * others[6 - n])) for n in range(7)]
        left = jnp.concatenate([part[c] for c, e in PAIRS[:8]], axis=0)
        right = jnp.concatenate([part[e] for c, e in PAIRS[:8]], axis=0)
        eight = left * right
        rows = [order[n] * eight for n in range(7)]
        stack = jnp.concatenate(order + [jnp.zeros_like(phase)], axis=0)
        rows.append(stack * (part[2] * part[3]))
        rows.append(stack * (part[3] * part[3]))
        rows = split_two(jnp.concatenate(rows, axis=0))
        group = jnp.floor(knot * (1.0 / 256.0))
        low = jnp.maximum(knot, 0.0) - 256.0 * jnp.maximum(group, 0.0)
        return grouped(rows, group, 4), hot_lanes(low, 256)

    def body(chunks):
        rows, hots = zip(*[work(tile, knot) for tile, knot, block, i in chunks])
        total[...] += outer(jnp.concatenate(rows, axis=1), jnp.concatenate(hots, axis=1))

    each_batch(windows_ref, order, size, body)


def join(here_ref, there_ref, windows_ref, at=0):
    windows_ref[at] = here_ref[:, 0:SPAN]
    windows_ref[at + 1] = there_ref[:, SPAN : 2 * SPAN]


def first_kernel(here_hbm, there_ref, total, windows_ref, order, sem):
    copy = pltpu.make_async_copy(here_hbm.at[:, pl.ds(0, SPAN)], windows_ref.at[0], sem)
    copy.start()
    total[...] = jnp.zeros_like(total)
    windows_ref[1] = there_ref[:, SPAN : 2 * SPAN]
    copy.wait()
    add_moments(windows_ref, total, order, PART)


def next_kernel(before_ref, one_ref, one_there_ref, three_ref, three_there_ref, total, windows_ref, order):
    total[...] = before_ref[...]
    join(one_ref, one_there_ref, windows_ref)
    join(three_ref, three_there_ref, windows_ref, 2)
    add_moments(windows_ref, total, order, BATCH)


def last_kernel(before_ref, *refs):
    pairs, (select_ref, out_ref, total, tiles, windows_ref, order) = refs[:8], refs[8:]
    total[...] = before_ref[...]
    join(pairs[4], pairs[5], windows_ref)
    add_moments(windows_ref, total, order, PART)
    parts = []
    for g in range(4):
        group = total[2 * MOMENTS * g : 2 * MOMENTS * (g + 1)]
        high = group.astype(BF16)
        low = (group - high.astype(F32)).astype(BF16)
        parts.append(
            jnp.dot(
                select_ref[...], jnp.concatenate([high, low, high], axis=0), preferred_element_type=F32
            )
        )
    parts.append(jnp.zeros((160, 128), F32))
    orders = jnp.concatenate(parts, axis=1)
    band = orders[0:40]
    for a in range(1, 4):
        band = band + pltpu.roll(orders[40 * a : 40 * a + 40], a, 1)
    for q in range(8):
        tiles[0:40, q, :] = band[:, 128 * q : 128 * (q + 1)]
    spill = band[:, K : K + 128]
    packed = spill[0:8]
    for g in range(1, 5):
        packed = packed + pltpu.roll(spill[8 * g : 8 * g + 8], 8 * g, 1)
    tiles[SPILL] = packed
    near, one, two, three = [
        pairs[2 * d][:, 2 * SPAN : WIDTH] + pairs[2 * d + 1][:, 2 * SPAN : WIDTH] for d in range(4)
    ]
    sums = (near + two) + (one + three)
    for s in range(N_SRC):
        for r in range(3):
            at = 3 * s + r
            out_ref[s, 8 * r : 8 * r + 8, :] = tiles[at] if at <= SPILL else jnp.zeros((8, 128), F32)
            out_ref[s, 24 + 8 * r : 32 + 8 * r, :] = sums[:, 128 * r : 128 * (r + 1)]


def side_kernel(*refs):
    pairs, (parts_ref, out_ref, step_ref, total, windows_ref, order) = refs[:8], refs[8:]
    total[...] = jnp.zeros_like(total)
    for d in range(4):
        join(pairs[2 * d], pairs[2 * d + 1], windows_ref, 2 * d)
    both = parts_ref[0]
    for s in range(1, N_SRC):
        both = both + parts_ref[s]
    prior = float(OBS_DEV * N_SRC * N_TM // NCAL)
    totals = both[24:48]
    zero_moment = totals[0:4] + prior
    first = totals[4:8]
    second_moment = totals[8:12] + prior
    third, fourth = totals[12:16], totals[16:20]
    det = zero_moment * second_moment - first * first
    offset = (second_moment * third - first * fourth) / det
    slope = (zero_moment * fourth - first * third) / det
    for h in range(4):
        step_ref[0:1, 128 * h : 128 * (h + 1)] = offset[h : h + 1]
        step_ref[1:2, 128 * h : 128 * (h + 1)] = slope[h : h + 1]
    steps = jnp.concatenate([offset, slope], axis=0)
    sub = lax.broadcasted_iota(jnp.int32, (8, CHUNK), 0)
    quarter = (sub & 3).astype(F32)
    upper = sub < 4

    def work(tile, knot, block, i):
        shift = windows_ref[block, pl.ds(i, 1), MORE:SPAN]
        ids = windows_ref[block, pl.ds(4 + i, 1), MORE:SPAN]
        phase, weight, resid = tile[5:6], tile[6:7], tile[7:8]
        high = jnp.floor(ids * (1.0 / 128.0))
        low = jnp.broadcast_to((ids - 128.0 * high).astype(jnp.int32), (8, CHUNK))
        found = jnp.concatenate(
            [jnp.take_along_axis(steps, low[:, 128 * k : 128 * (k + 1)], axis=1) for k in range(CHUNK // 128)],
            axis=1,
        )
        found = jnp.where(quarter == high, found, 0.0) * jnp.where(upper, 1.0, shift)
        corrected = resid - jnp.sum(found, axis=0, keepdims=True)
        basis = spline_basis(phase)
        four = tile[0:4] * (weight * corrected)
        double = jnp.concatenate([four, four], axis=0)
        rows = []
        for a in (0, 2):
            order = jnp.concatenate([basis[a]] * 4 + [basis[a + 1]] * 4, axis=0)
            rows.append(double * order)
        rows = split_two(jnp.concatenate(rows, axis=0))
        group = jnp.floor(knot * (1.0 / 128.0))
        low = jnp.maximum(knot, 0.0) - 128.0 * jnp.maximum(group, 0.0)
        return grouped(rows, group, 8), hot_lanes(low, 128)

    def body(chunks):
        rows, hots = zip(*[work(*chunk) for chunk in chunks])
        total[...] += outer(jnp.concatenate(rows, axis=1), jnp.concatenate(hots, axis=1))

    each_batch(windows_ref, order, BATCH, body)
    orders = [total[32 * g : 32 * g + 16] + total[32 * g + 16 : 32 * g + 32] for g in range(8)]
    orders = jnp.concatenate(orders + [jnp.zeros((16, 128), F32)], axis=1)
    side = orders[0:4]
    for a in range(1, 4):
        side = side + pltpu.roll(orders, a, 1)[4 * a : 4 * a + 4]
    share = both[0:24]
    spill = jnp.concatenate([side[:, K : K + 128], jnp.zeros((4, 128), F32)], axis=0)
    rows = [share]
    for c in range(4):
        rows += [side[c : c + 1, 128 * q : 128 * (q + 1)] for q in range(8)]
    rows = jnp.concatenate(rows + [spill], axis=0)
    for s in range(N_SRC):
        out_ref[s] = rows


def gather_kernel(parts_ref, out_ref):
    side = parts_ref[0, 24:64, :]
    for s in range(1, N_SRC):
        side = side + parts_ref[s, 24:64, :]
    spill = pltpu.roll(side[32:40], SPILL, 1) + parts_ref[SPILL // 3, 8 * (SPILL % 3) : 8 * (SPILL % 3) + 8, :]
    for i in range(40):
        out_ref[8 * i : 8 * i + 8, :] = parts_ref[i // 3, 8 * (i % 3) : 8 * (i % 3) + 8, :]
    out_ref[8 * SPILL : 8 * SPILL + 8, :] = spill
    out_ref[8 * SIDE : 8 * TILES, :] = side[0:32]


def stack_kernel(first_ref, second_ref, third_ref, fourth_ref, out_ref):
    for d, ref in enumerate((first_ref, second_ref, third_ref, fourth_ref)):
        out_ref[d] = ref[...]


def solve_kernel(
    place_ref, mine_ref, other_ref, coeffs_ref, within_ref, across_ref, out_ref,
    band, inverse, field, ahead, lower, applied, resid, delta, filtered, smooth, spare,
):
    lane8 = lax.broadcasted_iota(jnp.int32, (8, 128), 1)
    lane = lax.broadcasted_iota(jnp.int32, (64, 128), 1)
    core, place_z = place_ref[0] & 1, place_ref[0] >> 1
    halves = ((mine_ref, core), (other_ref, 1 - core))
    for ref, parity in halves:
        for d in range(4):
            rows = pl.ds(pl.multiple_of(8 * (2 * ((place_z - d) & 3) + parity), 8), 8)
            for i in range(44):
                at = i if i < 40 else SIDE + i - 40
                band[i, rows, :] = ref[d, 8 * at : 8 * at + 8, :]
    for ref, parity in halves:
        for d in range(4):
            row = pl.ds(pl.multiple_of(8 * (2 * ((place_z - d) & 3) + parity) + 8, 8), 1)
            packed = ref[d, 8 * SPILL : 8 * SPILL + 8, :]
            for g in range(6):
                moved = packed if g == 0 else pltpu.roll(packed, 128 - 8 * g, 1)
                moved = jnp.where(lane8 < 3, moved, 0.0)
                for u in range(min(8, 44 - 8 * g)):
                    band[8 * g + u, row, :] += moved[u : u + 1]
    for c in range(4):
        inverse[c] = 1.0 / (ATTITUDE_PRIOR + band[PAIR_AT[(c, c)], 0:64, :])
    field[...] = jnp.zeros_like(field)
    spare[...] = jnp.zeros_like(spare)

    def total_of(left, right):
        value = left * right
        value = jnp.sum(value.reshape(32, 8, 128), axis=0)
        return jnp.sum(jnp.sum(value, axis=0, keepdims=True), axis=1, keepdims=True)

    def precondition(source):
        res = source[...].reshape(256, 128)
        high = res.astype(BF16)
        low = (res - high.astype(F32)).astype(BF16)
        spreads = jnp.dot(
            jnp.concatenate([high, low, high], axis=1), within_ref[...], preferred_element_type=F32
        )
        for c in range(4):
            own = spreads[64 * c : 64 * c + 64]
            carried = jnp.concatenate([own[:, 128:256], own[:, 256:384], own[:, 384:512]], axis=0)
            high = carried.astype(BF16)
            low = (carried - high.astype(F32)).astype(BF16)
            carry = jnp.dot(
                across_ref[...], jnp.concatenate([high, low, high], axis=0), preferred_element_type=F32
            )
            filtered[c] = source[c] * inverse[c] + own[:, :128] + carry

    def apply_normals():
        for e in range(4):
            here, after = field[e, 8:72, :], field[e, 9:73, :]
            for d in range(1, 4):
                ahead[d - 1, e] = pltpu.roll(jnp.where(lane < d, after, here), 128 - d, 1)
        for t in range(N_TM):
            rows = slice(8 * t, 8 * t + 8)
            padded = slice(8 * t + 8, 8 * t + 16)
            own = [field[e, padded, :] for e in range(4)]
            sums = [own[c] * ATTITUDE_PRIOR for c in range(4)]
            for d in range(4):
                near = own if d == 0 else [ahead[d - 1, e, rows, :] for e in range(4)]
                tiles = [band[10 * d + i, rows, :] for i in range(10)]
                for c in range(4):
                    for e in range(4):
                        sums[c] = sums[c] + tiles[PAIR_AT[(c, e)]] * near[e]
                if d:
                    for c in range(4):
                        back = tiles[PAIR_AT[(c, 0)]] * own[0]
                        for e in range(1, 4):
                            back = back + tiles[PAIR_AT[(c, e)]] * own[e]
                        lower[d - 1, c, rows, :] = back
            for c in range(4):
                applied[c, rows, :] = sums[c]
        for c in range(4):
            result = applied[c]
            wrapped = jnp.zeros((64, 128), F32)
            for d in range(1, 4):
                moved = pltpu.roll(lower[d - 1, c], d, 1)
                result = result + jnp.where(lane >= d, moved, 0.0)
                wrapped = wrapped + jnp.where(lane < d, moved, 0.0)
            spare[c, 8:72, :] = wrapped
            applied[c] = result + spare[c, 7:71, :]

    resid[...] = band[40:44, 0:64, :]
    precondition(resid)
    smooth[...] = filtered[...]
    field[:, 8:72, :] = filtered[...]
    delta[...] = jnp.zeros_like(delta)
    energy = total_of(resid[...], smooth[...])

    def iterate(i, energy):
        apply_normals()
        precondition(applied)
        step = energy / total_of(field[:, 8:72, :], applied[...])
        delta[...] += step * field[:, 8:72, :]
        rest = resid[...] - step * applied[...]
        after = smooth[...] - step * filtered[...]
        resid[...] = rest
        smooth[...] = after
        fresh = total_of(rest, after)
        field[:, 8:72, :] = after + (fresh / energy) * field[:, 8:72, :]
        return fresh

    energy = lax.fori_loop(0, ITERS - 1, iterate, energy)
    apply_normals()
    step = energy / total_of(field[:, 8:72, :], applied[...])
    delta[...] += step * field[:, 8:72, :]
    mine = pl.ds(pl.multiple_of(place_ref[0] * 8, 8), 8)
    for c in range(4):
        tile = delta[c, mine, :]
        for q in range(8):
            lanes = slice(128 * q, 128 * q + 128)
            out_ref[c : c + 1, lanes] = coeffs_ref[c : c + 1, lanes] + tile[q : q + 1]


VMEM_SPEC = pl.BlockSpec(memory_space=pltpu.VMEM)
SMEM_SPEC = pl.BlockSpec(memory_space=pltpu.SMEM)
HBM_SPEC = pl.BlockSpec(memory_space=pltpu.HBM)
PARAMS = pltpu.CompilerParams(vmem_limit_bytes=VMEM_LIMIT)
CHUNKS = N_TM * CAP // CHUNK


def to_other_core(value):
    return lax.ppermute(value, "tm", [(i, i ^ 1) for i in range(N_TM)])


def along_z(value, d):
    return lax.ppermute(value, "tm", [(i, (i + 2 * d) % N_TM) for i in range(N_TM)])


def cost(microseconds):
    return pl.CostEstimate(
        flops=int(microseconds * 1_000_000_000), bytes_accessed=1_000_000, transcendentals=0
    )


def local(
    knot_index, block_counts, knot_phase, partials, obs_weight, residuals, cal_id, across, coeffs
):
    dense = [
        value.reshape(64, 128)
        for value in (cal_id, obs_weight, across, residuals, knot_index, knot_phase)
    ]
    place = lax.axis_index("tm").reshape(1)
    with jax.named_scope("windows"):
        windows = pl.pallas_call(
            window_kernel,
            out_shape=(jax.ShapeDtypeStruct((8, WIDTH), F32),) * 4,
            in_specs=[SMEM_SPEC] * 2 + [HBM_SPEC] * 7,
            out_specs=(HBM_SPEC,) * 4,
            scratch_shapes=[pltpu.VMEM((64, 128), value.dtype) for value in dense]
            + [
                pltpu.VMEM((4, OBS_DEV), F32),
                pltpu.VMEM((8, OBS_DEV + CAP + 128), F32),
                pltpu.VMEM((8, OBS_DEV + CAP + 128), F32),
                pltpu.VMEM((4, 8, WIDTH), F32),
                pltpu.SMEM((N_TM,), jnp.int32),
                pltpu.SemaphoreType.DMA((7,)),
                pltpu.SemaphoreType.DMA((4,)),
            ],
            compiler_params=pltpu.CompilerParams(vmem_limit_bytes=56 * 1024 * 1024),
        )(place, block_counts, *dense, partials)
    with jax.named_scope("to_owners"):
        windows = [windows[0]] + [along_z(windows[d], d) for d in (1, 2, 3)]
        near = (windows[0], to_other_core(windows[0]))
    with jax.named_scope("moments"):
        total = jax.ShapeDtypeStruct((8 * MOMENTS, 256), F32)
        scratch = [pltpu.VMEM((2, 8, SPAN), F32), pltpu.SMEM((CHUNKS,), jnp.int32)]
        moments = pl.pallas_call(
            first_kernel,
            out_shape=total,
            in_specs=[HBM_SPEC, VMEM_SPEC],
            out_specs=VMEM_SPEC,
            scratch_shapes=[*scratch, pltpu.SemaphoreType.DMA],
            compiler_params=PARAMS,
            cost_estimate=cost(2),
        )(*near)
        moments, one = lax.optimization_barrier((moments, windows[1]))
        moments, three = lax.optimization_barrier((moments, windows[3]))
        pairs = [near] + [(here, to_other_core(here)) for here in (one, windows[2], three)]
        moments = pl.pallas_call(
            next_kernel,
            out_shape=total,
            in_specs=[VMEM_SPEC] * 5,
            out_specs=VMEM_SPEC,
            scratch_shapes=[pltpu.VMEM((4, 8, SPAN), F32), pltpu.SMEM((CHUNKS,), jnp.int32)],
            compiler_params=PARAMS,
            cost_estimate=cost(2),
        )(moments, *pairs[1], *pairs[3])
        refs = [ref for pair in pairs for ref in pair]
        parts = pl.pallas_call(
            last_kernel,
            out_shape=jax.ShapeDtypeStruct((N_SRC, 48, 128), F32),
            in_specs=[VMEM_SPEC] * 10,
            out_specs=VMEM_SPEC,
            scratch_shapes=[
                pltpu.VMEM((8 * MOMENTS, 256), F32),
                pltpu.VMEM((SPILL + 1, 8, 128), F32),
                *scratch,
            ],
            compiler_params=PARAMS,
        )(moments, *refs, jnp.asarray(select_rows()))
    with jax.named_scope("band_reduce"):
        parts = lax.all_to_all(parts, "src", 0, 0)
    with jax.named_scope("side"):
        parts, calibration_step = pl.pallas_call(
            side_kernel,
            out_shape=(
                jax.ShapeDtypeStruct((N_SRC, 64, 128), F32),
                jax.ShapeDtypeStruct((2, NCAL), F32),
            ),
            in_specs=[VMEM_SPEC] * 9,
            out_specs=(VMEM_SPEC, VMEM_SPEC),
            scratch_shapes=[
                pltpu.VMEM((256, 128), F32),
                pltpu.VMEM((N_TM, 8, SPAN), F32),
                pltpu.SMEM((CHUNKS + BATCH,), jnp.int32),
            ],
            compiler_params=PARAMS,
        )(*refs, parts)
    with jax.named_scope("gather_src"):
        parts = lax.all_to_all(parts, "src", 0, 0)
    with jax.named_scope("gather"):
        parts = pl.pallas_call(
            gather_kernel,
            out_shape=jax.ShapeDtypeStruct((8 * TILES, 128), F32),
            in_specs=[VMEM_SPEC],
            out_specs=VMEM_SPEC,
            compiler_params=PARAMS,
        )(parts)
    with jax.named_scope("gather_z"):
        mine = pl.pallas_call(
            stack_kernel,
            out_shape=jax.ShapeDtypeStruct((4, 8 * TILES, 128), F32),
            in_specs=[VMEM_SPEC] * 4,
            out_specs=VMEM_SPEC,
            compiler_params=PARAMS,
        )(parts, *[along_z(parts, d) for d in (1, 2, 3)])
    with jax.named_scope("gather_core"):
        other = to_other_core(mine)
    tables = [jnp.asarray(table) for table in filter_tables()]
    with jax.named_scope("solve"):
        new_coeffs = pl.pallas_call(
            solve_kernel,
            out_shape=jax.ShapeDtypeStruct((4, K), F32),
            in_specs=[SMEM_SPEC] + [VMEM_SPEC] * 5,
            out_specs=VMEM_SPEC,
            scratch_shapes=[
                pltpu.VMEM((44, 72, 128), F32),
                pltpu.VMEM((4, 64, 128), F32),
                pltpu.VMEM((4, 80, 128), F32),
                pltpu.VMEM((3, 4, 64, 128), F32),
                pltpu.VMEM((3, 4, 64, 128), F32),
                pltpu.VMEM((4, 64, 128), F32),
                pltpu.VMEM((4, 64, 128), F32),
                pltpu.VMEM((4, 64, 128), F32),
                pltpu.VMEM((4, 64, 128), F32),
                pltpu.VMEM((4, 64, 128), F32),
                pltpu.VMEM((4, 80, 128), F32),
            ],
            compiler_params=PARAMS,
        )(place, mine, other, coeffs, *tables)
    return (new_coeffs, calibration_step)


def solution(mesh):
    placed = (
        P(("src", "tm")),
        P(("src", "tm"), None),
        P(("src", "tm")),
        P(None, ("src", "tm")),
        P(("src", "tm")),
        P(("src", "tm")),
        P(("src", "tm")),
        P(("src", "tm")),
        P(None, "tm"),
    )
    return jax.shard_map(
        local, mesh=mesh, in_specs=placed, out_specs=(P(None, "tm"), P()), check_vma=False
    )
```

```python
import jax
import jax.numpy as jnp
import ml_dtypes
import numpy as np
from jax import lax
from jax.experimental import pallas as pl
from jax.experimental.pallas import tpu as pltpu
from jax.sharding import PartitionSpec as P

K = 1024
OBS_DEV = 8192
NCAL = 512
ITERS = 6
N_SRC = 16
N_TM = 8
NK = K * N_TM
CAP = 2 * OBS_DEV // N_TM
ATTITUDE_PRIOR = 1.0
FILTER_GAIN = 0.05
CHUNK = 512
PART, BATCH = 2, 4
UNROLL = 8
HIGHEST = lax.Precision.HIGHEST
F32 = jnp.float32
BF16 = jnp.bfloat16
VMEM_LIMIT = 48 * 1024 * 1024

PAIRS = [(a, b) for a in range(4) for b in range(a, 4)]
PAIR_AT = {pair: i for i, pair in enumerate(PAIRS)}
PAIR_AT.update({(b, a): i for (a, b), i in list(PAIR_AT.items())})
SPILL, SIDE, TILES = 40, 41, 45
MORE, SPAN = CAP, CAP + CHUNK
WIDTH = 2 * SPAN + 384
MOMENTS = 72
BINOMIAL = [1.0, 6.0, 15.0, 20.0, 15.0, 6.0, 1.0]


def halves(table):
    high = table.astype(ml_dtypes.bfloat16)
    return high, (table - high.astype(np.float64)).astype(ml_dtypes.bfloat16)


def select_rows():
    cubic = np.array([[1, 0, 0, 0], [4, 4, 2, 1], [1, 2, 4, 4], [0, 0, 0, 1]]) / 6.0
    scaled = cubic * np.array([1.0, 3.0, 3.0, 1.0])
    table = np.zeros((4, 40, 2 * MOMENTS))
    for a in range(4):
        for lag in range(4 - a):
            share = np.convolve(scaled[a], scaled[a + lag]) / np.array(BINOMIAL)
            for pair in range(10):
                for n in range(7):
                    row = 8 * n + pair if pair < 8 else 56 + 8 * (pair - 8) + n
                    table[a, 10 * lag + pair, row] = share[n]
                    table[a, 10 * lag + pair, MOMENTS + row] = share[n]
    high, low = halves(table.reshape(160, 2 * MOMENTS))
    return np.concatenate([high, high, low], axis=1)


def filter_tables():
    rate = 0.1 ** (1.0 / NK)
    gain = FILTER_GAIN * (1.0 - rate) ** 2 / (1.0 - rate * rate)
    lane = np.arange(128.0)
    row = np.arange(64.0)
    near = rate ** np.abs(lane[:, None] - lane[None, :])
    from_left = np.outer(rate ** (127 - lane), rate ** (lane + 1))
    from_right = np.outer(rate**lane, rate ** (128 - lane))
    edge = np.outer(rate ** (127 - lane), rate ** (128 - lane))
    within = gain * np.concatenate([near, from_left, from_right, edge], axis=1)
    gap = row[:, None] - row[None, :]
    left = np.where(gap > 0, rate ** (128 * np.maximum(gap - 1, 0)), 0.0)
    right = np.where(gap < 0, rate ** (128 * np.maximum(-gap - 1, 0)), 0.0)
    closing = -np.outer(rate ** (NK - 128 * row - 128), rate ** (NK - 128 * row - 127))
    across = np.concatenate([left, right, closing], axis=1)
    (near_high, near_low), (far_high, far_low) = halves(within), halves(across)
    return (
        np.concatenate([near_high, near_high, near_low], axis=0),
        np.concatenate([far_high, far_high, far_low], axis=1),
    )


def split_two(value):
    high = value.astype(BF16).astype(F32)
    return jnp.concatenate([high, value - high], axis=0).astype(BF16)


def spread(value, u, rows=8):
    return jnp.broadcast_to(value[u : u + 1, :], (rows, value.shape[1]))


def sixteen(row):
    return jnp.broadcast_to(row, (16, row.shape[1])).astype(BF16)


def hot_lanes(low, count):
    low = sixteen(low)
    want = lax.broadcasted_iota(jnp.int32, low.shape, 0).astype(F32).astype(BF16)
    one, zero = jnp.ones_like(low), jnp.zeros_like(low)
    return jnp.concatenate(
        [jnp.where(low == want + BF16(16 * j), one, zero) for j in range(count // 16)], axis=0
    )


def grouped(rows, group, count):
    parts = []
    for g in range(count):
        mask = sixteen(jnp.where(group == float(g), 1.0, 0.0))
        parts.append(rows * jnp.concatenate([mask] * (rows.shape[0] // 16), axis=0))
    return jnp.concatenate(parts, axis=0)


def outer(rows, hot):
    return lax.dot_general(rows, hot, (((1,), (1,)), ((), ())), preferred_element_type=F32)


def window_kernel(
    place_ref, counts_ref, cal_hbm, weight_hbm, across_hbm, resid_hbm, knot_hbm, phase_hbm, partial_hbm,
    near_hbm, one_hbm, two_hbm, three_hbm, cal_ref, weight_ref, across_ref, resid_ref, knot_ref, phase_ref, partial_ref,
    table, more, window, begins, sems, out_sems,
):
    pairs = [
        (cal_hbm, cal_ref), (weight_hbm, weight_ref), (across_hbm, across_ref), (resid_hbm, resid_ref),
        (knot_hbm, knot_ref), (phase_hbm, phase_ref), (partial_hbm, partial_ref),
    ]
    copies = [pltpu.make_async_copy(a, b, sems.at[i]) for i, (a, b) in enumerate(pairs)]
    for copy in copies:
        copy.start()
    sub = lax.broadcasted_iota(jnp.int32, (8, 128), 0)
    lane = lax.broadcasted_iota(jnp.int32, (8, 128), 1)
    quarter = sub & 3
    upper = sub < 4
    for copy in copies[:4]:
        copy.wait()

    def step(i, total):
        tiles, hots = [], []
        for part in range(UNROLL):
            rows = pl.ds(pl.multiple_of(8 * UNROLL * i + 8 * part, 8), 8)
            ids, weight = cal_ref[rows, :], weight_ref[rows, :]
            shift, resid = across_ref[rows, :], resid_ref[rows, :]
            low, high = (ids & 127).astype(F32), ids >> 7
            weighted = weight * shift
            second = weighted * shift
            third = weight * resid
            fourth = weighted * resid
            for u in range(8):
                mask = spread(high, u) == quarter

                def pick(top, bottom):
                    return jnp.where(mask, jnp.where(upper, spread(top, u), spread(bottom, u)), 0.0)

                last = jnp.where(mask & upper, spread(fourth, u), 0.0)
                tiles.append(jnp.concatenate([pick(weight, weighted), pick(second, third), last], axis=0))
                hots.append(hot_lanes(low[u : u + 1, :], 128))
        return total + outer(split_two(jnp.concatenate(tiles, axis=1)), jnp.concatenate(hots, axis=1))

    total = lax.fori_loop(0, 8 // UNROLL, step, jnp.zeros((48, 128), F32))
    total = total[:24] + total[24:]
    for copy in copies[4:]:
        copy.wait()

    def fill(i, carry):
        rows = pl.ds(pl.multiple_of(8 * i, 8), 8)
        knot, phase = knot_ref[rows, :].astype(F32), phase_ref[rows, :]
        weight, resid = weight_ref[rows, :], resid_ref[rows, :]
        shift, number = across_ref[rows, :], cal_ref[rows, :].astype(F32)
        for u in range(8):
            here = pl.ds(pl.multiple_of(1024 * i + 128 * u, 128), 128)
            table[4:8, here] = jnp.concatenate(
                [knot[u : u + 1], phase[u : u + 1], weight[u : u + 1], resid[u : u + 1]], axis=0
            )
            more[0:2, here] = jnp.concatenate([shift[u : u + 1], number[u : u + 1]], axis=0)
        lanes = pl.ds(pl.multiple_of(1024 * i, 1024), 1024)
        table[0:4, lanes] = partial_ref[:, lanes]
        return carry

    lax.fori_loop(0, 8, fill, 0)
    begin = jnp.int32(0)
    for block in range(N_TM):
        begins[block] = begin
        begin = begin + counts_ref[0, block]
    dead = jnp.where(sub == 4, -1.0, 0.0)
    core, place_z = place_ref[0] & 1, place_ref[0] >> 1
    sent = []
    for n in range(N_TM):
        d, half = (2, 1, 3, 0)[n // 2], n % 2
        start = SPAN * half
        out_hbm = (near_hbm, one_hbm, two_hbm, three_hbm)[d]
        block = 2 * ((place_z + d) & 3) + (1 - core if half else core)
        count, begin = counts_ref[0, block], begins[block]
        base = pl.multiple_of((begin >> 7) << 7, 128)
        off = begin & 127
        back = (128 - off) & 127
        early = lane < 128 - off
        rolled = pltpu.roll(table[:, pl.ds(base, 128)], back, 1)
        rolled_more = pltpu.roll(more[:, pl.ds(base, 128)], back, 1)
        for j in range(CAP // 128):
            here = pl.ds(base + 128 * (j + 1), 128)
            after = pltpu.roll(table[:, here], back, 1)
            after_more = pltpu.roll(more[:, here], back, 1)
            live = lane + 128 * j < count
            window[d, :, start + 128 * j : start + 128 * (j + 1)] = jnp.where(live, jnp.where(early, rolled, after), dead)
            tile = jnp.where(live, jnp.where(early, rolled_more, after_more), 0.0)
            row, lanes = j // 4, pl.ds(start + MORE + 128 * (j % 4), 128)
            window[d, row : row + 1, lanes] = tile[0:1]
            window[d, 4 + row : 5 + row, lanes] = tile[1:2]
            rolled, rolled_more = after, after_more
        if half:
            for k in range(3):
                at = 2 * SPAN + 128 * k
                window[d, :, at : at + 128] = total[8 * k : 8 * k + 8]
            sent.append(pltpu.make_async_copy(window.at[d], out_hbm, out_sems.at[d]))
            sent[-1].start()
    for copy in sent:
        copy.wait()


def each_batch(windows_ref, order, size, body):
    found = jnp.int32(0)
    for block in range(windows_ref.shape[0]):
        count = jnp.sum((windows_ref[block, 4:5, :CAP] >= 0.0).astype(jnp.int32))
        for i in range(CAP // CHUNK):
            order[found] = 4 * block + i
            found = found + (count > i * CHUNK).astype(jnp.int32)
    for u in range(size - 1):
        order[found + u] = 0

    def step(batch, carry):
        chunks = []
        for u in range(size):
            at = order[size * batch + u]
            block, i = at >> 2, at & 3
            tile = windows_ref[block, :, pl.ds(pl.multiple_of(i * CHUNK, CHUNK), CHUNK)]
            knot = jnp.where(size * batch + u < found, tile[4:5], -1.0)
            chunks.append((tile, knot, block, i))
        body(chunks)
        return carry

    lax.fori_loop(0, (found + size - 1) // size, step, 0)


def spline_basis(phase):
    square = phase * phase
    cube = square * phase
    remain = 1.0 - phase
    return [
        remain * remain * remain * (1.0 / 6.0),
        (3.0 * cube - 6.0 * square + 4.0) * (1.0 / 6.0),
        (-3.0 * cube + 3.0 * square + 3.0 * phase + 1.0) * (1.0 / 6.0),
        cube * (1.0 / 6.0),
    ]


def add_moments(windows_ref, total, order, size):
    def work(tile, knot):
        part = [tile[c : c + 1] for c in range(4)]
        phase, weight = tile[5:6], tile[6:7]
        remain = 1.0 - phase
        powers, others = [jnp.ones_like(phase), phase], [jnp.ones_like(phase), remain]
        for n in range(2, 7):
            powers.append(powers[n // 2] * powers[n - n // 2])
            others.append(others[n // 2] * others[n - n // 2])
        order = [weight * (BINOMIAL[n] * (powers[n] * others[6 - n])) for n in range(7)]
        left = jnp.concatenate([part[c] for c, e in PAIRS[:8]], axis=0)
        right = jnp.concatenate([part[e] for c, e in PAIRS[:8]], axis=0)
        eight = left * right
        rows = [order[n] * eight for n in range(7)]
        stack = jnp.concatenate(order + [jnp.zeros_like(phase)], axis=0)
        rows.append(stack * (part[2] * part[3]))
        rows.append(stack * (part[3] * part[3]))
        rows = split_two(jnp.concatenate(rows, axis=0))
        group = jnp.floor(knot * (1.0 / 256.0))
        low = jnp.maximum(knot, 0.0) - 256.0 * jnp.maximum(group, 0.0)
        return grouped(rows, group, 4), hot_lanes(low, 256)

    def body(chunks):
        rows, hots = zip(*[work(tile, knot) for tile, knot, block, i in chunks])
        total[...] += outer(jnp.concatenate(rows, axis=1), jnp.concatenate(hots, axis=1))

    each_batch(windows_ref, order, size, body)


def join(here_ref, there_ref, windows_ref, at=0):
    windows_ref[at] = here_ref[:, 0:SPAN]
    windows_ref[at + 1] = there_ref[:, SPAN : 2 * SPAN]


def first_kernel(here_hbm, there_ref, total, windows_ref, order, sem):
    copy = pltpu.make_async_copy(here_hbm.at[:, pl.ds(0, SPAN)], windows_ref.at[0], sem)
    copy.start()
    total[...] = jnp.zeros_like(total)
    windows_ref[1] = there_ref[:, SPAN : 2 * SPAN]
    copy.wait()
    add_moments(windows_ref, total, order, PART)


def next_kernel(before_ref, one_ref, one_there_ref, three_ref, three_there_ref, total, windows_ref, order):
    total[...] = before_ref[...]
    join(one_ref, one_there_ref, windows_ref)
    join(three_ref, three_there_ref, windows_ref, 2)
    add_moments(windows_ref, total, order, BATCH)


def last_kernel(before_ref, *refs):
    pairs, (select_ref, out_ref, total, tiles, windows_ref, order) = refs[:8], refs[8:]
    total[...] = before_ref[...]
    join(pairs[4], pairs[5], windows_ref)
    add_moments(windows_ref, total, order, PART)
    parts = []
    for g in range(4):
        group = total[2 * MOMENTS * g : 2 * MOMENTS * (g + 1)]
        high = group.astype(BF16)
        low = (group - high.astype(F32)).astype(BF16)
        parts.append(
            jnp.dot(
                select_ref[...], jnp.concatenate([high, low, high], axis=0), preferred_element_type=F32
            )
        )
    parts.append(jnp.zeros((160, 128), F32))
    orders = jnp.concatenate(parts, axis=1)
    band = orders[0:40]
    for a in range(1, 4):
        band = band + pltpu.roll(orders[40 * a : 40 * a + 40], a, 1)
    for q in range(8):
        tiles[0:40, q, :] = band[:, 128 * q : 128 * (q + 1)]
    spill = band[:, K : K + 128]
    packed = spill[0:8]
    for g in range(1, 5):
        packed = packed + pltpu.roll(spill[8 * g : 8 * g + 8], 8 * g, 1)
    tiles[SPILL] = packed
    near, one, two, three = [
        pairs[2 * d][:, 2 * SPAN : WIDTH] + pairs[2 * d + 1][:, 2 * SPAN : WIDTH] for d in range(4)
    ]
    sums = (near + two) + (one + three)
    for s in range(N_SRC):
        for r in range(3):
            at = 3 * s + r
            out_ref[s, 8 * r : 8 * r + 8, :] = tiles[at] if at <= SPILL else jnp.zeros((8, 128), F32)
            out_ref[s, 24 + 8 * r : 32 + 8 * r, :] = sums[:, 128 * r : 128 * (r + 1)]


def side_kernel(*refs):
    pairs, (parts_ref, out_ref, step_ref, total, windows_ref, order) = refs[:8], refs[8:]
    total[...] = jnp.zeros_like(total)
    for d in range(4):
        join(pairs[2 * d], pairs[2 * d + 1], windows_ref, 2 * d)
    both = parts_ref[0]
    for s in range(1, N_SRC):
        both = both + parts_ref[s]
    prior = float(OBS_DEV * N_SRC * N_TM // NCAL)
    totals = both[24:48]
    zero_moment = totals[0:4] + prior
    first = totals[4:8]
    second_moment = totals[8:12] + prior
    third, fourth = totals[12:16], totals[16:20]
    det = zero_moment * second_moment - first * first
    offset = (second_moment * third - first * fourth) / det
    slope = (zero_moment * fourth - first * third) / det
    for h in range(4):
        step_ref[0:1, 128 * h : 128 * (h + 1)] = offset[h : h + 1]
        step_ref[1:2, 128 * h : 128 * (h + 1)] = slope[h : h + 1]
    steps = jnp.concatenate([offset, slope], axis=0)
    sub = lax.broadcasted_iota(jnp.int32, (8, CHUNK), 0)
    quarter = (sub & 3).astype(F32)
    upper = sub < 4

    def work(tile, knot, block, i):
        shift = windows_ref[block, pl.ds(i, 1), MORE:SPAN]
        ids = windows_ref[block, pl.ds(4 + i, 1), MORE:SPAN]
        phase, weight, resid = tile[5:6], tile[6:7], tile[7:8]
        high = jnp.floor(ids * (1.0 / 128.0))
        low = jnp.broadcast_to((ids - 128.0 * high).astype(jnp.int32), (8, CHUNK))
        found = jnp.concatenate(
            [jnp.take_along_axis(steps, low[:, 128 * k : 128 * (k + 1)], axis=1) for k in range(CHUNK // 128)],
            axis=1,
        )
        found = jnp.where(quarter == high, found, 0.0) * jnp.where(upper, 1.0, shift)
        corrected = resid - jnp.sum(found, axis=0, keepdims=True)
        basis = spline_basis(phase)
        four = tile[0:4] * (weight * corrected)
        double = jnp.concatenate([four, four], axis=0)
        rows = []
        for a in (0, 2):
            order = jnp.concatenate([basis[a]] * 4 + [basis[a + 1]] * 4, axis=0)
            rows.append(double * order)
        rows = split_two(jnp.concatenate(rows, axis=0))
        group = jnp.floor(knot * (1.0 / 128.0))
        low = jnp.maximum(knot, 0.0) - 128.0 * jnp.maximum(group, 0.0)
        return grouped(rows, group, 8), hot_lanes(low, 128)

    def body(chunks):
        rows, hots = zip(*[work(*chunk) for chunk in chunks])
        total[...] += outer(jnp.concatenate(rows, axis=1), jnp.concatenate(hots, axis=1))

    each_batch(windows_ref, order, BATCH, body)
    orders = [total[32 * g : 32 * g + 16] + total[32 * g + 16 : 32 * g + 32] for g in range(8)]
    orders = jnp.concatenate(orders + [jnp.zeros((16, 128), F32)], axis=1)
    side = orders[0:4]
    for a in range(1, 4):
        side = side + pltpu.roll(orders, a, 1)[4 * a : 4 * a + 4]
    share = both[0:24]
    spill = jnp.concatenate([side[:, K : K + 128], jnp.zeros((4, 128), F32)], axis=0)
    rows = [share]
    for c in range(4):
        rows += [side[c : c + 1, 128 * q : 128 * (q + 1)] for q in range(8)]
    rows = jnp.concatenate(rows + [spill], axis=0)
    for s in range(N_SRC):
        out_ref[s] = rows


def gather_kernel(parts_ref, out_ref):
    side = parts_ref[0, 24:64, :]
    for s in range(1, N_SRC):
        side = side + parts_ref[s, 24:64, :]
    spill = pltpu.roll(side[32:40], SPILL, 1) + parts_ref[SPILL // 3, 8 * (SPILL % 3) : 8 * (SPILL % 3) + 8, :]
    for i in range(40):
        out_ref[8 * i : 8 * i + 8, :] = parts_ref[i // 3, 8 * (i % 3) : 8 * (i % 3) + 8, :]
    out_ref[8 * SPILL : 8 * SPILL + 8, :] = spill
    out_ref[8 * SIDE : 8 * TILES, :] = side[0:32]


def stack_kernel(first_ref, second_ref, third_ref, fourth_ref, out_ref):
    for d, ref in enumerate((first_ref, second_ref, third_ref, fourth_ref)):
        out_ref[d] = ref[...]


def solve_kernel(
    place_ref, mine_ref, other_ref, coeffs_ref, within_ref, across_ref, out_ref,
    band, inverse, field, ahead, lower, applied, resid, delta, filtered, smooth, spare, direction, along,
):
    lane8 = lax.broadcasted_iota(jnp.int32, (8, 128), 1)
    lane = lax.broadcasted_iota(jnp.int32, (64, 128), 1)
    core, place_z = place_ref[0] & 1, place_ref[0] >> 1
    halves = ((mine_ref, core), (other_ref, 1 - core))
    for ref, parity in halves:
        for d in range(4):
            rows = pl.ds(pl.multiple_of(8 * (2 * ((place_z - d) & 3) + parity), 8), 8)
            for i in range(44):
                at = i if i < 40 else SIDE + i - 40
                band[i, rows, :] = ref[d, 8 * at : 8 * at + 8, :]
    for ref, parity in halves:
        for d in range(4):
            row = pl.ds(pl.multiple_of(8 * (2 * ((place_z - d) & 3) + parity) + 8, 8), 1)
            packed = ref[d, 8 * SPILL : 8 * SPILL + 8, :]
            for g in range(6):
                moved = packed if g == 0 else pltpu.roll(packed, 128 - 8 * g, 1)
                moved = jnp.where(lane8 < 3, moved, 0.0)
                for u in range(min(8, 44 - 8 * g)):
                    band[8 * g + u, row, :] += moved[u : u + 1]
    for c in range(4):
        inverse[c] = 1.0 / (ATTITUDE_PRIOR + band[PAIR_AT[(c, c)], 0:64, :])
    field[...] = jnp.zeros_like(field)
    spare[...] = jnp.zeros_like(spare)

    def total_of(left, right):
        value = left * right
        value = jnp.sum(value.reshape(32, 8, 128), axis=0)
        return jnp.sum(jnp.sum(value, axis=0, keepdims=True), axis=1, keepdims=True)

    def precondition(source):
        res = source[...].reshape(256, 128)
        high = res.astype(BF16)
        low = (res - high.astype(F32)).astype(BF16)
        spreads = jnp.dot(
            jnp.concatenate([high, low, high], axis=1), within_ref[...], preferred_element_type=F32
        )
        for c in range(4):
            own = spreads[64 * c : 64 * c + 64]
            carried = jnp.concatenate([own[:, 128:256], own[:, 256:384], own[:, 384:512]], axis=0)
            high = carried.astype(BF16)
            low = (carried - high.astype(F32)).astype(BF16)
            carry = jnp.dot(
                across_ref[...], jnp.concatenate([high, low, high], axis=0), preferred_element_type=F32
            )
            filtered[c] = source[c] * inverse[c] + own[:, :128] + carry

    def apply_normals():
        for e in range(4):
            here, after = field[e, 8:72, :], field[e, 9:73, :]
            for d in range(1, 4):
                ahead[d - 1, e] = pltpu.roll(jnp.where(lane < d, after, here), 128 - d, 1)
        for t in range(N_TM):
            rows = slice(8 * t, 8 * t + 8)
            padded = slice(8 * t + 8, 8 * t + 16)
            own = [field[e, padded, :] for e in range(4)]
            sums = [own[c] * ATTITUDE_PRIOR for c in range(4)]
            for d in range(4):
                near = own if d == 0 else [ahead[d - 1, e, rows, :] for e in range(4)]
                tiles = [band[10 * d + i, rows, :] for i in range(10)]
                for c in range(4):
                    for e in range(4):
                        sums[c] = sums[c] + tiles[PAIR_AT[(c, e)]] * near[e]
                if d:
                    for c in range(4):
                        back = tiles[PAIR_AT[(c, 0)]] * own[0]
                        for e in range(1, 4):
                            back = back + tiles[PAIR_AT[(c, e)]] * own[e]
                        lower[d - 1, c, rows, :] = back
            for c in range(4):
                applied[c, rows, :] = sums[c]
        for c in range(4):
            result = applied[c]
            wrapped = jnp.zeros((64, 128), F32)
            for d in range(1, 4):
                moved = pltpu.roll(lower[d - 1, c], d, 1)
                result = result + jnp.where(lane >= d, moved, 0.0)
                wrapped = wrapped + jnp.where(lane < d, moved, 0.0)
            spare[c, 8:72, :] = wrapped
            applied[c] = result + spare[c, 7:71, :]

    resid[...] = band[40:44, 0:64, :]
    precondition(resid)
    field[:, 8:72, :] = filtered[...]
    delta[...] = jnp.zeros_like(delta)
    energy = total_of(resid[...], filtered[...])
    for i in range(ITERS):
        apply_normals()
        if i < ITERS - 1:
            precondition(applied)
        if i == 0:
            toward, image, smooth_image = field[:, 8:72, :], applied[...], filtered[...]
        else:
            toward = field[:, 8:72, :] + ratio * direction[...]
            image = applied[...] + ratio * along[...]
            smooth_image = filtered[...] + ratio * smooth[...]
        step = energy / total_of(toward, image)
        delta[...] += step * toward
        if i < ITERS - 1:
            direction[...], along[...], smooth[...] = toward, image, smooth_image
            rest = resid[...] - step * image
            after = field[:, 8:72, :] - step * smooth_image
            resid[...] = rest
            field[:, 8:72, :] = after
            fresh = total_of(rest, after)
            ratio, energy = fresh / energy, fresh
    mine = pl.ds(pl.multiple_of(place_ref[0] * 8, 8), 8)
    for c in range(4):
        tile = delta[c, mine, :]
        for q in range(8):
            lanes = slice(128 * q, 128 * q + 128)
            out_ref[c : c + 1, lanes] = coeffs_ref[c : c + 1, lanes] + tile[q : q + 1]


VMEM_SPEC = pl.BlockSpec(memory_space=pltpu.VMEM)
SMEM_SPEC = pl.BlockSpec(memory_space=pltpu.SMEM)
HBM_SPEC = pl.BlockSpec(memory_space=pltpu.HBM)
PARAMS = pltpu.CompilerParams(vmem_limit_bytes=VMEM_LIMIT)
CHUNKS = N_TM * CAP // CHUNK


def to_other_core(value):
    return lax.ppermute(value, "tm", [(i, i ^ 1) for i in range(N_TM)])


def along_z(value, d):
    return lax.ppermute(value, "tm", [(i, (i + 2 * d) % N_TM) for i in range(N_TM)])


def cost(microseconds):
    return pl.CostEstimate(
        flops=int(microseconds * 1_000_000_000), bytes_accessed=1_000_000, transcendentals=0
    )


def local(
    knot_index, block_counts, knot_phase, partials, obs_weight, residuals, cal_id, across, coeffs
):
    dense = [
        value.reshape(64, 128)
        for value in (cal_id, obs_weight, across, residuals, knot_index, knot_phase)
    ]
    place = lax.axis_index("tm").reshape(1)
    with jax.named_scope("windows"):
        windows = pl.pallas_call(
            window_kernel,
            out_shape=(jax.ShapeDtypeStruct((8, WIDTH), F32),) * 4,
            in_specs=[SMEM_SPEC] * 2 + [HBM_SPEC] * 7,
            out_specs=(HBM_SPEC,) * 4,
            scratch_shapes=[pltpu.VMEM((64, 128), value.dtype) for value in dense]
            + [
                pltpu.VMEM((4, OBS_DEV), F32),
                pltpu.VMEM((8, OBS_DEV + CAP + 128), F32),
                pltpu.VMEM((8, OBS_DEV + CAP + 128), F32),
                pltpu.VMEM((4, 8, WIDTH), F32),
                pltpu.SMEM((N_TM,), jnp.int32),
                pltpu.SemaphoreType.DMA((7,)),
                pltpu.SemaphoreType.DMA((4,)),
            ],
            compiler_params=pltpu.CompilerParams(vmem_limit_bytes=56 * 1024 * 1024),
        )(place, block_counts, *dense, partials)
    with jax.named_scope("to_owners"):
        windows = [windows[0]] + [along_z(windows[d], d) for d in (1, 2, 3)]
        near = (windows[0], to_other_core(windows[0]))
    with jax.named_scope("moments"):
        total = jax.ShapeDtypeStruct((8 * MOMENTS, 256), F32)
        scratch = [pltpu.VMEM((2, 8, SPAN), F32), pltpu.SMEM((CHUNKS,), jnp.int32)]
        moments = pl.pallas_call(
            first_kernel,
            out_shape=total,
            in_specs=[HBM_SPEC, VMEM_SPEC],
            out_specs=VMEM_SPEC,
            scratch_shapes=[*scratch, pltpu.SemaphoreType.DMA],
            compiler_params=PARAMS,
            cost_estimate=cost(2),
        )(*near)
        moments, one = lax.optimization_barrier((moments, windows[1]))
        moments, three = lax.optimization_barrier((moments, windows[3]))
        pairs = [near] + [(here, to_other_core(here)) for here in (one, windows[2], three)]
        moments = pl.pallas_call(
            next_kernel,
            out_shape=total,
            in_specs=[VMEM_SPEC] * 5,
            out_specs=VMEM_SPEC,
            scratch_shapes=[pltpu.VMEM((4, 8, SPAN), F32), pltpu.SMEM((CHUNKS,), jnp.int32)],
            compiler_params=PARAMS,
            cost_estimate=cost(2),
        )(moments, *pairs[1], *pairs[3])
        refs = [ref for pair in pairs for ref in pair]
        parts = pl.pallas_call(
            last_kernel,
            out_shape=jax.ShapeDtypeStruct((N_SRC, 48, 128), F32),
            in_specs=[VMEM_SPEC] * 10,
            out_specs=VMEM_SPEC,
            scratch_shapes=[
                pltpu.VMEM((8 * MOMENTS, 256), F32),
                pltpu.VMEM((SPILL + 1, 8, 128), F32),
                *scratch,
            ],
            compiler_params=PARAMS,
        )(moments, *refs, jnp.asarray(select_rows()))
    with jax.named_scope("band_reduce"):
        parts = lax.all_to_all(parts, "src", 0, 0)
    with jax.named_scope("side"):
        parts, calibration_step = pl.pallas_call(
            side_kernel,
            out_shape=(
                jax.ShapeDtypeStruct((N_SRC, 64, 128), F32),
                jax.ShapeDtypeStruct((2, NCAL), F32),
            ),
            in_specs=[VMEM_SPEC] * 9,
            out_specs=(VMEM_SPEC, VMEM_SPEC),
            scratch_shapes=[
                pltpu.VMEM((256, 128), F32),
                pltpu.VMEM((N_TM, 8, SPAN), F32),
                pltpu.SMEM((CHUNKS + BATCH,), jnp.int32),
            ],
            compiler_params=PARAMS,
        )(*refs, parts)
    with jax.named_scope("gather_src"):
        parts = lax.all_to_all(parts, "src", 0, 0)
    with jax.named_scope("gather"):
        parts = pl.pallas_call(
            gather_kernel,
            out_shape=jax.ShapeDtypeStruct((8 * TILES, 128), F32),
            in_specs=[VMEM_SPEC],
            out_specs=VMEM_SPEC,
            compiler_params=PARAMS,
        )(parts)
    with jax.named_scope("gather_z"):
        mine = pl.pallas_call(
            stack_kernel,
            out_shape=jax.ShapeDtypeStruct((4, 8 * TILES, 128), F32),
            in_specs=[VMEM_SPEC] * 4,
            out_specs=VMEM_SPEC,
            compiler_params=PARAMS,
        )(parts, *[along_z(parts, d) for d in (1, 2, 3)])
    with jax.named_scope("gather_core"):
        other = to_other_core(mine)
    tables = [jnp.asarray(table) for table in filter_tables()]
    with jax.named_scope("solve"):
        new_coeffs = pl.pallas_call(
            solve_kernel,
            out_shape=jax.ShapeDtypeStruct((4, K), F32),
            in_specs=[SMEM_SPEC] + [VMEM_SPEC] * 5,
            out_specs=VMEM_SPEC,
            scratch_shapes=[
                pltpu.VMEM((44, 72, 128), F32),
                pltpu.VMEM((4, 64, 128), F32),
                pltpu.VMEM((4, 80, 128), F32),
                pltpu.VMEM((3, 4, 64, 128), F32),
                pltpu.VMEM((3, 4, 64, 128), F32),
                pltpu.VMEM((4, 64, 128), F32),
                pltpu.VMEM((4, 64, 128), F32),
                pltpu.VMEM((4, 64, 128), F32),
                pltpu.VMEM((4, 64, 128), F32),
                pltpu.VMEM((4, 64, 128), F32),
                pltpu.VMEM((4, 80, 128), F32),
                pltpu.VMEM((4, 64, 128), F32),
                pltpu.VMEM((4, 64, 128), F32),
            ],
            compiler_params=PARAMS,
        )(place, mine, other, coeffs, *tables)
    return (new_coeffs, calibration_step)


def solution(mesh):
    placed = (
        P(("src", "tm")),
        P(("src", "tm"), None),
        P(("src", "tm")),
        P(None, ("src", "tm")),
        P(("src", "tm")),
        P(("src", "tm")),
        P(("src", "tm")),
        P(("src", "tm")),
        P(None, "tm"),
    )
    return jax.shard_map(
        local, mesh=mesh, in_specs=placed, out_specs=(P(None, "tm"), P()), check_vma=False
    )
```

```python
import jax
import jax.numpy as jnp
import ml_dtypes
import numpy as np
from jax import lax
from jax.experimental import pallas as pl
from jax.experimental.pallas import tpu as pltpu
from jax.sharding import PartitionSpec as P

K = 1024
OBS_DEV = 8192
NCAL = 512
ITERS = 6
N_SRC = 16
N_TM = 8
NK = K * N_TM
CAP = 2 * OBS_DEV // N_TM
ATTITUDE_PRIOR = 1.0
FILTER_GAIN = 0.05
CHUNK = 512
PART, BATCH = 2, 4
UNROLL = 8
HIGHEST = lax.Precision.HIGHEST
F32 = jnp.float32
BF16 = jnp.bfloat16
VMEM_LIMIT = 48 * 1024 * 1024

PAIRS = [(a, b) for a in range(4) for b in range(a, 4)]
PAIR_AT = {pair: i for i, pair in enumerate(PAIRS)}
PAIR_AT.update({(b, a): i for (a, b), i in list(PAIR_AT.items())})
SPILL, SIDE, TILES = 40, 41, 45
SHARE = 21
MORE, SPAN = CAP, CAP + CHUNK
WIDTH = 2 * SPAN + 384
MOMENTS = 72
BINOMIAL = [1.0, 6.0, 15.0, 20.0, 15.0, 6.0, 1.0]


def halves(table):
    high = table.astype(ml_dtypes.bfloat16)
    return high, (table - high.astype(np.float64)).astype(ml_dtypes.bfloat16)


def select_rows():
    cubic = np.array([[1, 0, 0, 0], [4, 4, 2, 1], [1, 2, 4, 4], [0, 0, 0, 1]]) / 6.0
    scaled = cubic * np.array([1.0, 3.0, 3.0, 1.0])
    table = np.zeros((4, 40, 2 * MOMENTS))
    for a in range(4):
        for lag in range(4 - a):
            share = np.convolve(scaled[a], scaled[a + lag]) / np.array(BINOMIAL)
            for pair in range(10):
                for n in range(7):
                    row = 8 * n + pair if pair < 8 else 56 + 8 * (pair - 8) + n
                    table[a, 10 * lag + pair, row] = share[n]
                    table[a, 10 * lag + pair, MOMENTS + row] = share[n]
    high, low = halves(table.reshape(160, 2 * MOMENTS))
    return np.concatenate([high, high, low], axis=1)


def filter_tables():
    rate = 0.1 ** (1.0 / NK)
    gain = FILTER_GAIN * (1.0 - rate) ** 2 / (1.0 - rate * rate)
    lane = np.arange(128.0)
    row = np.arange(64.0)
    near = rate ** np.abs(lane[:, None] - lane[None, :])
    from_left = np.outer(rate ** (127 - lane), rate ** (lane + 1))
    from_right = np.outer(rate**lane, rate ** (128 - lane))
    edge = np.outer(rate ** (127 - lane), rate ** (128 - lane))
    within = gain * np.concatenate([near, from_left, from_right, edge], axis=1)
    gap = row[:, None] - row[None, :]
    left = np.where(gap > 0, rate ** (128 * np.maximum(gap - 1, 0)), 0.0)
    right = np.where(gap < 0, rate ** (128 * np.maximum(-gap - 1, 0)), 0.0)
    closing = -np.outer(rate ** (NK - 128 * row - 128), rate ** (NK - 128 * row - 127))
    across = np.concatenate([left, right, closing], axis=1)
    (near_high, near_low), (far_high, far_low) = halves(within), halves(across)
    return (
        np.concatenate([near_high, near_high, near_low], axis=0),
        np.concatenate([far_high, far_high, far_low], axis=1),
    )


def split_two(value):
    high = value.astype(BF16).astype(F32)
    return jnp.concatenate([high, value - high], axis=0).astype(BF16)


def spread(value, u, rows=8):
    return jnp.broadcast_to(value[u : u + 1, :], (rows, value.shape[1]))


def sixteen(row):
    return jnp.broadcast_to(row, (16, row.shape[1])).astype(BF16)


def hot_lanes(low, count):
    low = sixteen(low)
    want = lax.broadcasted_iota(jnp.int32, low.shape, 0).astype(F32).astype(BF16)
    one, zero = jnp.ones_like(low), jnp.zeros_like(low)
    return jnp.concatenate(
        [jnp.where(low == want + BF16(16 * j), one, zero) for j in range(count // 16)], axis=0
    )


def grouped(rows, group, count):
    parts = []
    for g in range(count):
        mask = sixteen(jnp.where(group == float(g), 1.0, 0.0))
        parts.append(rows * jnp.concatenate([mask] * (rows.shape[0] // 16), axis=0))
    return jnp.concatenate(parts, axis=0)


def outer(rows, hot):
    return lax.dot_general(rows, hot, (((1,), (1,)), ((), ())), preferred_element_type=F32)


def window_kernel(
    place_ref, counts_ref, cal_hbm, weight_hbm, across_hbm, resid_hbm, knot_hbm, phase_hbm, partial_hbm,
    near_hbm, one_hbm, two_hbm, three_hbm, cal_ref, weight_ref, across_ref, resid_ref, knot_ref, phase_ref, partial_ref,
    table, more, window, begins, sems, out_sems,
):
    pairs = [
        (cal_hbm, cal_ref), (weight_hbm, weight_ref), (across_hbm, across_ref), (resid_hbm, resid_ref),
        (knot_hbm, knot_ref), (phase_hbm, phase_ref), (partial_hbm, partial_ref),
    ]
    copies = [pltpu.make_async_copy(a, b, sems.at[i]) for i, (a, b) in enumerate(pairs)]
    for copy in copies:
        copy.start()
    sub = lax.broadcasted_iota(jnp.int32, (8, 128), 0)
    lane = lax.broadcasted_iota(jnp.int32, (8, 128), 1)
    quarter = sub & 3
    upper = sub < 4
    for copy in copies[:4]:
        copy.wait()

    def step(i, total):
        tiles, hots = [], []
        for part in range(UNROLL):
            rows = pl.ds(pl.multiple_of(8 * UNROLL * i + 8 * part, 8), 8)
            ids, weight = cal_ref[rows, :], weight_ref[rows, :]
            shift, resid = across_ref[rows, :], resid_ref[rows, :]
            low, high = (ids & 127).astype(F32), ids >> 7
            weighted = weight * shift
            second = weighted * shift
            third = weight * resid
            fourth = weighted * resid
            for u in range(8):
                mask = spread(high, u) == quarter

                def pick(top, bottom):
                    return jnp.where(mask, jnp.where(upper, spread(top, u), spread(bottom, u)), 0.0)

                last = jnp.where(mask & upper, spread(fourth, u), 0.0)
                tiles.append(jnp.concatenate([pick(weight, weighted), pick(second, third), last], axis=0))
                hots.append(hot_lanes(low[u : u + 1, :], 128))
        return total + outer(split_two(jnp.concatenate(tiles, axis=1)), jnp.concatenate(hots, axis=1))

    total = lax.fori_loop(0, 8 // UNROLL, step, jnp.zeros((48, 128), F32))
    total = total[:24] + total[24:]
    for copy in copies[4:]:
        copy.wait()

    def fill(i, carry):
        rows = pl.ds(pl.multiple_of(8 * i, 8), 8)
        knot, phase = knot_ref[rows, :].astype(F32), phase_ref[rows, :]
        weight, resid = weight_ref[rows, :], resid_ref[rows, :]
        shift, number = across_ref[rows, :], cal_ref[rows, :].astype(F32)
        for u in range(8):
            here = pl.ds(pl.multiple_of(1024 * i + 128 * u, 128), 128)
            table[4:8, here] = jnp.concatenate(
                [knot[u : u + 1], phase[u : u + 1], weight[u : u + 1], resid[u : u + 1]], axis=0
            )
            more[0:2, here] = jnp.concatenate([shift[u : u + 1], number[u : u + 1]], axis=0)
        lanes = pl.ds(pl.multiple_of(1024 * i, 1024), 1024)
        table[0:4, lanes] = partial_ref[:, lanes]
        return carry

    lax.fori_loop(0, 8, fill, 0)
    begin = jnp.int32(0)
    for block in range(N_TM):
        begins[block] = begin
        begin = begin + counts_ref[0, block]
    dead = jnp.where(sub == 4, -1.0, 0.0)
    core, place_z = place_ref[0] & 1, place_ref[0] >> 1
    sent = []
    for n in range(N_TM):
        d, half = (2, 1, 3, 0)[n // 2], n % 2
        start = SPAN * half
        out_hbm = (near_hbm, one_hbm, two_hbm, three_hbm)[d]
        block = 2 * ((place_z + d) & 3) + (1 - core if half else core)
        count, begin = counts_ref[0, block], begins[block]
        base = pl.multiple_of((begin >> 7) << 7, 128)
        off = begin & 127
        back = (128 - off) & 127
        early = lane < 128 - off
        rolled = pltpu.roll(table[:, pl.ds(base, 128)], back, 1)
        rolled_more = pltpu.roll(more[:, pl.ds(base, 128)], back, 1)
        for j in range(CAP // 128):
            here = pl.ds(base + 128 * (j + 1), 128)
            after = pltpu.roll(table[:, here], back, 1)
            after_more = pltpu.roll(more[:, here], back, 1)
            live = lane + 128 * j < count
            window[d, :, start + 128 * j : start + 128 * (j + 1)] = jnp.where(live, jnp.where(early, rolled, after), dead)
            tile = jnp.where(live, jnp.where(early, rolled_more, after_more), 0.0)
            row, lanes = j // 4, pl.ds(start + MORE + 128 * (j % 4), 128)
            window[d, row : row + 1, lanes] = tile[0:1]
            window[d, 4 + row : 5 + row, lanes] = tile[1:2]
            rolled, rolled_more = after, after_more
        if half:
            for k in range(3):
                at = 2 * SPAN + 128 * k
                window[d, :, at : at + 128] = total[8 * k : 8 * k + 8]
            sent.append(pltpu.make_async_copy(window.at[d], out_hbm, out_sems.at[d]))
            sent[-1].start()
    for copy in sent:
        copy.wait()


def each_batch(windows_ref, order, size, body):
    found = jnp.int32(0)
    for block in range(windows_ref.shape[0]):
        count = jnp.sum((windows_ref[block, 4:5, :CAP] >= 0.0).astype(jnp.int32))
        for i in range(CAP // CHUNK):
            order[found] = 4 * block + i
            found = found + (count > i * CHUNK).astype(jnp.int32)
    for u in range(size - 1):
        order[found + u] = 0

    def step(batch, carry):
        chunks = []
        for u in range(size):
            at = order[size * batch + u]
            block, i = at >> 2, at & 3
            tile = windows_ref[block, :, pl.ds(pl.multiple_of(i * CHUNK, CHUNK), CHUNK)]
            knot = jnp.where(size * batch + u < found, tile[4:5], -1.0)
            chunks.append((tile, knot, block, i))
        body(chunks)
        return carry

    lax.fori_loop(0, (found + size - 1) // size, step, 0)


def spline_basis(phase):
    square = phase * phase
    cube = square * phase
    remain = 1.0 - phase
    return [
        remain * remain * remain * (1.0 / 6.0),
        (3.0 * cube - 6.0 * square + 4.0) * (1.0 / 6.0),
        (-3.0 * cube + 3.0 * square + 3.0 * phase + 1.0) * (1.0 / 6.0),
        cube * (1.0 / 6.0),
    ]


def add_moments(windows_ref, total, order, size):
    def work(tile, knot):
        part = [tile[c : c + 1] for c in range(4)]
        phase, weight = tile[5:6], tile[6:7]
        remain = 1.0 - phase
        powers, others = [jnp.ones_like(phase), phase], [jnp.ones_like(phase), remain]
        for n in range(2, 7):
            powers.append(powers[n // 2] * powers[n - n // 2])
            others.append(others[n // 2] * others[n - n // 2])
        order = [weight * (BINOMIAL[n] * (powers[n] * others[6 - n])) for n in range(7)]
        left = jnp.concatenate([part[c] for c, e in PAIRS[:8]], axis=0)
        right = jnp.concatenate([part[e] for c, e in PAIRS[:8]], axis=0)
        eight = left * right
        rows = [order[n] * eight for n in range(7)]
        stack = jnp.concatenate(order + [jnp.zeros_like(phase)], axis=0)
        rows.append(stack * (part[2] * part[3]))
        rows.append(stack * (part[3] * part[3]))
        rows = split_two(jnp.concatenate(rows, axis=0))
        group = jnp.floor(knot * (1.0 / 256.0))
        low = jnp.maximum(knot, 0.0) - 256.0 * jnp.maximum(group, 0.0)
        return grouped(rows, group, 4), hot_lanes(low, 256)

    def body(chunks):
        rows, hots = zip(*[work(tile, knot) for tile, knot, block, i in chunks])
        total[...] += outer(jnp.concatenate(rows, axis=1), jnp.concatenate(hots, axis=1))

    each_batch(windows_ref, order, size, body)


def join(here_ref, there_ref, windows_ref, at=0):
    windows_ref[at] = here_ref[:, 0:SPAN]
    windows_ref[at + 1] = there_ref[:, SPAN : 2 * SPAN]


def first_kernel(here_hbm, there_ref, total, windows_ref, order, sem):
    copy = pltpu.make_async_copy(here_hbm.at[:, pl.ds(0, SPAN)], windows_ref.at[0], sem)
    copy.start()
    total[...] = jnp.zeros_like(total)
    windows_ref[1] = there_ref[:, SPAN : 2 * SPAN]
    copy.wait()
    add_moments(windows_ref, total, order, PART)


def next_kernel(before_ref, one_ref, one_there_ref, three_ref, three_there_ref, total, windows_ref, order):
    total[...] = before_ref[...]
    join(one_ref, one_there_ref, windows_ref)
    join(three_ref, three_there_ref, windows_ref, 2)
    add_moments(windows_ref, total, order, BATCH)


def last_kernel(before_ref, *refs):
    pairs, (select_ref, out_ref, total, tiles, windows_ref, order) = refs[:8], refs[8:]
    total[...] = before_ref[...]
    join(pairs[4], pairs[5], windows_ref)
    add_moments(windows_ref, total, order, PART)
    parts = []
    for g in range(4):
        group = total[2 * MOMENTS * g : 2 * MOMENTS * (g + 1)]
        high = group.astype(BF16)
        low = (group - high.astype(F32)).astype(BF16)
        parts.append(
            jnp.dot(
                select_ref[...], jnp.concatenate([high, low, high], axis=0), preferred_element_type=F32
            )
        )
    parts.append(jnp.zeros((160, 128), F32))
    orders = jnp.concatenate(parts, axis=1)
    band = orders[0:40]
    for a in range(1, 4):
        band = band + pltpu.roll(orders[40 * a : 40 * a + 40], a, 1)
    for q in range(8):
        for i in range(40):
            tiles[8 * i + q : 8 * i + q + 1, :] = band[i : i + 1, 128 * q : 128 * (q + 1)]
    spill = band[:, K : K + 128]
    packed = spill[0:8]
    for g in range(1, 5):
        packed = packed + pltpu.roll(spill[8 * g : 8 * g + 8], 8 * g, 1)
    tiles[8 * SPILL : 8 * SPILL + 8, :] = packed
    near, one, two, three = [
        pairs[2 * d][:, 2 * SPAN : WIDTH] + pairs[2 * d + 1][:, 2 * SPAN : WIDTH] for d in range(4)
    ]
    sums = (near + two) + (one + three)
    for s in range(N_SRC):
        count = min(SHARE, 8 * (SPILL + 1) - SHARE * s)
        out_ref[s, 0:24, :] = jnp.zeros((24, 128), F32)
        out_ref[s, 0:count, :] = tiles[SHARE * s : SHARE * s + count, :]
        for r in range(3):
            out_ref[s, 24 + 8 * r : 32 + 8 * r, :] = sums[:, 128 * r : 128 * (r + 1)]


def side_kernel(*refs):
    pairs, (parts_ref, out_ref, step_ref, total, windows_ref, order) = refs[:8], refs[8:]
    total[...] = jnp.zeros_like(total)
    for d in range(4):
        join(pairs[2 * d], pairs[2 * d + 1], windows_ref, 2 * d)
    both = parts_ref[0]
    for s in range(1, N_SRC):
        both = both + parts_ref[s]
    prior = float(OBS_DEV * N_SRC * N_TM // NCAL)
    totals = both[24:48]
    zero_moment = totals[0:4] + prior
    first = totals[4:8]
    second_moment = totals[8:12] + prior
    third, fourth = totals[12:16], totals[16:20]
    det = zero_moment * second_moment - first * first
    offset = (second_moment * third - first * fourth) / det
    slope = (zero_moment * fourth - first * third) / det
    for h in range(4):
        step_ref[0:1, 128 * h : 128 * (h + 1)] = offset[h : h + 1]
        step_ref[1:2, 128 * h : 128 * (h + 1)] = slope[h : h + 1]
    steps = jnp.concatenate([offset, slope], axis=0)
    sub = lax.broadcasted_iota(jnp.int32, (8, CHUNK), 0)
    quarter = (sub & 3).astype(F32)
    upper = sub < 4

    def work(tile, knot, block, i):
        shift = windows_ref[block, pl.ds(i, 1), MORE:SPAN]
        ids = windows_ref[block, pl.ds(4 + i, 1), MORE:SPAN]
        phase, weight, resid = tile[5:6], tile[6:7], tile[7:8]
        high = jnp.floor(ids * (1.0 / 128.0))
        low = jnp.broadcast_to((ids - 128.0 * high).astype(jnp.int32), (8, CHUNK))
        found = jnp.concatenate(
            [jnp.take_along_axis(steps, low[:, 128 * k : 128 * (k + 1)], axis=1) for k in range(CHUNK // 128)],
            axis=1,
        )
        found = jnp.where(quarter == high, found, 0.0) * jnp.where(upper, 1.0, shift)
        corrected = resid - jnp.sum(found, axis=0, keepdims=True)
        basis = spline_basis(phase)
        four = tile[0:4] * (weight * corrected)
        double = jnp.concatenate([four, four], axis=0)
        rows = []
        for a in (0, 2):
            order = jnp.concatenate([basis[a]] * 4 + [basis[a + 1]] * 4, axis=0)
            rows.append(double * order)
        rows = split_two(jnp.concatenate(rows, axis=0))
        group = jnp.floor(knot * (1.0 / 128.0))
        low = jnp.maximum(knot, 0.0) - 128.0 * jnp.maximum(group, 0.0)
        return grouped(rows, group, 8), hot_lanes(low, 128)

    def body(chunks):
        rows, hots = zip(*[work(*chunk) for chunk in chunks])
        total[...] += outer(jnp.concatenate(rows, axis=1), jnp.concatenate(hots, axis=1))

    each_batch(windows_ref, order, BATCH, body)
    orders = [total[32 * g : 32 * g + 16] + total[32 * g + 16 : 32 * g + 32] for g in range(8)]
    orders = jnp.concatenate(orders + [jnp.zeros((16, 128), F32)], axis=1)
    side = orders[0:4]
    for a in range(1, 4):
        side = side + pltpu.roll(orders, a, 1)[4 * a : 4 * a + 4]
    past = side[:, K : K + 128]
    spill = past[0:1]
    for c in range(1, 4):
        spill = spill + pltpu.roll(past[c : c + 1], 8 * c, 1)
    rows = [both[0:23], spill]
    for c in range(4):
        rows += [side[c : c + 1, 128 * q : 128 * (q + 1)] for q in range(8)]
    rows = jnp.concatenate(rows, axis=0)
    for s in range(N_SRC):
        out_ref[s] = rows


def gather_kernel(parts_ref, out_ref):
    side = parts_ref[0, 24:56, :]
    past = parts_ref[0, 23:24, :]
    for s in range(1, N_SRC):
        side = side + parts_ref[s, 24:56, :]
        past = past + parts_ref[s, 23:24, :]
    for s in range(N_SRC):
        count = min(SHARE, 8 * (SPILL + 1) - SHARE * s)
        out_ref[SHARE * s : SHARE * s + count, :] = parts_ref[s, 0:count, :]
    for c in range(4):
        lanes = slice(SPILL, SPILL + 3)
        out_ref[8 * SPILL + c : 8 * SPILL + c + 1, lanes] = past[:, 8 * c : 8 * c + 3]
    out_ref[8 * SIDE : 8 * TILES, :] = side


def stack_kernel(first_ref, second_ref, third_ref, fourth_ref, out_ref):
    for d, ref in enumerate((first_ref, second_ref, third_ref, fourth_ref)):
        out_ref[d] = ref[...]


def solve_kernel(
    place_ref, mine_ref, other_ref, coeffs_ref, within_ref, across_ref, out_ref,
    band, inverse, field, ahead, lower, applied, resid, delta, filtered, smooth, spare, direction, along,
):
    lane8 = lax.broadcasted_iota(jnp.int32, (8, 128), 1)
    lane = lax.broadcasted_iota(jnp.int32, (64, 128), 1)
    core, place_z = place_ref[0] & 1, place_ref[0] >> 1
    halves = ((mine_ref, core), (other_ref, 1 - core))
    for ref, parity in halves:
        for d in range(4):
            rows = pl.ds(pl.multiple_of(8 * (2 * ((place_z - d) & 3) + parity), 8), 8)
            for i in range(44):
                at = i if i < 40 else SIDE + i - 40
                band[i, rows, :] = ref[d, 8 * at : 8 * at + 8, :]
    for ref, parity in halves:
        for d in range(4):
            row = pl.ds(pl.multiple_of(8 * (2 * ((place_z - d) & 3) + parity) + 8, 8), 1)
            packed = ref[d, 8 * SPILL : 8 * SPILL + 8, :]
            for g in range(6):
                moved = packed if g == 0 else pltpu.roll(packed, 128 - 8 * g, 1)
                moved = jnp.where(lane8 < 3, moved, 0.0)
                for u in range(min(8, 44 - 8 * g)):
                    band[8 * g + u, row, :] += moved[u : u + 1]
    for c in range(4):
        inverse[c] = 1.0 / (ATTITUDE_PRIOR + band[PAIR_AT[(c, c)], 0:64, :])
    field[...] = jnp.zeros_like(field)
    spare[...] = jnp.zeros_like(spare)

    def total_of(left, right):
        value = left * right
        value = jnp.sum(value.reshape(32, 8, 128), axis=0)
        return jnp.sum(jnp.sum(value, axis=0, keepdims=True), axis=1, keepdims=True)

    def precondition(source):
        res = source[...].reshape(256, 128)
        high = res.astype(BF16)
        low = (res - high.astype(F32)).astype(BF16)
        spreads = jnp.dot(
            jnp.concatenate([high, low, high], axis=1), within_ref[...], preferred_element_type=F32
        )
        for c in range(4):
            own = spreads[64 * c : 64 * c + 64]
            carried = jnp.concatenate([own[:, 128:256], own[:, 256:384], own[:, 384:512]], axis=0)
            high = carried.astype(BF16)
            low = (carried - high.astype(F32)).astype(BF16)
            carry = jnp.dot(
                across_ref[...], jnp.concatenate([high, low, high], axis=0), preferred_element_type=F32
            )
            filtered[c] = source[c] * inverse[c] + own[:, :128] + carry

    def apply_normals():
        for e in range(4):
            here, after = field[e, 8:72, :], field[e, 9:73, :]
            for d in range(1, 4):
                ahead[d - 1, e] = pltpu.roll(jnp.where(lane < d, after, here), 128 - d, 1)
        for t in range(N_TM):
            rows = slice(8 * t, 8 * t + 8)
            padded = slice(8 * t + 8, 8 * t + 16)
            own = [field[e, padded, :] for e in range(4)]
            sums = [own[c] * ATTITUDE_PRIOR for c in range(4)]
            for d in range(4):
                near = own if d == 0 else [ahead[d - 1, e, rows, :] for e in range(4)]
                tiles = [band[10 * d + i, rows, :] for i in range(10)]
                for c in range(4):
                    for e in range(4):
                        sums[c] = sums[c] + tiles[PAIR_AT[(c, e)]] * near[e]
                if d:
                    for c in range(4):
                        back = tiles[PAIR_AT[(c, 0)]] * own[0]
                        for e in range(1, 4):
                            back = back + tiles[PAIR_AT[(c, e)]] * own[e]
                        lower[d - 1, c, rows, :] = back
            for c in range(4):
                applied[c, rows, :] = sums[c]
        for c in range(4):
            result = applied[c]
            wrapped = jnp.zeros((64, 128), F32)
            for d in range(1, 4):
                moved = pltpu.roll(lower[d - 1, c], d, 1)
                result = result + jnp.where(lane >= d, moved, 0.0)
                wrapped = wrapped + jnp.where(lane < d, moved, 0.0)
            spare[c, 8:72, :] = wrapped
            applied[c] = result + spare[c, 7:71, :]

    resid[...] = band[40:44, 0:64, :]
    precondition(resid)
    field[:, 8:72, :] = filtered[...]
    delta[...] = jnp.zeros_like(delta)
    energy = total_of(resid[...], filtered[...])
    for i in range(ITERS):
        apply_normals()
        if i < ITERS - 1:
            precondition(applied)
        if i == 0:
            toward, image, smooth_image = field[:, 8:72, :], applied[...], filtered[...]
        else:
            toward = field[:, 8:72, :] + ratio * direction[...]
            image = applied[...] + ratio * along[...]
            smooth_image = filtered[...] + ratio * smooth[...]
        step = energy / total_of(toward, image)
        delta[...] += step * toward
        if i < ITERS - 1:
            direction[...], along[...], smooth[...] = toward, image, smooth_image
            rest = resid[...] - step * image
            after = field[:, 8:72, :] - step * smooth_image
            resid[...] = rest
            field[:, 8:72, :] = after
            fresh = total_of(rest, after)
            ratio, energy = fresh / energy, fresh
    mine = pl.ds(pl.multiple_of(place_ref[0] * 8, 8), 8)
    for c in range(4):
        tile = delta[c, mine, :]
        for q in range(8):
            lanes = slice(128 * q, 128 * q + 128)
            out_ref[c : c + 1, lanes] = coeffs_ref[c : c + 1, lanes] + tile[q : q + 1]


VMEM_SPEC = pl.BlockSpec(memory_space=pltpu.VMEM)
SMEM_SPEC = pl.BlockSpec(memory_space=pltpu.SMEM)
HBM_SPEC = pl.BlockSpec(memory_space=pltpu.HBM)
PARAMS = pltpu.CompilerParams(vmem_limit_bytes=VMEM_LIMIT)
CHUNKS = N_TM * CAP // CHUNK


def to_other_core(value):
    return lax.ppermute(value, "tm", [(i, i ^ 1) for i in range(N_TM)])


def along_z(value, d):
    return lax.ppermute(value, "tm", [(i, (i + 2 * d) % N_TM) for i in range(N_TM)])


def cost(microseconds):
    return pl.CostEstimate(
        flops=int(microseconds * 1_000_000_000), bytes_accessed=1_000_000, transcendentals=0
    )


def local(
    knot_index, block_counts, knot_phase, partials, obs_weight, residuals, cal_id, across, coeffs
):
    dense = [
        value.reshape(64, 128)
        for value in (cal_id, obs_weight, across, residuals, knot_index, knot_phase)
    ]
    place = lax.axis_index("tm").reshape(1)
    with jax.named_scope("windows"):
        windows = pl.pallas_call(
            window_kernel,
            out_shape=(jax.ShapeDtypeStruct((8, WIDTH), F32),) * 4,
            in_specs=[SMEM_SPEC] * 2 + [HBM_SPEC] * 7,
            out_specs=(HBM_SPEC,) * 4,
            scratch_shapes=[pltpu.VMEM((64, 128), value.dtype) for value in dense]
            + [
                pltpu.VMEM((4, OBS_DEV), F32),
                pltpu.VMEM((8, OBS_DEV + CAP + 128), F32),
                pltpu.VMEM((8, OBS_DEV + CAP + 128), F32),
                pltpu.VMEM((4, 8, WIDTH), F32),
                pltpu.SMEM((N_TM,), jnp.int32),
                pltpu.SemaphoreType.DMA((7,)),
                pltpu.SemaphoreType.DMA((4,)),
            ],
            compiler_params=pltpu.CompilerParams(vmem_limit_bytes=56 * 1024 * 1024),
        )(place, block_counts, *dense, partials)
    with jax.named_scope("to_owners"):
        windows = [windows[0]] + [along_z(windows[d], d) for d in (1, 2, 3)]
        near = (windows[0], to_other_core(windows[0]))
    with jax.named_scope("moments"):
        total = jax.ShapeDtypeStruct((8 * MOMENTS, 256), F32)
        scratch = [pltpu.VMEM((2, 8, SPAN), F32), pltpu.SMEM((CHUNKS,), jnp.int32)]
        moments = pl.pallas_call(
            first_kernel,
            out_shape=total,
            in_specs=[HBM_SPEC, VMEM_SPEC],
            out_specs=VMEM_SPEC,
            scratch_shapes=[*scratch, pltpu.SemaphoreType.DMA],
            compiler_params=PARAMS,
            cost_estimate=cost(2),
        )(*near)
        moments, one = lax.optimization_barrier((moments, windows[1]))
        moments, three = lax.optimization_barrier((moments, windows[3]))
        pairs = [near] + [(here, to_other_core(here)) for here in (one, windows[2], three)]
        moments = pl.pallas_call(
            next_kernel,
            out_shape=total,
            in_specs=[VMEM_SPEC] * 5,
            out_specs=VMEM_SPEC,
            scratch_shapes=[pltpu.VMEM((4, 8, SPAN), F32), pltpu.SMEM((CHUNKS,), jnp.int32)],
            compiler_params=PARAMS,
            cost_estimate=cost(2),
        )(moments, *pairs[1], *pairs[3])
        refs = [ref for pair in pairs for ref in pair]
        parts = pl.pallas_call(
            last_kernel,
            out_shape=jax.ShapeDtypeStruct((N_SRC, 48, 128), F32),
            in_specs=[VMEM_SPEC] * 10,
            out_specs=VMEM_SPEC,
            scratch_shapes=[
                pltpu.VMEM((8 * MOMENTS, 256), F32),
                pltpu.VMEM((8 * (SPILL + 1), 128), F32),
                *scratch,
            ],
            compiler_params=PARAMS,
        )(moments, *refs, jnp.asarray(select_rows()))
    with jax.named_scope("band_reduce"):
        parts = lax.all_to_all(parts, "src", 0, 0)
    with jax.named_scope("side"):
        parts, calibration_step = pl.pallas_call(
            side_kernel,
            out_shape=(
                jax.ShapeDtypeStruct((N_SRC, 56, 128), F32),
                jax.ShapeDtypeStruct((2, NCAL), F32),
            ),
            in_specs=[VMEM_SPEC] * 9,
            out_specs=(VMEM_SPEC, VMEM_SPEC),
            scratch_shapes=[
                pltpu.VMEM((256, 128), F32),
                pltpu.VMEM((N_TM, 8, SPAN), F32),
                pltpu.SMEM((CHUNKS + BATCH,), jnp.int32),
            ],
            compiler_params=PARAMS,
        )(*refs, parts)
    with jax.named_scope("gather_src"):
        parts = lax.all_to_all(parts, "src", 0, 0)
    with jax.named_scope("gather"):
        parts = pl.pallas_call(
            gather_kernel,
            out_shape=jax.ShapeDtypeStruct((8 * TILES, 128), F32),
            in_specs=[VMEM_SPEC],
            out_specs=VMEM_SPEC,
            compiler_params=PARAMS,
        )(parts)
    with jax.named_scope("gather_z"):
        mine = pl.pallas_call(
            stack_kernel,
            out_shape=jax.ShapeDtypeStruct((4, 8 * TILES, 128), F32),
            in_specs=[VMEM_SPEC] * 4,
            out_specs=VMEM_SPEC,
            compiler_params=PARAMS,
        )(parts, *[along_z(parts, d) for d in (1, 2, 3)])
    with jax.named_scope("gather_core"):
        other = to_other_core(mine)
    tables = [jnp.asarray(table) for table in filter_tables()]
    with jax.named_scope("solve"):
        new_coeffs = pl.pallas_call(
            solve_kernel,
            out_shape=jax.ShapeDtypeStruct((4, K), F32),
            in_specs=[SMEM_SPEC] + [VMEM_SPEC] * 5,
            out_specs=VMEM_SPEC,
            scratch_shapes=[
                pltpu.VMEM((44, 72, 128), F32),
                pltpu.VMEM((4, 64, 128), F32),
                pltpu.VMEM((4, 80, 128), F32),
                pltpu.VMEM((3, 4, 64, 128), F32),
                pltpu.VMEM((3, 4, 64, 128), F32),
                pltpu.VMEM((4, 64, 128), F32),
                pltpu.VMEM((4, 64, 128), F32),
                pltpu.VMEM((4, 64, 128), F32),
                pltpu.VMEM((4, 64, 128), F32),
                pltpu.VMEM((4, 64, 128), F32),
                pltpu.VMEM((4, 80, 128), F32),
                pltpu.VMEM((4, 64, 128), F32),
                pltpu.VMEM((4, 64, 128), F32),
            ],
            compiler_params=PARAMS,
        )(place, mine, other, coeffs, *tables)
    return (new_coeffs, calibration_step)


def solution(mesh):
    placed = (
        P(("src", "tm")),
        P(("src", "tm"), None),
        P(("src", "tm")),
        P(None, ("src", "tm")),
        P(("src", "tm")),
        P(("src", "tm")),
        P(("src", "tm")),
        P(("src", "tm")),
        P(None, "tm"),
    )
    return jax.shard_map(
        local, mesh=mesh, in_specs=placed, out_specs=(P(None, "tm"), P()), check_vma=False
    )
```
